32 devices in a mesh: expert: 4 (over z), dp: 8 (over y, x, core).
Axes of the slice: x: 2, y: 2, z: 4, core: 2. Of those that a mesh axis runs over, the one named last changes fastest.
Arguments:
- tokens: bfloat16 [128, 512, 512], P(('expert', 'dp')), may hold values from -6 to 6
- memory: bfloat16 [128, 512, 512], P(('expert', 'dp')), may hold values from -6 to 6
- cotangent: bfloat16 [128, 512, 512], P(('expert', 'dp')), may hold values from -6 to 6
- target_length: int32 [128], P(('expert', 'dp')), may hold values from 256 to 512, as said below
- memory_length: int32 [128], P(('expert', 'dp')), may hold values from 256 to 512, as said below
- expert_of: int32 [128], replicated, may hold values from 0 to 7, as said below
- self_norm_gain: float32 [512], replicated, may hold values from 0.5 to 1.5
- self_norm_bias: float32 [512], replicated, may hold values from -1.25 to 1.25
- self_query: bfloat16 [512, 512], replicated, may hold values from -0.25 to 0.25
- self_key: bfloat16 [512, 512], replicated, may hold values from -0.25 to 0.25
- self_value: bfloat16 [512, 512], replicated, may hold values from -0.25 to 0.25
- self_out: bfloat16 [512, 512], replicated, may hold values from -1.5 to 1.5
- self_query_bias: float32 [512], replicated, may hold values from -1.25 to 1.25
- self_value_bias: float32 [512], replicated, may hold values from -1.25 to 1.25
- self_out_bias: float32 [512], replicated, may hold values from -1.25 to 1.25
- cross_norm_gain: float32 [512], replicated, may hold values from 0.5 to 1.5
- cross_norm_bias: float32 [512], replicated, may hold values from -1.25 to 1.25
- cross_query: bfloat16 [512, 512], replicated, may hold values from -0.25 to 0.25
- cross_key: bfloat16 [512, 512], replicated, may hold values from -0.25 to 0.25
- cross_value: bfloat16 [512, 512], replicated, may hold values from -0.25 to 0.25
- cross_out: bfloat16 [512, 512], replicated, may hold values from -1.5 to 1.5
- cross_attention_query_bias: float32 [512], replicated, may hold values from -1.25 to 1.25
- cross_value_bias: float32 [512], replicated, may hold values from -1.25 to 1.25
- cross_out_bias: float32 [512], replicated, may hold values from -1.25 to 1.25
- expert_norm_gain: float32 [512], replicated, may hold values from 0.5 to 1.5
- expert_norm_bias: float32 [512], replicated, may hold values from -1.25 to 1.25
- expert_in: bfloat16 [8, 512, 2048], P('expert'), may hold values from -0.25 to 0.25
- expert_in_bias: float32 [8, 2048], P('expert'), may hold values from -0.625 to 0.625
- expert_out: bfloat16 [8, 2048, 512], P('expert'), may hold values from -0.1875 to 0.1875
- expert_out_bias: float32 [8, 512], P('expert'), may hold values from -0.625 to 0.625
Outputs:
- output: bfloat16 [128, 512, 512], P(('expert', 'dp'))
- tokens_grad: float32 [128, 512, 512], P(('expert', 'dp'))
- memory_grad: float32 [128, 512, 512], P(('expert', 'dp'))
- self_norm_gain_grad: float32 [512], replicated
- self_norm_bias_grad: float32 [512], replicated
- self_query_grad: float32 [512, 512], replicated
- self_key_grad: float32 [512, 512], replicated
- self_value_grad: float32 [512, 512], replicated
- self_out_grad: float32 [512, 512], replicated
- self_query_bias_grad: float32 [512], replicated
- self_value_bias_grad: float32 [512], replicated
- self_out_bias_grad: float32 [512], replicated
- cross_norm_gain_grad: float32 [512], replicated
- cross_norm_bias_grad: float32 [512], replicated
- cross_query_grad: float32 [512, 512], replicated
- cross_key_grad: float32 [512, 512], replicated
- cross_value_grad: float32 [512, 512], replicated
- cross_out_grad: float32 [512, 512], replicated
- cross_query_bias_grad: float32 [512], replicated
- cross_value_bias_grad: float32 [512], replicated
- cross_out_bias_grad: float32 [512], replicated
- expert_norm_gain_grad: float32 [512], replicated
- expert_norm_bias_grad: float32 [512], replicated
- expert_in_grad: float32 [8, 512, 2048], P('expert', 'dp')
- expert_in_bias_grad: float32 [8, 2048], P('expert', 'dp')
- expert_out_grad: float32 [8, 2048, 512], P('expert', 'dp')
- expert_out_bias_grad: float32 [8, 512], P('expert', 'dp')
The draws below stay inside these ranges and needn't reach their ends.
Inputs may be any that keep to these rules, and one draw needn't show every extreme that they name: `target_length`: valid tokens of a sequence stand first. `memory_length`: valid memory tokens of a sequence stand first. `expert_of`: the 4 sequences of one device name experts of 4 different groups, a group being the ids with one quotient by 2.
All inputs are finite; a program needn't handle non-finite values.
Results may differ from the reference program's by a relative error of at most 0.019.
Values may be sent and summed in bfloat16 or wider, within the bound.
No kernel may reach another device: no remote copies, remote signals or barrier semaphores. Data moves between devices by JAX's collectives and lax.ppermute only.
A program may use at most 192 MiB of HBM per device.

```python
import jax
import jax.numpy as jnp
from jax import lax

D = 512
HEADS = 8
HEAD_DIM = 64
FF = 2048
EXP_DEV = 2
S_DEV = 4
LEN = 512
MEM = 512
EXPERTS = 8
SEQS = 128


def draw_target_length(key, part):
    key_values, key_spot = jax.random.split(key)
    lengths = jax.random.randint(key_values, (SEQS,), LEN // 2, LEN + 1)
    spot_index = jax.random.randint(key_spot, (), 0, SEQS)
    lengths = lengths.at[spot_index].set(LEN)
    return lengths.at[(spot_index + 1) % SEQS].set(LEN // 2).astype(jnp.int32)


def draw_memory_length(key, part):
    key_values, key_spot = jax.random.split(jax.random.fold_in(key, 7))
    lengths = jax.random.randint(key_values, (SEQS,), MEM // 2, MEM + 1)
    spot_index = jax.random.randint(key_spot, (), 0, SEQS)
    lengths = lengths.at[spot_index].set(MEM)
    return lengths.at[(spot_index + 1) % SEQS].set(MEM // 2).astype(jnp.int32)


def draw_expert_of(key, part):
    groups = EXPERTS // EXP_DEV
    devices = SEQS // S_DEV
    places = devices // groups
    key_rank, key_noise, key_column, key_owner, key_local = jax.random.split(jax.random.fold_in(key, 11), 5)
    owner_rank = jax.random.permutation(key_rank, groups)
    weight = 1 + 5 * (owner_rank == 0).astype(jnp.int32) + 2 * (owner_rank == 1).astype(jnp.int32)
    noise_draw = jax.random.randint(key_noise, (devices, groups), 0, 1024)
    owner_index = lax.broadcasted_iota(jnp.int32, (devices, groups), 1)
    device_index = lax.broadcasted_iota(jnp.int32, (devices, groups), 0)
    hot_column = jax.random.randint(key_column, (), 0, places)
    hot_owner = jax.random.randint(key_owner, (), 0, groups)
    favoured = (device_index % places == hot_column) & (owner_index == hot_owner)
    scores = (noise_draw * weight[None, :] + 16384 * favoured.astype(jnp.int32)) * groups + owner_index
    chosen = lax.top_k(scores, S_DEV)[1]
    local_pick = jax.random.randint(key_local, (devices, S_DEV), 0, EXP_DEV)
    return (chosen * EXP_DEV + local_pick).reshape(SEQS).astype(jnp.int32)


def level_of(stream_key, dims, cuts, low, top_value):
    level = 1.0
    for axis_at, shards_of in cuts:
        steps = jax.random.uniform(jax.random.fold_in(jax.random.fold_in(stream_key, 6), axis_at), (shards_of,), jnp.float32, low / len(cuts), top_value / len(cuts))
        level = level * jnp.repeat(jnp.exp(steps), dims[axis_at] // shards_of).reshape((-1,) + (1,) * (len(dims) - 1 - axis_at))
    return level


def scatter_about(key, extent, spread, most, cuts=(), kind=jnp.bfloat16):
    values = spread * jax.random.normal(key, extent, jnp.float32)
    if cuts:
        values = values * level_of(key, extent, cuts, -0.22, 0.18)
    return jnp.clip(values, -most, most).astype(kind)


def setup_inputs(seed: int = 0) -> dict:
    key_of = jax.random.split(jax.random.key(seed), 31)
    return {
        "tokens": scatter_about(key_of[0], (SEQS, LEN, D), 1.0, 6.0, ((0, 32),)),
        "memory": scatter_about(key_of[1], (SEQS, MEM, D), 1.0, 6.0, ((0, 32),)),
        "cotangent": scatter_about(key_of[2], (SEQS, LEN, D), 1.0, 6.0, ((0, 32),)),
        "target_length": draw_target_length(jax.random.fold_in(key_of[30], 71), 0),
        "memory_length": draw_memory_length(jax.random.fold_in(key_of[30], 71), 0),
        "expert_of": draw_expert_of(jax.random.fold_in(key_of[30], 71), 0),
        "self_norm_gain": jnp.clip(1.0 + 0.1 * jax.random.normal(key_of[6], (D,), jnp.float32), 0.5, 1.5),
        "self_norm_bias": scatter_about(key_of[7], (D,), 0.2, 1.25, (), jnp.float32),
        "self_query": scatter_about(key_of[8], (D, D), D ** -0.5, 0.25),
        "self_key": scatter_about(key_of[9], (D, D), D ** -0.5, 0.25),
        "self_value": scatter_about(key_of[10], (D, D), D ** -0.5, 0.25),
        "self_out": scatter_about(key_of[11], (D, D), (D // 32) ** -0.5, 1.5),
        "self_query_bias": scatter_about(key_of[12], (D,), 0.2, 1.25, (), jnp.float32),
        "self_value_bias": scatter_about(key_of[13], (D,), 0.2, 1.25, (), jnp.float32),
        "self_out_bias": scatter_about(key_of[14], (D,), 0.2, 1.25, (), jnp.float32),
        "cross_norm_gain": jnp.clip(1.0 + 0.1 * jax.random.normal(key_of[15], (D,), jnp.float32), 0.5, 1.5),
        "cross_norm_bias": scatter_about(key_of[16], (D,), 0.2, 1.25, (), jnp.float32),
        "cross_query": scatter_about(key_of[17], (D, D), D ** -0.5, 0.25),
        "cross_key": scatter_about(key_of[18], (D, D), D ** -0.5, 0.25),
        "cross_value": scatter_about(key_of[19], (D, D), D ** -0.5, 0.25),
        "cross_out": scatter_about(key_of[20], (D, D), (D // 32) ** -0.5, 1.5),
        "cross_attention_query_bias": scatter_about(key_of[21], (D,), 0.2, 1.25, (), jnp.float32),
        "cross_value_bias": scatter_about(key_of[22], (D,), 0.2, 1.25, (), jnp.float32),
        "cross_out_bias": scatter_about(key_of[23], (D,), 0.2, 1.25, (), jnp.float32),
        "expert_norm_gain": jnp.clip(1.0 + 0.1 * jax.random.normal(key_of[24], (D,), jnp.float32), 0.5, 1.5),
        "expert_norm_bias": scatter_about(key_of[25], (D,), 0.2, 1.25, (), jnp.float32),
        "expert_in": scatter_about(key_of[26], (EXPERTS, D, FF), D ** -0.5, 0.25, ((0, 4),)),
        "expert_in_bias": scatter_about(key_of[27], (EXPERTS, FF), 0.1, 0.625, ((0, 4),), jnp.float32),
        "expert_out": scatter_about(key_of[28], (EXPERTS, FF, D), (FF // 2) ** -0.5, 0.1875, ((0, 4),)),
        "expert_out_bias": scatter_about(key_of[29], (EXPERTS, D), 0.1, 0.625, ((0, 4),), jnp.float32),
    }


@jax.custom_vjp
def low(v):
    return lax.optimization_barrier(v.astype(jnp.bfloat16)).astype(jnp.float32)

@jax.custom_vjp
def low_back(v):
    return v

def low_keep(v):
    return (low(v), None)

def low_pass(kept, grad):
    return (grad,)

def back_keep(v):
    return (v, None)

def back_low(kept, grad):
    return (low(grad),)
low.defvjp(low_keep, low_pass)
low_back.defvjp(back_keep, back_low)
EPSILON = 1e-05
SCORE_SCALE = 0.125
NEGATIVE = -1e+30
HIGHEST = lax.Precision.HIGHEST

def rounded(values):
    return low_back(low(values))

def layer_norm(values, norm_gain, norm_shift):
    centre = values - lax.optimization_barrier(jnp.mean(values, axis=-1, keepdims=True))
    inverse = lax.rsqrt(lax.optimization_barrier(jnp.mean(centre * centre, axis=-1, keepdims=True)) + EPSILON)
    return centre * inverse * norm_gain + norm_shift

def matmul(left, right):
    return jnp.dot(left, right, precision=HIGHEST)

def attend(queries, key_rows, value_rows, allowed):
    query_heads = queries.reshape(queries.shape[0], HEADS, HEAD_DIM)
    key_heads = key_rows.reshape(key_rows.shape[0], HEADS, HEAD_DIM)
    value_heads = value_rows.reshape(value_rows.shape[0], HEADS, HEAD_DIM)
    scores = jnp.einsum('qhd,khd->hqk', query_heads, key_heads, precision=HIGHEST) * SCORE_SCALE
    scores = low_back(scores)
    scores = jnp.where(allowed[None], scores, NEGATIVE)
    highest = lax.optimization_barrier(jnp.max(scores, axis=-1, keepdims=True))
    raised = jnp.exp(scores - highest)
    chance = low(raised / lax.optimization_barrier(jnp.sum(raised, axis=-1, keepdims=True)))
    context = jnp.einsum('hqk,khd->qhd', chance, value_heads, precision=HIGHEST)
    return rounded(context.reshape(queries.shape[0], D))

def sequence_forward(params, pieces):
    self_norm_gain, self_norm_bias, self_query, self_key, self_value, self_out, self_query_bias, self_value_bias, self_out_bias, cross_norm_gain, cross_norm_bias, cross_query, cross_key, cross_value, cross_out, cross_attention_query_bias, cross_value_bias, cross_out_bias, expert_norm_gain, expert_norm_bias, expert_in, expert_in_bias, expert_out, expert_out_bias = params
    token_rows, memory_rows, target_count, memory_count, expert_pick = pieces
    positions = lax.broadcasted_iota(jnp.int32, (LEN, 1), 0)
    valid_rows = (positions < target_count).astype(jnp.float32)
    start_rows = token_rows * valid_rows
    normed_self = low(layer_norm(start_rows, self_norm_gain, self_norm_bias))
    query_one = rounded(matmul(normed_self, self_query) + self_query_bias)
    key_one = rounded(matmul(normed_self, self_key))
    value_one = rounded(matmul(normed_self, self_value) + self_value_bias)
    causal = lax.broadcasted_iota(jnp.int32, (LEN, LEN), 0) >= lax.broadcasted_iota(jnp.int32, (LEN, LEN), 1)
    context_one = attend(query_one, key_one, value_one, causal)
    middle_rows = start_rows + low_back(matmul(context_one, self_out) + self_out_bias)
    normed_cross = low(layer_norm(middle_rows, cross_norm_gain, cross_norm_bias))
    query_two = rounded(matmul(normed_cross, cross_query) + cross_attention_query_bias)
    key_two = rounded(matmul(memory_rows, cross_key))
    value_two = rounded(matmul(memory_rows, cross_value) + cross_value_bias)
    reach = lax.broadcasted_iota(jnp.int32, (LEN, MEM), 1) < memory_count
    context_two = attend(query_two, key_two, value_two, reach)
    later_rows = middle_rows + low_back(matmul(context_two, cross_out) + cross_out_bias)
    normed_expert = rounded(layer_norm(later_rows, expert_norm_gain, expert_norm_bias))
    weight_in = lax.dynamic_index_in_dim(expert_in, expert_pick, 0, False)
    bias_in = lax.dynamic_index_in_dim(expert_in_bias, expert_pick, 0, False)
    weight_out = lax.dynamic_index_in_dim(expert_out, expert_pick, 0, False)
    bias_out = lax.dynamic_index_in_dim(expert_out_bias, expert_pick, 0, False)
    pre_active = low_back(matmul(normed_expert, weight_in) + bias_in)
    hidden = rounded(jax.nn.silu(pre_active))
    made_rows = rounded(matmul(hidden, weight_out) + bias_out)
    return (later_rows + made_rows) * valid_rows

def reference(tokens, memory, cotangent, target_length, memory_length, expert_of, self_norm_gain, self_norm_bias, self_query, self_key, self_value, self_out, self_query_bias, self_value_bias, self_out_bias, cross_norm_gain, cross_norm_bias, cross_query, cross_key, cross_value, cross_out, cross_attention_query_bias, cross_value_bias, cross_out_bias, expert_norm_gain, expert_norm_bias, expert_in, expert_in_bias, expert_out, expert_out_bias):
    params = tuple((item.astype(jnp.float32) for item in (self_norm_gain, self_norm_bias, self_query, self_key, self_value, self_out, self_query_bias, self_value_bias, self_out_bias, cross_norm_gain, cross_norm_bias, cross_query, cross_key, cross_value, cross_out, cross_attention_query_bias, cross_value_bias, cross_out_bias, expert_norm_gain, expert_norm_bias, expert_in, expert_in_bias, expert_out, expert_out_bias)))
    stepper = jax.checkpoint(sequence_forward)

    def whole(weights, tokens_float, memory_float):

        def step(running, pieces):
            return (running, stepper(weights, pieces))
        _, produced = lax.scan(step, jnp.zeros((), jnp.float32), (tokens_float, memory_float, target_length, memory_length, expert_of))
        return produced
    result, pullback = jax.vjp(whole, params, tokens.astype(jnp.float32), memory.astype(jnp.float32))
    param_grads, tokens_grad, memory_grad = pullback(cotangent.astype(jnp.float32))
    return (result.astype(jnp.bfloat16), tokens_grad, memory_grad, param_grads[0], param_grads[1], param_grads[2], param_grads[3], param_grads[4], param_grads[5], param_grads[6], param_grads[7], param_grads[8], param_grads[9], param_grads[10], param_grads[11], param_grads[12], param_grads[13], param_grads[14], param_grads[15], param_grads[16], param_grads[17], param_grads[18], param_grads[19], param_grads[20], param_grads[21], param_grads[22], param_grads[23])
```

```python
import functools

import jax
import jax.numpy as jnp
from jax import lax
from jax.experimental import pallas as pl
from jax.experimental.pallas import tpu as pltpu
from jax.sharding import PartitionSpec as P

HEADS = 8
HEAD_DIM = 64
PAIR = 2 * HEAD_DIM
EPSILON = 1e-05
SCORE_SCALE = 0.125
NEGATIVE = -1e30
LOG2E = 1.4426950408889634
LN2 = 0.6931471805599453
VMEM_LIMIT = 60 * 1024 * 1024
F32 = jnp.float32
BF16 = jnp.bfloat16


def contract(left, right, left_dim, right_dim):
    return lax.dot_general(
        left, right, (((left_dim,), (right_dim,)), ((), ())), preferred_element_type=F32
    )


def nn(left, right):
    return contract(left, right, 1, 0)


def nt(left, right):
    return contract(left, right, 1, 1)


def tn(left, right):
    return contract(left, right, 0, 0)


def normalise(rows):
    centre = rows - jnp.mean(rows, axis=-1, keepdims=True)
    inverse = lax.rsqrt(jnp.mean(centre * centre, axis=-1, keepdims=True) + EPSILON)
    return centre * inverse, inverse


def normalise_back(grad, normed, inverse, gain):
    scaled = grad * gain
    return inverse * (
        scaled
        - jnp.mean(scaled, axis=-1, keepdims=True)
        - normed * jnp.mean(scaled * normed, axis=-1, keepdims=True)
    )


def column_sum(rows):
    return jnp.sum(rows.astype(F32), axis=0, keepdims=True)


def head_masks():
    lane = lax.broadcasted_iota(jnp.int32, (1, PAIR), 1)
    mine = [(lane // HEAD_DIM == half).astype(F32).astype(BF16) for half in (0, 1)]
    spare = [(lane == HEAD_DIM * (1 - half)).astype(F32).astype(BF16) for half in (0, 1)]
    return mine, spare


def key_bias(count, mem_rows):
    place = lax.broadcasted_iota(jnp.int32, (mem_rows, PAIR), 0)
    return jnp.where(place < count, 0.0, NEGATIVE).astype(BF16)


def score_operands(keys, queries, half, mine, spare, bias):
    picked = queries * mine[half]
    if bias is None:
        return keys, picked
    return keys * (1 - spare[half]) + bias * spare[half], picked + spare[half]


def causal_scores(scores, query_start, block):
    last = scores.shape[0] - block
    key_at = lax.broadcasted_iota(jnp.int32, (block, block), 0)
    query_at = lax.broadcasted_iota(jnp.int32, (block, block), 1)
    edge = jnp.where(key_at <= query_at, scores[last:], NEGATIVE)
    return jnp.concatenate([scores[:last], edge], axis=0) if last else edge


def attend(query_ref, key_ref, value_t_ref, context_t_ref, logsum_ref, bias):
    length = query_ref.shape[0]
    block = length // 2
    mine, spare = head_masks()

    def pair_step(pair, carry):
        columns = pl.ds(pl.multiple_of(pair * PAIR, PAIR), PAIR)
        keys, queries = key_ref[:, columns], query_ref[:, columns]
        for half in (0, 1):
            rows = pl.ds(pl.multiple_of(pair * PAIR + half * HEAD_DIM, HEAD_DIM), HEAD_DIM)
            left, right = score_operands(keys, queries, half, mine, spare, bias)
            for part in (0, 1):
                place = slice(part * block, (part + 1) * block)
                reach = key_ref.shape[0] if bias is not None else (part + 1) * block
                scores = nt(left[:reach], right[place])
                if bias is None:
                    scores = causal_scores(scores, part * block, block)
                highest = jnp.max(scores, axis=0, keepdims=True)
                raised = jnp.exp2(scores - highest)
                summed = jnp.sum(raised, axis=0, keepdims=True)
                context = nn(value_t_ref[rows, :reach], raised.astype(BF16))
                context_t_ref[rows, place] = (context * (1.0 / summed)).astype(BF16)
                logsum_ref[pl.ds(2 * pair + half, 1), place] = highest + LOG2E * jnp.log(summed)
        return carry

    lax.fori_loop(0, HEADS // 2, pair_step, 0)


def attend_back(
    query_ref,
    key_ref,
    value_ref,
    key_t_ref,
    grad_ref,
    delta_ref,
    logsum_ref,
    grad_query_t_ref,
    grad_key_ref,
    grad_value_ref,
    bias,
):
    length = query_ref.shape[0]
    keys_all = key_ref.shape[0]
    block = length // 2
    mine, spare = head_masks()

    def pair_step(pair, carry):
        columns = pl.ds(pl.multiple_of(pair * PAIR, PAIR), PAIR)
        keys, queries, values = key_ref[:, columns], query_ref[:, columns], value_ref[:, columns]
        grads = grad_ref[:, columns]
        chances, slopes, picked_grads, picked_queries = {}, {}, [], []
        for half in (0, 1):
            head = pl.ds(2 * pair + half, 1)
            rows = pl.ds(pl.multiple_of(pair * PAIR + half * HEAD_DIM, HEAD_DIM), HEAD_DIM)
            left, right = score_operands(keys, queries, half, mine, spare, bias)
            grad_half = grads * mine[half]
            picked_grads.append(grad_half)
            picked_queries.append(queries * mine[half])
            for part in (0, 1):
                place = slice(part * block, (part + 1) * block)
                reach = keys_all if bias is not None else (part + 1) * block
                scores = nt(left[:reach], right[place])
                if bias is None:
                    scores = causal_scores(scores, part * block, block)
                chance = jnp.exp2(scores - logsum_ref[head, place])
                grad_chance = nt(values[:reach], grad_half[place])
                slope = (chance * (grad_chance - delta_ref[head, place])).astype(BF16)
                chances[half, part] = chance.astype(BF16)
                slopes[half, part] = slope
                grad_query_t_ref[rows, place] = (
                    nn(key_t_ref[rows, :reach], slope) * SCORE_SCALE
                ).astype(BF16)

        def gather(table, others):
            if bias is not None:
                wide = jnp.concatenate([table[h, p] for h in (0, 1) for p in (0, 1)], axis=1)
                return nn(wide, jnp.concatenate(others, axis=0))
            upper = jnp.concatenate([table[h, p][:block] for h in (0, 1) for p in (0, 1)], axis=1)
            lower = jnp.concatenate([table[h, 1][block:] for h in (0, 1)], axis=1)
            return jnp.concatenate(
                [
                    nn(upper, jnp.concatenate(others, axis=0)),
                    nn(lower, jnp.concatenate([item[block:] for item in others], axis=0)),
                ],
                axis=0,
            )

        grad_value_ref[:, columns] = gather(chances, picked_grads).astype(BF16)
        grad_key_ref[:, columns] = (gather(slopes, picked_queries) * LN2).astype(BF16)
        return carry

    lax.fori_loop(0, HEADS // 2, pair_step, 0)


def head_sums(grad, context_t):
    product = grad.T.astype(F32) * context_t.astype(F32)
    return jnp.sum(product.reshape(HEADS, HEAD_DIM, product.shape[1]), axis=1)


def valid_rows_of(count, length):
    return (lax.broadcasted_iota(jnp.int32, (length, 1), 0) < count).astype(F32)


def forward_kernel(
    order_ref,
    target_ref,
    memory_length_ref,
    tokens_ref,
    memory_ref,
    vectors_ref,
    self_query,
    self_key,
    self_value,
    self_out,
    cross_query,
    cross_key,
    cross_value,
    cross_out,
    normed_expert_ref,
    later_ref,
    middle_ref,
    query_one_ref,
    key_one_ref,
    value_one_ref,
    context_one_ref,
    logsum_one_ref,
    query_two_ref,
    key_two_ref,
    value_two_ref,
    context_two_ref,
    logsum_two_ref,
    value_t_ref,
):
    sequence = order_ref[pl.program_id(0)]
    length = tokens_ref.shape[1]
    vector = lambda at: vectors_ref[at : at + 1, :]
    start = tokens_ref[0].astype(F32) * valid_rows_of(target_ref[sequence], length)
    normed = (normalise(start)[0] * vector(0) + vector(1)).astype(BF16)
    scale = SCORE_SCALE * LOG2E
    query_one_ref[0] = ((nn(normed, self_query[...]) + vector(2)) * scale).astype(BF16)
    key_one_ref[0] = nn(normed, self_key[...]).astype(BF16)
    value = (nn(normed, self_value[...]) + vector(3)).astype(BF16)
    value_one_ref[0] = value
    value_t_ref[...] = value.T
    attend(
        query_one_ref.at[0],
        key_one_ref.at[0],
        value_t_ref,
        context_one_ref.at[0],
        logsum_one_ref.at[0],
        None,
    )
    middle = start + tn(context_one_ref[0], self_out[...]) + vector(4)
    middle_ref[0] = middle
    normed = (normalise(middle)[0] * vector(5) + vector(6)).astype(BF16)
    memory = memory_ref[0]
    query_two_ref[0] = ((nn(normed, cross_query[...]) + vector(7)) * scale).astype(BF16)
    key_two_ref[0] = nn(memory, cross_key[...]).astype(BF16)
    value = (nn(memory, cross_value[...]) + vector(8)).astype(BF16)
    value_two_ref[0] = value
    value_t_ref[...] = value.T
    attend(
        query_two_ref.at[0],
        key_two_ref.at[0],
        value_t_ref,
        context_two_ref.at[0],
        logsum_two_ref.at[0],
        key_bias(memory_length_ref[sequence], memory.shape[0]),
    )
    later = middle_ref[0] + tn(context_two_ref[0], cross_out[...]) + vector(9)
    later_ref[0] = later
    normed_expert_ref[0] = (normalise(later)[0] * vector(10) + vector(11)).astype(BF16)


def silu_parts(pre):
    gate = 1.0 / (1.0 + jnp.exp2(pre * -LOG2E))
    return gate, pre * gate


def expert_kernel(
    pick_ref,
    used_ref,
    rows_ref,
    grads_ref,
    weight_in,
    bias_in,
    weight_out,
    bias_out,
    hidden_ref,
    grad_pre_ref,
    made_ref,
    grad_rows_ref,
    made_sum,
    grad_sum,
):
    tile = pl.program_id(0)
    last = pl.num_programs(0) - 1
    used = used_ref[0] > 0

    @pl.when(used)
    def _():
        pre = nn(rows_ref[...], weight_in[0]) + bias_in[0]
        gate, active = silu_parts(pre)
        hidden = active.astype(BF16)
        hidden_ref[...] = hidden
        grad_hidden = nt(grads_ref[...], weight_out[0]).astype(BF16).astype(F32)
        grad_pre = (grad_hidden * (gate * (1.0 + pre * (1.0 - gate)))).astype(BF16)
        grad_pre_ref[...] = grad_pre
        made = nn(hidden, weight_out[0])
        grad_rows = nt(grad_pre, weight_in[0])

        @pl.when(tile == 0)
        def _():
            made_sum[...] = made
            grad_sum[...] = grad_rows

        @pl.when(tile > 0)
        def _():
            made_sum[...] += made
            grad_sum[...] += grad_rows

        @pl.when(tile == last)
        def _():
            made_ref[...] = (made_sum[...] + bias_out[0]).astype(BF16)
            grad_rows_ref[...] = grad_sum[...].astype(BF16)

    @pl.when(jnp.logical_not(used))
    def _():
        hidden_ref[...] = jnp.zeros_like(hidden_ref)
        grad_pre_ref[...] = jnp.zeros_like(grad_pre_ref)
        made_ref[...] = jnp.zeros_like(made_ref)
        grad_rows_ref[...] = jnp.zeros_like(grad_rows_ref)


def expert_weights_kernel(slots, pick_ref, used_ref, *refs):
    rows, grads = refs[:slots], refs[slots : 2 * slots]
    hidden, grad_pre = refs[2 * slots : 3 * slots], refs[3 * slots : 4 * slots]
    in_ref, out_ref, in_bias_ref, out_bias_ref, in_sum, out_sum, in_bias, out_bias = refs[4 * slots :]
    for total in (in_sum, out_sum, in_bias, out_bias):
        total[...] = jnp.zeros_like(total)
    for slot in range(slots):

        @pl.when(used_ref[slot] > 0)
        def _():
            pick = pick_ref[slot]
            in_sum[pick] += tn(rows[slot][...], grad_pre[slot][...])
            out_sum[pick] += tn(hidden[slot][...], grads[slot][...])
            in_bias[pick] += column_sum(grad_pre[slot][...])
            out_bias[pick] += column_sum(grads[slot][...])

    in_ref[...] = in_sum[...].astype(BF16)
    out_ref[...] = out_sum[...].astype(BF16)
    in_bias_ref[...] = in_bias[...]
    out_bias_ref[...] = out_bias[...]


def output_kernel(slots, order_ref, target_ref, later_ref, *refs):
    made, output_ref = refs[:slots], refs[slots]
    position = pl.program_id(0)
    valid = valid_rows_of(target_ref[order_ref[position]], later_ref.shape[1])
    for at in range(slots):

        @pl.when(position == at)
        def _():
            output_ref[0] = ((later_ref[0] + made[at][...].astype(F32)) * valid).astype(BF16)


def cross_back_kernel(slots, order_ref, target_ref, memory_length_ref, *refs):
    grad_normed = refs[:slots]
    (
        cotangent_ref,
        memory_ref,
        later_ref,
        middle_ref,
        query_ref,
        key_ref,
        value_ref,
        context_ref,
        logsum_ref,
        vectors_ref,
        cross_query,
        cross_key,
        cross_value,
        cross_out,
        grad_middle_ref,
        memory_grad_ref,
        weights_ref,
        sums_ref,
        weight_sum,
        grad_expert,
        key_t,
        grad_context,
        delta,
        grad_query_t,
        grad_key,
        grad_value,
    ) = refs[slots:]
    position = pl.program_id(0)
    sequence = order_ref[position]
    length = cotangent_ref.shape[1]
    vector = lambda at: vectors_ref[at : at + 1, :]

    @pl.when(position == 0)
    def _():
        weight_sum[...] = jnp.zeros_like(weight_sum)
        sums_ref[...] = jnp.zeros_like(sums_ref)

    for at in range(slots):

        @pl.when(position == at)
        def _():
            grad_expert[...] = grad_normed[at][...]

    def add_vector(at, value):
        sums_ref[at : at + 1, :] += value

    valid = valid_rows_of(target_ref[sequence], length)
    normed, inverse = normalise(later_ref[0])
    grad = grad_expert[...].astype(F32)
    add_vector(0, column_sum(grad * normed))
    add_vector(1, column_sum(grad))
    grad_later = cotangent_ref[0].astype(F32) * valid + normalise_back(
        grad, normed, inverse, vector(10)
    )
    branch = grad_later.astype(BF16)
    grad_middle_ref[0] = grad_later
    add_vector(2, column_sum(branch))
    weight_sum[3] += nn(context_ref[0], branch)
    context_grad = nt(branch, cross_out[...]).astype(BF16)
    grad_context[...] = context_grad
    delta[...] = head_sums(context_grad, context_ref[0])
    key_t[...] = key_ref[0].T
    attend_back(
        query_ref.at[0],
        key_ref.at[0],
        value_ref.at[0],
        key_t,
        grad_context,
        delta,
        logsum_ref.at[0],
        grad_query_t,
        grad_key,
        grad_value,
        key_bias(memory_length_ref[sequence], memory_ref.shape[1]),
    )
    memory_t = memory_ref[0].T
    weight_sum[1] += nn(memory_t, grad_key[...])
    weight_sum[2] += nn(memory_t, grad_value[...])
    add_vector(3, column_sum(grad_value[...]))
    memory_grad_ref[0] = nt(grad_key[...], cross_key[...]) + nt(grad_value[...], cross_value[...])
    normed, inverse = normalise(middle_ref[0])
    weight_sum[0] += nn(grad_query_t[...], (normed * vector(5) + vector(6)).astype(BF16))
    grad_query = grad_query_t[...].T
    add_vector(4, column_sum(grad_query))
    grad = nt(grad_query, cross_query[...])
    add_vector(5, column_sum(grad * normed))
    add_vector(6, column_sum(grad))
    grad_middle_ref[0] += normalise_back(grad, normed, inverse, vector(5))

    @pl.when(position == pl.num_programs(0) - 1)
    def _():
        width = weight_sum.shape[1]
        weights_ref[:width] = weight_sum[0].T.astype(BF16)
        for at in (1, 2, 3):
            weights_ref[at * width : (at + 1) * width] = weight_sum[at].astype(BF16)


def self_back_kernel(
    order_ref,
    target_ref,
    tokens_ref,
    grad_middle_ref,
    query_ref,
    key_ref,
    value_ref,
    context_ref,
    logsum_ref,
    vectors_ref,
    self_query,
    self_key,
    self_value,
    self_out,
    tokens_grad_ref,
    weights_ref,
    sums_ref,
    weight_sum,
    key_t,
    grad_context,
    delta,
    grad_query_t,
    grad_key,
    grad_value,
):
    position = pl.program_id(0)
    sequence = order_ref[position]
    length = tokens_ref.shape[1]
    vector = lambda at: vectors_ref[at : at + 1, :]

    @pl.when(position == 0)
    def _():
        weight_sum[...] = jnp.zeros_like(weight_sum)
        sums_ref[...] = jnp.zeros_like(sums_ref)

    def add_vector(at, value):
        sums_ref[at : at + 1, :] += value

    valid = valid_rows_of(target_ref[sequence], length)
    branch = grad_middle_ref[0].astype(BF16)
    add_vector(0, column_sum(branch))
    weight_sum[3] += nn(context_ref[0], branch)
    context_grad = nt(branch, self_out[...]).astype(BF16)
    grad_context[...] = context_grad
    delta[...] = head_sums(context_grad, context_ref[0])
    key_t[...] = key_ref[0].T
    attend_back(
        query_ref.at[0],
        key_ref.at[0],
        value_ref.at[0],
        key_t,
        grad_context,
        delta,
        logsum_ref.at[0],
        grad_query_t,
        grad_key,
        grad_value,
        None,
    )
    normed, inverse = normalise(tokens_ref[0].astype(F32) * valid)
    inputs = (normed * vector(0) + vector(1)).astype(BF16)
    inputs_t = inputs.T
    weight_sum[0] += nn(grad_query_t[...], inputs)
    weight_sum[1] += nn(inputs_t, grad_key[...])
    weight_sum[2] += nn(inputs_t, grad_value[...])
    grad_query = grad_query_t[...].T
    add_vector(1, column_sum(grad_query))
    add_vector(2, column_sum(grad_value[...]))
    grad = (
        nt(grad_query, self_query[...])
        + nt(grad_key[...], self_key[...])
        + nt(grad_value[...], self_value[...])
    )
    add_vector(3, column_sum(grad * normed))
    add_vector(4, column_sum(grad))
    tokens_grad_ref[0] = (
        grad_middle_ref[0] + normalise_back(grad, normed, inverse, vector(0))
    ) * valid

    @pl.when(position == pl.num_programs(0) - 1)
    def _():
        width = weight_sum.shape[1]
        weights_ref[:width] = weight_sum[0].T.astype(BF16)
        for at in (1, 2, 3):
            weights_ref[at * width : (at + 1) * width] = weight_sum[at].astype(BF16)


def params(dims=1):
    return pltpu.CompilerParams(
        dimension_semantics=("arbitrary",) * dims, vmem_limit_bytes=VMEM_LIMIT
    )


def fixed(shape):
    return pl.BlockSpec(shape, lambda *_: (0,) * len(shape))


def at_position(shape):
    return pl.BlockSpec((1,) + shape, lambda step, *_: (step,) + (0,) * len(shape))


def at_sequence(shape):
    return pl.BlockSpec((1,) + shape, lambda step, order, *_: (order[step],) + (0,) * len(shape))


def struct(shape, kind):
    return jax.ShapeDtypeStruct(shape, kind)


def halves_step(parts, axis, bit):
    size = lax.axis_size(axis)
    route = [(place, place ^ bit) for place in range(size)]
    high = (lax.axis_index(axis) // bit) % 2
    kept = []
    for part in parts:
        half = part.shape[0] // 2
        given = lax.dynamic_slice_in_dim(part, (1 - high) * half, half, 0)
        mine = lax.dynamic_slice_in_dim(part, high * half, half, 0)
        got = lax.ppermute(given, axis, route)
        kept.append((mine.astype(F32) + got.astype(F32)).astype(BF16))
    return kept


def join_step(parts, axis, bit):
    size = lax.axis_size(axis)
    route = [(place, place ^ bit) for place in range(size)]
    high = (lax.axis_index(axis) // bit) % 2
    joined = []
    for part in parts:
        got = lax.ppermute(part, axis, route)
        low = jnp.where(high == 0, part, got)
        top = jnp.where(high == 0, got, part)
        joined.append(jnp.concatenate([low, top], axis=0))
    return joined


def bits_of(axis):
    return [1 << at for at in range(lax.axis_size(axis).bit_length() - 1)]


def sum_everywhere(rows):
    steps = [("dp", bit) for bit in bits_of("dp")] + [("expert", bit) for bit in bits_of("expert")]
    parts = [rows]
    for axis, bit in steps:
        parts = halves_step(parts, axis, bit)
    for axis, bit in steps[::-1]:
        parts = join_step(parts, axis, bit)
    return parts[0]


def on_device(
    tokens,
    memory,
    cotangent,
    target_length,
    memory_length,
    expert_of,
    self_norm_gain,
    self_norm_bias,
    self_query,
    self_key,
    self_value,
    self_out,
    self_query_bias,
    self_value_bias,
    self_out_bias,
    cross_norm_gain,
    cross_norm_bias,
    cross_query,
    cross_key,
    cross_value,
    cross_out,
    cross_attention_query_bias,
    cross_value_bias,
    cross_out_bias,
    expert_norm_gain,
    expert_norm_bias,
    expert_in,
    expert_in_bias,
    expert_out,
    expert_out_bias,
):
    seqs, length, width = tokens.shape
    mem_rows = memory.shape[1]
    local_count, _, hidden_width = expert_in.shape
    groups = lax.axis_size("expert")
    places = lax.axis_size("dp")
    own_group = lax.axis_index("expert")
    column = lax.axis_index("dp")

    shifts = [2, 1, 3, 0] if groups == 4 else [s for s in range(1, groups)] + [0]
    id_table = expert_of.reshape(groups, places, seqs)
    column_ids = lax.dynamic_index_in_dim(id_table, column, 1, False)
    own_ids = lax.dynamic_index_in_dim(column_ids, own_group, 0, False)
    distance = (own_ids // local_count - own_group) % groups
    shift_rank = jnp.zeros((groups,), jnp.int32).at[jnp.array(shifts)].set(jnp.arange(groups))
    rank = shift_rank[distance]
    position_of = jnp.sum(rank[:, None] > rank[None, :], axis=1).astype(jnp.int32)
    order = jnp.sum(
        jnp.where(position_of[None, :] == jnp.arange(seqs)[:, None], jnp.arange(seqs)[None, :], 0),
        axis=1,
    ).astype(jnp.int32)
    arriving = column_ids // local_count == own_group
    from_group_pick = jnp.sum(jnp.where(arriving, column_ids % local_count, 0), axis=1)
    from_group_used = jnp.any(arriving, axis=1)
    source = (own_group - jnp.array(shifts)) % groups
    picks = from_group_pick[source].astype(jnp.int32)
    used = from_group_used[source].astype(jnp.int32)
    whole = groups == seqs
    position_distance = distance[order]

    def outgoing(stack, slot):
        if whole:
            return stack[slot]
        match = position_distance == shifts[slot]
        return lax.dynamic_index_in_dim(stack, jnp.argmax(match), 0, False)

    def move(rows, slot, back=False):
        shift = shifts[slot]
        if shift == 0:
            return rows
        turn = -shift if back else shift
        return lax.ppermute(rows, "expert", [(g, (g + turn) % groups) for g in range(groups)])

    def arranged(per_slot):
        if whole:
            return per_slot
        stack = jnp.stack(per_slot)
        slot_at = shift_rank[position_distance]
        return [lax.dynamic_index_in_dim(stack, slot_at[at], 0, False) for at in range(seqs)]

    vectors = jnp.stack(
        [
            self_norm_gain,
            self_norm_bias,
            self_query_bias,
            self_value_bias,
            self_out_bias,
            cross_norm_gain,
            cross_norm_bias,
            cross_attention_query_bias,
            cross_value_bias,
            cross_out_bias,
            expert_norm_gain,
            expert_norm_bias,
        ]
        + [jnp.zeros_like(self_norm_gain)] * 4
    )
    rows_shape, square = (length, width), (width, width)
    mem_shape, heads_shape = (mem_rows, width), (HEADS, length)
    weights = [fixed(square)] * 4

    grads_home = (
        cotangent
        * (lax.broadcasted_iota(jnp.int32, cotangent.shape, 1) < target_length[:, None, None])
    )[order]
    grads_in = [move(outgoing(grads_home, slot), slot) for slot in range(groups)]

    saved = [
        (rows_shape, BF16),
        (rows_shape, F32),
        (rows_shape, F32),
        (rows_shape, BF16),
        (rows_shape, BF16),
        (rows_shape, BF16),
        ((width, length), BF16),
        (heads_shape, F32),
        (rows_shape, BF16),
        (mem_shape, BF16),
        (mem_shape, BF16),
        ((width, length), BF16),
        (heads_shape, F32),
    ]
    (
        normed_expert,
        later,
        middle,
        query_one,
        key_one,
        value_one,
        context_one,
        logsum_one,
        query_two,
        key_two,
        value_two,
        context_two,
        logsum_two,
    ) = pl.pallas_call(
        forward_kernel,
        grid_spec=pltpu.PrefetchScalarGridSpec(
            num_scalar_prefetch=3,
            grid=(seqs,),
            in_specs=[at_sequence(rows_shape), at_sequence(mem_shape), fixed(vectors.shape)]
            + weights
            + weights,
            out_specs=[at_position(shape) for shape, _ in saved],
            scratch_shapes=[pltpu.VMEM((width, length), BF16)],
        ),
        out_shape=[struct((seqs,) + shape, kind) for shape, kind in saved],
        compiler_params=params(),
        name="forward",
    )(
        order,
        target_length,
        memory_length,
        tokens,
        memory,
        vectors,
        self_query,
        self_key,
        self_value,
        self_out,
        cross_query,
        cross_key,
        cross_value,
        cross_out,
    )

    rows_in = [move(outgoing(normed_expert, slot), slot) for slot in range(groups)]
    tiles = 4
    tile_width = hidden_width // tiles
    in_tile = pl.BlockSpec((1, width, tile_width), lambda t, pick, _: (pick[0], 0, t))
    out_tile = pl.BlockSpec((1, tile_width, width), lambda t, pick, _: (pick[0], t, 0))
    hidden_tile = pl.BlockSpec((length, tile_width), lambda t, *_: (0, t))
    hidden, grad_pre, made, grad_rows = [], [], [], []
    for slot in range(groups):
        results = pl.pallas_call(
            expert_kernel,
            grid_spec=pltpu.PrefetchScalarGridSpec(
                num_scalar_prefetch=2,
                grid=(tiles,),
                in_specs=[
                    fixed(rows_shape),
                    fixed(rows_shape),
                    in_tile,
                    pl.BlockSpec((1, 1, tile_width), lambda t, pick, _: (pick[0], 0, t)),
                    out_tile,
                    pl.BlockSpec((1, 1, width), lambda t, pick, _: (pick[0], 0, 0)),
                ],
                out_specs=[hidden_tile, hidden_tile, fixed(rows_shape), fixed(rows_shape)],
                scratch_shapes=[pltpu.VMEM(rows_shape, F32)] * 2,
            ),
            out_shape=[struct((length, hidden_width), BF16)] * 2 + [struct(rows_shape, BF16)] * 2,
            compiler_params=params(),
            name="expert",
        )(
            picks[slot : slot + 1],
            used[slot : slot + 1],
            rows_in[slot],
            grads_in[slot],
            expert_in,
            expert_in_bias[:, None, :],
            expert_out,
            expert_out_bias[:, None, :],
        )
        for table, result in zip((hidden, grad_pre, made, grad_rows), results):
            table.append(result)

    grad_home = arranged([move(grad_rows[slot], slot, True) for slot in range(groups)])
    made_home = arranged([move(made[slot], slot, True) for slot in range(groups)])

    in_sums, out_sums, in_bias_sums, out_bias_sums = pl.pallas_call(
        functools.partial(expert_weights_kernel, groups),
        grid_spec=pltpu.PrefetchScalarGridSpec(
            num_scalar_prefetch=2,
            grid=(tiles,),
            in_specs=[fixed(rows_shape)] * (2 * groups) + [hidden_tile] * (2 * groups),
            out_specs=[
                pl.BlockSpec((local_count, width, tile_width), lambda t, *_: (0, 0, t)),
                pl.BlockSpec((local_count, tile_width, width), lambda t, *_: (0, t, 0)),
                pl.BlockSpec((local_count, 1, tile_width), lambda t, *_: (0, 0, t)),
                fixed((local_count, 1, width)),
            ],
            scratch_shapes=[
                pltpu.VMEM((local_count, width, tile_width), F32),
                pltpu.VMEM((local_count, tile_width, width), F32),
                pltpu.VMEM((local_count, 1, tile_width), F32),
                pltpu.VMEM((local_count, 1, width), F32),
            ],
        ),
        out_shape=[
            struct((local_count, width, hidden_width), BF16),
            struct((local_count, hidden_width, width), BF16),
            struct((local_count, 1, hidden_width), F32),
            struct((local_count, 1, width), F32),
        ],
        compiler_params=params(),
        name="expert_weights",
    )(picks, used, *rows_in, *grads_in, *hidden, *grad_pre)
    expert_in_grad = lax.psum_scatter(in_sums, "dp", scatter_dimension=1, tiled=True)
    expert_out_grad = lax.psum_scatter(out_sums, "dp", scatter_dimension=1, tiled=True)

    back_scratch = [
        pltpu.VMEM((4,) + square, F32),
        pltpu.VMEM((width, mem_rows), BF16),
        pltpu.VMEM(rows_shape, BF16),
        pltpu.VMEM(heads_shape, F32),
        pltpu.VMEM((width, length), BF16),
        pltpu.VMEM(mem_shape, BF16),
        pltpu.VMEM(mem_shape, BF16),
    ]
    grad_middle, memory_grad, cross_weights, cross_sums = pl.pallas_call(
        functools.partial(cross_back_kernel, seqs),
        grid_spec=pltpu.PrefetchScalarGridSpec(
            num_scalar_prefetch=3,
            grid=(seqs,),
            in_specs=[fixed(rows_shape)] * seqs
            + [
                at_sequence(rows_shape),
                at_sequence(mem_shape),
                at_position(rows_shape),
                at_position(rows_shape),
                at_position(rows_shape),
                at_position(mem_shape),
                at_position(mem_shape),
                at_position((width, length)),
                at_position(heads_shape),
                fixed(vectors.shape),
            ]
            + weights,
            out_specs=[
                at_position(rows_shape),
                at_sequence(mem_shape),
                fixed((4 * width, width)),
                fixed((8, width)),
            ],
            scratch_shapes=back_scratch[:1] + [pltpu.VMEM(rows_shape, BF16)] + back_scratch[1:],
        ),
        out_shape=[
            struct((seqs,) + rows_shape, F32),
            struct((seqs,) + mem_shape, F32),
            struct((4 * width, width), BF16),
            struct((8, width), F32),
        ],
        compiler_params=params(),
        name="cross_back",
    )(
        order,
        target_length,
        memory_length,
        *grad_home,
        cotangent,
        memory,
        later,
        middle,
        query_two,
        key_two,
        value_two,
        context_two,
        logsum_two,
        vectors,
        cross_query,
        cross_key,
        cross_value,
        cross_out,
    )
    cross_totals = sum_everywhere(cross_weights)

    tokens_grad, self_weights, self_sums = pl.pallas_call(
        self_back_kernel,
        grid_spec=pltpu.PrefetchScalarGridSpec(
            num_scalar_prefetch=2,
            grid=(seqs,),
            in_specs=[
                at_sequence(rows_shape),
                at_position(rows_shape),
                at_position(rows_shape),
                at_position(rows_shape),
                at_position(rows_shape),
                at_position((width, length)),
                at_position(heads_shape),
                fixed(vectors.shape),
            ]
            + weights,
            out_specs=[at_sequence(rows_shape), fixed((4 * width, width)), fixed((8, width))],
            scratch_shapes=back_scratch,
        ),
        out_shape=[
            struct((seqs,) + rows_shape, F32),
            struct((4 * width, width), BF16),
            struct((8, width), F32),
        ],
        compiler_params=params(),
        name="self_back",
    )(
        order,
        target_length,
        tokens,
        grad_middle,
        query_one,
        key_one,
        value_one,
        context_one,
        logsum_one,
        vectors,
        self_query,
        self_key,
        self_value,
        self_out,
    )
    self_totals = sum_everywhere(self_weights)
    output = pl.pallas_call(
        functools.partial(output_kernel, seqs),
        grid_spec=pltpu.PrefetchScalarGridSpec(
            num_scalar_prefetch=2,
            grid=(seqs,),
            in_specs=[at_position(rows_shape)] + [fixed(rows_shape)] * seqs,
            out_specs=[at_sequence(rows_shape)],
        ),
        out_shape=[struct((seqs,) + rows_shape, BF16)],
        compiler_params=params(),
        name="output",
    )(order, target_length, later, *made_home)[0]

    totals = lax.psum(jnp.concatenate([self_sums, cross_sums], axis=0), ("expert", "dp"))
    cross_q, cross_k, cross_v, cross_o = [
        cross_totals[at * width : (at + 1) * width].astype(F32) for at in range(4)
    ]
    self_q, self_k, self_v, self_o = [
        self_totals[at * width : (at + 1) * width].astype(F32) for at in range(4)
    ]
    bias_share = lax.psum_scatter(in_bias_sums[:, 0], "dp", scatter_dimension=1, tiled=True)
    out_bias_share = lax.psum_scatter(out_bias_sums[:, 0], "dp", scatter_dimension=1, tiled=True)
    return (
        output,
        tokens_grad,
        memory_grad,
        totals[3],
        totals[4],
        self_q,
        self_k,
        self_v,
        self_o,
        totals[1],
        totals[2],
        totals[0],
        totals[13],
        totals[14],
        cross_q,
        cross_k,
        cross_v,
        cross_o,
        totals[12],
        totals[11],
        totals[10],
        totals[8],
        totals[9],
        expert_in_grad.astype(F32),
        bias_share,
        expert_out_grad.astype(F32),
        out_bias_share,
    )


def solution(mesh):
    rows = P(("expert", "dp"), None, None)
    counts = P(("expert", "dp"))
    split = (P("expert", None, None), P("expert", None)) * 2
    shares = (P("expert", "dp", None), P("expert", "dp")) * 2
    return jax.shard_map(
        on_device,
        mesh=mesh,
        in_specs=(rows,) * 3 + (counts,) * 2 + (P(),) * 21 + split,
        out_specs=(rows,) * 3 + (P(),) * 20 + shares,
        check_vma=False,
    )
```

```python
import functools

import jax
import jax.numpy as jnp
from jax import lax
from jax.experimental import pallas as pl
from jax.experimental.pallas import tpu as pltpu
from jax.sharding import PartitionSpec as P

HEADS = 8
HEAD_DIM = 64
PAIR = 2 * HEAD_DIM
EPSILON = 1e-05
SCORE_SCALE = 0.125
NEGATIVE = -1e30
SAFE_SCORE = 80.0
SHARED_LINES = 16
EXPERT_LINES = 16
LINES = SHARED_LINES + EXPERT_LINES
LOG2E = 1.4426950408889634
LN2 = 0.6931471805599453
VMEM_LIMIT = 63 * 1024 * 1024
F32 = jnp.float32
BF16 = jnp.bfloat16


def contract(left, right, left_dim, right_dim):
    return lax.dot_general(
        left, right, (((left_dim,), (right_dim,)), ((), ())), preferred_element_type=F32
    )


def nn(left, right):
    return contract(left, right, 1, 0)


def nt(left, right):
    return contract(left, right, 1, 1)


def tn(left, right):
    return contract(left, right, 0, 0)


def normalise(rows):
    centre = rows - jnp.mean(rows, axis=-1, keepdims=True)
    inverse = lax.rsqrt(jnp.mean(centre * centre, axis=-1, keepdims=True) + EPSILON)
    return centre * inverse, inverse


def normalise_back(grad, normed, inverse, gain):
    scaled = grad * gain
    return inverse * (
        scaled
        - jnp.mean(scaled, axis=-1, keepdims=True)
        - normed * jnp.mean(scaled * normed, axis=-1, keepdims=True)
    )


def column_sum(rows):
    return jnp.sum(rows.astype(F32), axis=0, keepdims=True)


def head_masks():
    lane = lax.broadcasted_iota(jnp.int32, (1, PAIR), 1)
    mine = [(lane // HEAD_DIM == half).astype(F32).astype(BF16) for half in (0, 1)]
    spare = [(lane == HEAD_DIM * (1 - half)).astype(F32).astype(BF16) for half in (0, 1)]
    return mine, spare


def key_bias(count, mem_rows):
    place = lax.broadcasted_iota(jnp.int32, (mem_rows, PAIR), 0)
    return jnp.where(place < count, 0.0, NEGATIVE).astype(BF16)


def score_operands(keys, queries, half, mine, spare, bias):
    picked = queries * mine[half]
    if bias is None:
        return keys, picked
    return keys * (1 - spare[half]) + bias * spare[half], picked + spare[half]


def causal(scores, block):
    key_at = lax.broadcasted_iota(jnp.int32, (scores.shape[0], block), 0)
    query_at = lax.broadcasted_iota(jnp.int32, (scores.shape[0], block), 1)
    return jnp.where(key_at <= query_at, scores, NEGATIVE)


def lower(items, block):
    return jnp.concatenate([item[block:] for item in items], axis=0)


def lower_columns(items, block):
    return jnp.concatenate([item[:, block:] for item in items], axis=1)


def head_rows(pair, half):
    return pl.ds(pl.multiple_of(pair * PAIR + half * HEAD_DIM, HEAD_DIM), HEAD_DIM)


def pair_span(pair):
    return pl.ds(pl.multiple_of(pair * PAIR, PAIR), PAIR)


def head_part(both, half, block):
    return both[half * HEAD_DIM : (half + 1) * HEAD_DIM, half * block : (half + 1) * block]


def causal_pair_scores(keys, picked, block):
    upper = []
    for half in (0, 1):
        scores = nt(keys[:block], picked[half])
        upper.append(
            jnp.concatenate([causal(scores[:, :block], block), scores[:, block:]], axis=1)
        )
    scores = nt(keys[block:], lower(picked, block))
    low = jnp.concatenate([causal(scores[:, :block], block), causal(scores[:, block:], block)], axis=1)
    return upper, low


def head_blocks():
    feature = lax.broadcasted_iota(jnp.int32, (HEADS * HEAD_DIM, 128), 0)
    return (feature // HEAD_DIM == lax.broadcasted_iota(jnp.int32, (HEADS * HEAD_DIM, 128), 1)).astype(BF16)


def scores_small(query_ref, key_ref):
    blocks = head_blocks()
    squares = [nn(ref[...] * ref[...], blocks) for ref in (query_ref, key_ref)]
    most = [jnp.max(item, axis=0, keepdims=True) for item in squares]
    return jnp.max(most[0] * most[1]) < SAFE_SCORE * SAFE_SCORE


def attend_cross(plain, query_ref, key_ref, value_t_ref, context_t_ref, logsum_ref, bias):
    mine, spare = head_masks()

    def pair_step(pair, carry):
        columns = pair_span(pair)
        keys, queries = key_ref[:, columns], query_ref[:, columns]
        for half in (0, 1):
            rows = head_rows(pair, half)
            left, right = score_operands(keys, queries, half, mine, spare, bias)
            scores = nt(left, right)
            highest = 0.0 if plain else jnp.max(scores, axis=0, keepdims=True)
            raised = jnp.exp2(scores if plain else scores - highest)
            summed = jnp.sum(raised, axis=0, keepdims=True)
            context = nn(value_t_ref[rows, :], raised.astype(BF16))
            context_t_ref[rows, :] = (context * (1.0 / summed)).astype(BF16)
            logsum_ref[pl.ds(2 * pair + half, 1), :] = highest + LOG2E * jnp.log(summed)
        return carry

    lax.fori_loop(0, HEADS // 2, pair_step, 0)


def attend_self(plain, query_ref, key_ref, value_t_ref, context_t_ref, logsum_ref):
    block = query_ref.shape[0] // 2
    mine, _ = head_masks()

    def pair_step(pair, carry):
        columns = pair_span(pair)
        keys, queries = key_ref[:, columns], query_ref[:, columns]
        upper, low = causal_pair_scores(keys, [queries * mine[0], queries * mine[1]], block)
        if plain:
            highest = [0.0, 0.0]
            low = jnp.exp2(low)
        else:
            low_top = jnp.max(low, axis=0, keepdims=True)
            highest = []
            for half in (0, 1):
                top = jnp.max(upper[half], axis=0, keepdims=True)
                other = low_top[:, half * block : (half + 1) * block]
                highest.append(
                    jnp.concatenate([top[:, :block], jnp.maximum(top[:, block:], other)], axis=1)
                )
            low = jnp.exp2(low - lower_columns(highest, block))
        low_sum = jnp.sum(low, axis=0, keepdims=True)
        low_context = nn(value_t_ref[columns, block:], low.astype(BF16))
        for half in (0, 1):
            rows = head_rows(pair, half)
            raised = jnp.exp2(upper[half] if plain else upper[half] - highest[half])
            summed = jnp.sum(raised, axis=0, keepdims=True)
            part = low_sum[:, half * block : (half + 1) * block]
            summed = jnp.concatenate([summed[:, :block], summed[:, block:] + part], axis=1)
            context = nn(value_t_ref[rows, :block], raised.astype(BF16))
            context = jnp.concatenate(
                [context[:, :block], context[:, block:] + head_part(low_context, half, block)],
                axis=1,
            )
            context_t_ref[rows, :] = (context * (1.0 / summed)).astype(BF16)
            logsum_ref[pl.ds(2 * pair + half, 1), :] = highest[half] + LOG2E * jnp.log(summed)
        return carry

    lax.fori_loop(0, HEADS // 2, pair_step, 0)


def attend(kind, query_ref, key_ref, *refs):
    small = scores_small(query_ref, key_ref)

    @pl.when(small)
    def _():
        kind(True, query_ref, key_ref, *refs)

    @pl.when(jnp.logical_not(small))
    def _():
        kind(False, query_ref, key_ref, *refs)


def attend_cross_back(
    query_ref,
    key_ref,
    value_ref,
    key_t_ref,
    grad_ref,
    delta_ref,
    logsum_ref,
    grad_query_t_ref,
    grad_key_ref,
    grad_value_ref,
    bias,
):
    mine, spare = head_masks()

    def pair_step(pair, carry):
        columns = pair_span(pair)
        keys, queries, values = key_ref[:, columns], query_ref[:, columns], value_ref[:, columns]
        grads = grad_ref[:, columns]
        chances, slopes, picked_grads, picked_queries = [], [], [], []
        for half in (0, 1):
            head, rows = pl.ds(2 * pair + half, 1), head_rows(pair, half)
            left, right = score_operands(keys, queries, half, mine, spare, bias)
            picked_grads.append(grads * mine[half])
            picked_queries.append(queries * mine[half])
            chance = jnp.exp2(nt(left, right) - logsum_ref[head, :])
            slope = chance * (nt(values, picked_grads[half]) - delta_ref[head, :])
            chances.append(chance.astype(BF16))
            slopes.append(slope.astype(BF16))
            grad_query_t_ref[rows, :] = (nn(key_t_ref[rows, :], slopes[half]) * SCORE_SCALE).astype(
                BF16
            )
        grad_value_ref[:, columns] = nn(
            jnp.concatenate(chances, axis=1), jnp.concatenate(picked_grads, axis=0)
        ).astype(BF16)
        grad_key_ref[:, columns] = (
            nn(jnp.concatenate(slopes, axis=1), jnp.concatenate(picked_queries, axis=0)) * LN2
        ).astype(BF16)
        return carry

    lax.fori_loop(0, HEADS // 2, pair_step, 0)


def attend_self_back(
    query_ref,
    key_ref,
    value_ref,
    key_t_ref,
    grad_ref,
    delta_ref,
    logsum_ref,
    grad_query_t_ref,
    grad_key_ref,
    grad_value_ref,
):
    block = query_ref.shape[0] // 2
    mine, _ = head_masks()

    def pair_step(pair, carry):
        columns = pair_span(pair)
        keys, queries, values = key_ref[:, columns], query_ref[:, columns], value_ref[:, columns]
        grads = grad_ref[:, columns]
        picked = [queries * mine[0], queries * mine[1]]
        picked_grads = [grads * mine[0], grads * mine[1]]
        upper, low = causal_pair_scores(keys, picked, block)
        logsum = [logsum_ref[pl.ds(2 * pair + half, 1), :] for half in (0, 1)]
        delta = [delta_ref[pl.ds(2 * pair + half, 1), :] for half in (0, 1)]
        low_grads = lower(picked_grads, block)
        low = jnp.exp2(low - lower_columns(logsum, block))
        low_slope = (
            low * (nt(values[block:], low_grads) - lower_columns(delta, block))
        ).astype(BF16)
        low_query = nn(key_t_ref[columns, block:], low_slope)
        chances, slopes = [], []
        for half in (0, 1):
            chance = jnp.exp2(upper[half] - logsum[half])
            slope = chance * (nt(values[:block], picked_grads[half]) - delta[half])
            chances.append(chance.astype(BF16))
            slopes.append(slope.astype(BF16))
            rows = head_rows(pair, half)
            grad = nn(key_t_ref[rows, :block], slopes[half])
            grad = jnp.concatenate(
                [grad[:, :block], grad[:, block:] + head_part(low_query, half, block)], axis=1
            )
            grad_query_t_ref[rows, :] = (grad * SCORE_SCALE).astype(BF16)
        grad_value_ref[:block, columns] = nn(
            jnp.concatenate(chances, axis=1), jnp.concatenate(picked_grads, axis=0)
        ).astype(BF16)
        grad_value_ref[block:, columns] = nn(low.astype(BF16), low_grads).astype(BF16)
        grad_key_ref[:block, columns] = (
            nn(jnp.concatenate(slopes, axis=1), jnp.concatenate(picked, axis=0)) * LN2
        ).astype(BF16)
        grad_key_ref[block:, columns] = (nn(low_slope, lower(picked, block)) * LN2).astype(BF16)
        return carry

    lax.fori_loop(0, HEADS // 2, pair_step, 0)


def head_sums(grad, context_t):
    product = grad.T.astype(F32) * context_t.astype(F32)
    return jnp.sum(product.reshape(HEADS, HEAD_DIM, product.shape[1]), axis=1)


def valid_rows_of(count, length):
    return (lax.broadcasted_iota(jnp.int32, (length, 1), 0) < count).astype(F32)


def forward_kernel(
    start_at,
    steps,
    order_ref,
    target_ref,
    memory_length_ref,
    tokens_ref,
    memory_ref,
    vectors_ref,
    self_query,
    self_key,
    self_value,
    self_out,
    cross_query,
    cross_key,
    cross_value,
    cross_out,
    *refs,
):
    normed_refs, refs = refs[:steps], refs[steps:]
    (
    later_ref,
    middle_ref,
    query_one_ref,
    key_one_ref,
    value_one_ref,
    context_one_ref,
    logsum_one_ref,
    query_two_ref,
    key_two_ref,
    value_two_ref,
    context_two_ref,
    logsum_two_ref,
    value_t_ref,
    ) = refs
    step = pl.program_id(0)
    sequence = order_ref[start_at + step]
    length = tokens_ref.shape[1]
    vector = lambda at: vectors_ref[at : at + 1, :]
    start = tokens_ref[0].astype(F32) * valid_rows_of(target_ref[sequence], length)
    normed = (normalise(start)[0] * vector(0) + vector(1)).astype(BF16)
    scale = SCORE_SCALE * LOG2E
    query_one_ref[0] = ((nn(normed, self_query[...]) + vector(2)) * scale).astype(BF16)
    key_one_ref[0] = nn(normed, self_key[...]).astype(BF16)
    value = (nn(normed, self_value[...]) + vector(3)).astype(BF16)
    value_one_ref[0] = value
    value_t_ref[...] = value.T
    attend(
        attend_self,
        query_one_ref.at[0],
        key_one_ref.at[0],
        value_t_ref,
        context_one_ref.at[0],
        logsum_one_ref.at[0],
    )
    middle = start + tn(context_one_ref[0], self_out[...]) + vector(4)
    middle_ref[0] = middle
    normed = (normalise(middle)[0] * vector(5) + vector(6)).astype(BF16)
    memory = memory_ref[0]
    query_two_ref[0] = ((nn(normed, cross_query[...]) + vector(7)) * scale).astype(BF16)
    key_two_ref[0] = nn(memory, cross_key[...]).astype(BF16)
    value = (nn(memory, cross_value[...]) + vector(8)).astype(BF16)
    value_two_ref[0] = value
    value_t_ref[...] = value.T
    attend(
        attend_cross,
        query_two_ref.at[0],
        key_two_ref.at[0],
        value_t_ref,
        context_two_ref.at[0],
        logsum_two_ref.at[0],
        key_bias(memory_length_ref[sequence], memory.shape[0]),
    )
    later = middle_ref[0] + tn(context_two_ref[0], cross_out[...]) + vector(9)
    later_ref[0] = later
    normed = (normalise(later)[0] * vector(10) + vector(11)).astype(BF16)
    for at in range(steps):

        @pl.when(step == at)
        def _():
            normed_refs[at][...] = normed


def expert_kernel(
    slot,
    pick_ref,
    used_ref,
    rows_ref,
    grads_ref,
    weight_in,
    bias_in,
    weight_out,
    bias_out,
    hidden_ref,
    grad_pre_ref,
    made_ref,
    grad_rows_ref,
    pre_sum_ref,
    grads_sum_ref,
    made_sum,
    grad_sum,
):
    tile = pl.program_id(0)
    last = pl.num_programs(0) - 1
    used = used_ref[slot] > 0
    pick = pl.ds(pick_ref[slot], 1)

    @pl.when(used)
    def _():
        pre = nn(rows_ref[...], weight_in[0]) + bias_in[pick, :]
        grad_hidden = nt(grads_ref[...], weight_out[0])
        gate = 0.5 * jnp.tanh(0.5 * pre) + 0.5
        active = pre * gate
        hidden = active.astype(BF16)
        hidden_ref[...] = hidden
        grad_pre = grad_hidden * (gate + active * (1.0 - gate))
        pre_sum_ref[...] = jnp.sum(grad_pre, axis=0, keepdims=True)
        grad_pre = grad_pre.astype(BF16)
        grad_pre_ref[...] = grad_pre
        made = nn(hidden, weight_out[0])
        grad_rows = nt(grad_pre, weight_in[0])

        @pl.when(tile == 0)
        def _():
            made_sum[...] = made
            grad_sum[...] = grad_rows
            grads_sum_ref[...] = column_sum(grads_ref[...])

        @pl.when(tile > 0)
        def _():
            made_sum[...] += made
            grad_sum[...] += grad_rows

        @pl.when(tile == last)
        def _():
            made_ref[...] = (made_sum[...] + bias_out[pick, :]).astype(BF16)
            grad_rows_ref[...] = grad_sum[...].astype(BF16)

    @pl.when(jnp.logical_not(used))
    def _():
        for ref in (hidden_ref, grad_pre_ref, made_ref, grad_rows_ref, pre_sum_ref, grads_sum_ref):
            ref[...] = jnp.zeros_like(ref)


def expert_weights_kernel(slots, pick_ref, used_ref, *refs):
    rows, grads, hidden, grad_pre, pre_sum, grads_sum = [
        refs[at * slots : (at + 1) * slots] for at in range(6)
    ]
    in_ref, out_ref, lines_ref, in_sum, out_sum, in_bias, out_bias = refs[6 * slots :]
    for total in (in_sum, out_sum, in_bias, out_bias):
        total[...] = jnp.zeros_like(total)
    for slot in range(slots):

        @pl.when(used_ref[slot] > 0)
        def _():
            pick = pick_ref[slot]
            in_sum[pick] += tn(rows[slot][...], grad_pre[slot][...])
            out_sum[pick] += tn(hidden[slot][...], grads[slot][...])
            in_bias[pick] += pre_sum[slot][...]
            out_bias[pick] += grads_sum[slot][...]

    in_ref[...] = in_sum[...].astype(BF16)
    out_ref[...] = out_sum[...].astype(BF16)
    tile, tiles = pl.program_id(0), pl.num_programs(0)
    count = in_bias.shape[0]

    @pl.when(tile == 0)
    def _():
        lines_ref[...] = jnp.zeros_like(lines_ref)

    for pick in range(count):
        lines_ref[pl.ds(pick * tiles + tile, 1), :] = in_bias[pick]
        lines_ref[pl.ds(count * tiles + pick, 1), :] = out_bias[pick]


def plan_kernel(
    shifts,
    local_count,
    place_ref,
    expert_ref,
    target_ref,
    cotangent_ref,
    order_ref,
    pick_ref,
    used_ref,
    slot_ref,
    spot_ref,
    *grads_refs,
):
    groups, seqs = len(shifts), cotangent_ref.shape[0]
    own, column, places = place_ref[0], place_ref[1], place_ref[2]
    own_ids = [expert_ref[(own * places + column) * seqs + at] for at in range(seqs)]
    distance = [lax.rem(lax.div(item, local_count) - own + groups, groups) for item in own_ids]
    slots = [
        sum((jnp.where(item == shift, at, 0) for at, shift in enumerate(shifts)), jnp.int32(0))
        for item in distance
    ]
    for slot in range(groups):
        spot_ref[slot] = 0
        source = lax.rem(own - shifts[slot] + groups, groups)
        pick, used = jnp.int32(0), jnp.int32(0)
        for at in range(seqs):
            item = expert_ref[(source * places + column) * seqs + at]
            here = lax.div(item, local_count) == own
            pick = jnp.where(here, lax.rem(item, local_count), pick)
            used = jnp.where(here, 1, used)
        pick_ref[slot] = pick
        used_ref[slot] = used
    for at in range(seqs):
        spot = sum((jnp.where(other < slots[at], 1, 0) for other in slots), jnp.int32(0))
        order_ref[spot] = at
        slot_ref[spot] = slots[at]
        spot_ref[slots[at]] = spot
    order_ref[seqs] = order_ref[0]
    length = cotangent_ref.shape[1]
    for slot in range(groups):
        sequence = order_ref[spot_ref[slot]]
        valid = valid_rows_of(target_ref[sequence], length)
        grads_refs[slot][...] = (cotangent_ref[sequence].astype(F32) * valid).astype(BF16)


def output_kernel(slots, order_ref, target_ref, later_ref, *refs):
    made, output_ref = refs[:slots], refs[slots]
    position = pl.program_id(0)
    valid = valid_rows_of(target_ref[order_ref[position]], later_ref.shape[1])
    for at in range(slots):

        @pl.when(position == at)
        def _():
            output_ref[0] = ((later_ref[0] + made[at][...].astype(F32)) * valid).astype(BF16)


def open_sums(first, weight_sum, vector_sum, given):
    @pl.when(pl.program_id(0) == 0)
    def _():
        if first:
            weight_sum[...] = jnp.zeros_like(weight_sum)
            vector_sum[...] = jnp.zeros_like(vector_sum)
        else:
            weight_sum[...] = given[0][...]
            vector_sum[...] = given[1][...]


def put_halves(squares, lines, high, keep_ref, give_ref):
    height = squares[0].shape[0]
    half = height * len(squares) // 2
    for top, (low_ref, high_ref) in ((0, (keep_ref, give_ref)), (1, (give_ref, keep_ref))):

        @pl.when(high == top)
        def _():
            for at, square in enumerate(squares):
                for part, ref in enumerate((low_ref, high_ref)):
                    start, stop = max(at * height, part * half), min((at + 1) * height, (part + 1) * half)
                    if start < stop:
                        rows = square[start - at * height : stop - at * height]
                        ref[start - part * half : stop - part * half] = rows.astype(BF16)

    if lines is not None:
        keep_ref[half:] = lines.astype(BF16)
        give_ref[half:] = lines.astype(BF16)


def close_sums(final, weight_sum, vector_sum, high, outs):
    @pl.when(pl.program_id(0) == pl.num_programs(0) - 1)
    def _():
        outs[-1][...] = vector_sum[...]
        if final:
            squares = [weight_sum[0].T] + [weight_sum[at] for at in range(1, weight_sum.shape[0])]
            put_halves(squares, None, high, outs[0], outs[1])
        else:
            outs[0][...] = weight_sum[...]


def cross_back_kernel(
    start_at, first, final, slots, order_ref, target_ref, memory_length_ref, high_ref, *refs
):
    grad_normed, refs = refs[:slots], refs[slots:]
    given, refs = (None, refs) if first else (refs[:2], refs[2:])
    (
        cotangent_ref,
        memory_ref,
        later_ref,
        middle_ref,
        query_ref,
        key_ref,
        value_ref,
        context_ref,
        logsum_ref,
        context_one_ref,
        vectors_ref,
        cross_query,
        cross_key,
        cross_value,
        cross_out,
        grad_middle_ref,
        grad_key_ref,
        grad_value_ref,
        *outs,
        weight_sum,
        vector_sum,
        grad_expert,
        key_t,
        grad_context,
        delta,
        grad_query_t,
    ) = refs
    step = pl.program_id(0)
    sequence = order_ref[lax.rem(start_at + step, order_ref.shape[0] - 1)]
    length = cotangent_ref.shape[1]
    vector = lambda at: vectors_ref[at : at + 1, :]
    open_sums(first, weight_sum, vector_sum, given)

    for at in range(slots):

        @pl.when(step == at)
        def _():
            grad_expert[...] = grad_normed[at][...]

    def add_vector(at, value):
        vector_sum[at : at + 1, :] += value

    valid = valid_rows_of(target_ref[sequence], length)
    normed, inverse = normalise(later_ref[0])
    grad = grad_expert[...].astype(F32)
    add_vector(0, column_sum(grad * normed))
    add_vector(1, column_sum(grad))
    grad_later = cotangent_ref[0].astype(F32) * valid + normalise_back(
        grad, normed, inverse, vector(10)
    )
    branch = grad_later.astype(BF16)
    grad_middle_ref[0] = grad_later
    add_vector(2, column_sum(branch))
    weight_sum[3] += nn(context_ref[0], branch)
    context_grad = nt(branch, cross_out[...]).astype(BF16)
    grad_context[...] = context_grad
    delta[...] = head_sums(context_grad, context_ref[0])
    key_t[...] = key_ref[0].T
    attend_cross_back(
        query_ref.at[0],
        key_ref.at[0],
        value_ref.at[0],
        key_t,
        grad_context,
        delta,
        logsum_ref.at[0],
        grad_query_t,
        grad_key_ref.at[0],
        grad_value_ref.at[0],
        key_bias(memory_length_ref[sequence], memory_ref.shape[1]),
    )
    memory_t = memory_ref[0].T
    weight_sum[1] += nn(memory_t, grad_key_ref[0])
    weight_sum[2] += nn(memory_t, grad_value_ref[0])
    add_vector(3, column_sum(grad_value_ref[0]))
    normed, inverse = normalise(middle_ref[0])
    weight_sum[0] += nn(grad_query_t[...], (normed * vector(5) + vector(6)).astype(BF16))
    grad_query = grad_query_t[...].T
    add_vector(4, column_sum(grad_query))
    grad = nt(grad_query, cross_query[...])
    add_vector(5, column_sum(grad * normed))
    add_vector(6, column_sum(grad))
    grad_middle = grad_middle_ref[0] + normalise_back(grad, normed, inverse, vector(5))
    grad_middle_ref[0] = grad_middle
    branch = grad_middle.astype(BF16)
    add_vector(7, column_sum(branch))
    weight_sum[4] += nn(context_one_ref[0], branch)
    close_sums(final, weight_sum, vector_sum, high_ref[0], outs)


def self_back_kernel(start_at, first, final, order_ref, target_ref, high_ref, *refs):
    given, refs = (None, refs) if first else (refs[:2], refs[2:])
    cross_lines_ref, expert_lines_ref = refs[:2]
    refs = refs[2:]
    (
        tokens_ref,
        grad_middle_ref,
        query_ref,
        key_ref,
        value_ref,
        context_ref,
        logsum_ref,
        columns_ref,
        self_query,
        self_key,
        self_value,
        self_out,
        grad_query_ref,
        grad_key_ref,
        grad_value_ref,
        first_ref,
        second_ref,
        weight_sum,
        vector_sum,
        key_t,
        grad_context,
        delta,
        grad_query_t,
    ) = refs
    step = pl.program_id(0)
    sequence = order_ref[lax.rem(start_at + step, order_ref.shape[0] - 1)]
    length = tokens_ref.shape[1]
    open_sums(first, weight_sum, vector_sum, given)

    valid = valid_rows_of(target_ref[sequence], length)
    context_grad = nt(grad_middle_ref[0].astype(BF16), self_out[...]).astype(BF16)
    grad_context[...] = context_grad
    delta[...] = head_sums(context_grad, context_ref[0])
    key_t[...] = key_ref[0].T
    attend_self_back(
        query_ref.at[0],
        key_ref.at[0],
        value_ref.at[0],
        key_t,
        grad_context,
        delta,
        logsum_ref.at[0],
        grad_query_t,
        grad_key_ref.at[0],
        grad_value_ref.at[0],
    )
    normed = normalise(tokens_ref[0].astype(F32) * valid)[0].astype(BF16)
    normed_t = normed.T
    weight_sum[0] += nn(grad_query_t[...], normed)
    weight_sum[1] += nn(normed_t, grad_key_ref[0])
    weight_sum[2] += nn(normed_t, grad_value_ref[0])
    grad_query = grad_query_t[...].T
    grad_query_ref[0] = grad_query
    for at, item in enumerate((grad_query, grad_key_ref[0], grad_value_ref[0])):
        vector_sum[at : at + 1, :] += column_sum(item)

    @pl.when(step == pl.num_programs(0) - 1)
    def _():
        if not final:
            first_ref[...] = weight_sum[...]
            second_ref[...] = vector_sum[...]
            return
        width = weight_sum.shape[1]
        gain, shift = columns_ref[:, 0:1], columns_ref[:, 1:2]
        gain_grad = jnp.zeros((width, 1), F32)
        shift_grad = jnp.zeros((width, 1), F32)
        squares = []
        for at, matrix in enumerate((self_query, self_key, self_value)):
            total = weight_sum[at].T if at == 0 else weight_sum[at]
            column = vector_sum[at : at + 1, :]
            weights = matrix[...].astype(F32)
            gain_grad += jnp.sum(weights * total, axis=1, keepdims=True)
            shift_grad += jnp.sum(weights * column, axis=1, keepdims=True)
            squares.append((total * gain + shift * column).astype(BF16))
        lane = lax.broadcasted_iota(jnp.int32, (width, 128), 1)
        both = jnp.where(lane == 0, gain_grad, jnp.where(lane == 1, shift_grad, 0.0)).T
        lines = jnp.concatenate(
            [
                vector_sum[0:1, :],
                vector_sum[2:3, :],
                both[0:2, :],
                jnp.zeros((4, width), F32),
                cross_lines_ref[...],
                expert_lines_ref[...],
            ],
            axis=0,
        )
        put_halves(squares, lines, high_ref[0], first_ref, second_ref)


def tokens_back_kernel(
    start_at,
    order_ref,
    target_ref,
    tokens_ref,
    grad_middle_ref,
    grad_query_ref,
    grad_key_ref,
    grad_value_ref,
    vectors_ref,
    self_query,
    self_key,
    self_value,
    tokens_grad_ref,
):
    sequence = order_ref[lax.rem(start_at + pl.program_id(0), order_ref.shape[0] - 1)]
    valid = valid_rows_of(target_ref[sequence], tokens_ref.shape[1])
    normed, inverse = normalise(tokens_ref[0].astype(F32) * valid)
    grad = (
        nt(grad_query_ref[0], self_query[...])
        + nt(grad_key_ref[0], self_key[...])
        + nt(grad_value_ref[0], self_value[...])
    )
    tokens_grad_ref[0] = (
        grad_middle_ref[0] + normalise_back(grad, normed, inverse, vectors_ref[0:1, :])
    ) * valid


def memory_back_kernel(order_ref, grad_key_ref, grad_value_ref, cross_key, cross_value, memory_grad_ref):
    memory_grad_ref[0] = nt(grad_key_ref[0], cross_key[...]) + nt(
        grad_value_ref[0], cross_value[...]
    )


def apart(at, count, turn):
    return at ^ turn if count & (count - 1) == 0 else lax.rem(at + turn, count)


def heard(at, count, turn):
    return at ^ turn if count & (count - 1) == 0 else lax.rem(at + count - turn, count)


def fold_kernel(items, lines, shared, count, at_ref, *refs):
    parts, outs = refs[:items], refs[items:]
    total = parts[0][...].astype(F32)
    for part in parts[1:]:
        total = total + part[...].astype(F32)
    height = total.shape[0] - lines
    if count == 1:
        outs[0][...] = total[:height].astype(BF16)
        if lines:
            outs[1][...] = total[height:]
        return
    share, at = height // count, at_ref[0]
    stack = refs[-1]
    stack[...] = total[:height].astype(BF16)
    for turn in range(count):
        which = pl.multiple_of(apart(at, count, turn) * share, 16)
        outs[turn][:share] = stack[pl.ds(which, share), :]
        if shared:
            outs[turn][share:] = total[height : height + shared].astype(BF16)
    if lines > shared:
        outs[count][...] = total[height + shared :]


def spread_kernel(count, at_ref, *refs):
    parts, out = refs[:count], refs[count]
    share = parts[0].shape[0]
    for turn in range(count):
        place = pl.multiple_of(heard(at_ref[0], count, turn) * share, 16)
        out[pl.ds(place, share), :] = parts[turn][...]


def finish_kernel(high_ref, own_ref, got_ref, *outs):
    own, got = own_ref[...].astype(F32), got_ref[...].astype(F32)
    top = high_ref[0] > 0
    whole = [jnp.where(top, got, own), jnp.where(top, own, got)]
    height, half = outs[0].shape[0], own.shape[0]
    for at, out in enumerate(outs):
        start, stop = at * height, (at + 1) * height
        for part in (0, 1):
            low, top_row = max(start, part * half), min(stop, (part + 1) * half)
            if low < top_row:
                out[low - start : top_row - start] = whole[part][low - part * half : top_row - part * half]


def cast_kernel(*refs):
    count = len(refs) // 2
    for source, out in zip(refs[:count], refs[count:]):
        out[...] = source[...].astype(F32)


def fixed(shape):
    return pl.BlockSpec(shape, lambda *_: (0,) * len(shape))


def once(shape):
    return pl.BlockSpec(shape, lambda *_: (0,) * len(shape), pipeline_mode=pl.Buffered(1))


def at_position(shape, start, count):
    return pl.BlockSpec(
        (1,) + shape, lambda step, *_: (lax.rem(start + step, count),) + (0,) * len(shape)
    )


def at_sequence(shape, start, count):
    return pl.BlockSpec(
        (1,) + shape,
        lambda step, order, *_: (order[lax.rem(start + step, count)],) + (0,) * len(shape),
    )


def struct(shape, kind):
    return jax.ShapeDtypeStruct(shape, kind)


def launch(
    kernel,
    name,
    grid,
    scalars,
    inputs,
    in_specs,
    outs,
    out_specs,
    scratch=(),
    micros=10,
    after=(),
    into=None,
    carry=(),
):
    into = into or {}
    extra = list(after) + list(into.values()) + list(carry)
    lead, made = len(scalars) + len(inputs), len(outs)
    anywhere = pl.BlockSpec(memory_space=pl.ANY)

    def body(*refs):
        rest = refs[lead + len(extra) :]
        kernel(*refs[:lead], *rest[:made], *rest[made + len(carry) :])

    aliases = {lead + len(after) + at: out for at, out in enumerate(into)}
    first = lead + len(after) + len(into)
    aliases.update({first + at: made + at for at in range(len(carry))})
    return pl.pallas_call(
        body,
        grid_spec=pltpu.PrefetchScalarGridSpec(
            num_scalar_prefetch=len(scalars),
            grid=grid,
            in_specs=list(in_specs) + [anywhere] * len(extra),
            out_specs=list(out_specs) + [anywhere] * len(carry),
            scratch_shapes=list(scratch),
        ),
        out_shape=[struct(shape, kind) for shape, kind in outs]
        + [struct(item.shape, item.dtype) for item in carry],
        input_output_aliases=aliases,
        compiler_params=pltpu.CompilerParams(
            dimension_semantics=("arbitrary",) * len(grid), vmem_limit_bytes=VMEM_LIMIT
        ),
        cost_estimate=pl.CostEstimate(
            flops=int(micros * 1.0e9), bytes_accessed=int(micros * 2.0e6), transcendentals=0
        ),
        name=name,
    )(*scalars, *inputs, *extra)


def exchange(rows, way, turn):
    axis, stride, count = way
    route = []
    for place in range(lax.axis_size(axis)):
        at = (place // stride) % count
        other = at ^ turn if count & (count - 1) == 0 else (at + turn) % count
        route.append((place, place + (other - at) * stride))
    return lax.ppermute(rows, axis, route)


def coordinate(way):
    axis, stride, count = way
    return ((lax.axis_index(axis) // stride) % count).astype(jnp.int32)


def fold(parts, lines, way, shared=0, after=()):
    count = 1 if way is None else way[2]
    height, width = parts[0].shape[0] - lines, parts[0].shape[1]
    share = height // count
    outs = [((share + shared, width), BF16)] * count
    if way is None:
        outs += [((lines, width), F32)] if lines else []
    elif lines > shared:
        outs += [((lines - shared, width), F32)]
    if share % 16 == 0:
        at = coordinate(way).reshape(1) if way else jnp.zeros((1,), jnp.int32)
        return launch(
            functools.partial(fold_kernel, len(parts), lines, shared, count),
            "fold",
            (1,),
            (at,),
            tuple(parts),
            [fixed(parts[0].shape)] * len(parts),
            outs,
            [fixed(shape) for shape, _ in outs],
            [pltpu.VMEM((height, width), BF16)] if count > 1 else [],
            micros=2,
            after=after,
        )
    total = sum(part.astype(F32) for part in parts)
    if way is None:
        return [total[:height].astype(BF16)] + ([total[height:]] if lines else [])
    at = coordinate(way)
    results = [
        jnp.concatenate(
            [
                lax.dynamic_slice_in_dim(total, apart(at, count, turn) * share, share, 0),
                total[height : height + shared],
            ],
            axis=0,
        ).astype(BF16)
        for turn in range(count)
    ]
    return results + ([total[height + shared :]] if lines > shared else [])


def swap(gives, way):
    return [gives[0]] + [exchange(gives[turn], way, turn) for turn in range(1, way[2])]


def fetch(own, way):
    return [own] + [exchange(own, way, turn) for turn in range(1, way[2])]


def spread(parts, way, after=()):
    own, count = parts[0], way[2]
    share, width = own.shape
    at = coordinate(way)
    if share % 16 == 0:
        (whole,) = launch(
            functools.partial(spread_kernel, count),
            "spread",
            (1,),
            (at.reshape(1),),
            tuple(parts),
            [fixed(own.shape)] * count,
            [((share * count, width), BF16)],
            [fixed((share * count, width))],
            micros=2,
            after=after,
        )
        return whole
    stack = jnp.stack(parts)
    turns = [at ^ place if count & (count - 1) == 0 else (at - place) % count for place in range(count)]
    return jnp.concatenate(
        [lax.dynamic_index_in_dim(stack, turn, 0, False) for turn in turns], axis=0
    )


def finish(own, got, width, squares, after):
    high = (lax.axis_index("dp") % 2).astype(jnp.int32).reshape(1)
    return launch(
        finish_kernel,
        "finish",
        (1,),
        (high,),
        (own, got),
        [fixed(own.shape)] * 2,
        [((width, width), F32)] * squares,
        [fixed((width, width))] * squares,
        micros=2,
        after=after,
    )


def on_device(
    tokens,
    memory,
    cotangent,
    target_length,
    memory_length,
    expert_of,
    self_norm_gain,
    self_norm_bias,
    self_query,
    self_key,
    self_value,
    self_out,
    self_query_bias,
    self_value_bias,
    self_out_bias,
    cross_norm_gain,
    cross_norm_bias,
    cross_query,
    cross_key,
    cross_value,
    cross_out,
    cross_attention_query_bias,
    cross_value_bias,
    cross_out_bias,
    expert_norm_gain,
    expert_norm_bias,
    expert_in,
    expert_in_bias,
    expert_out,
    expert_out_bias,
):
    seqs, length, width = tokens.shape
    mem_rows = memory.shape[1]
    local_count, _, hidden_width = expert_in.shape
    groups = lax.axis_size("expert")
    places = lax.axis_size("dp")
    own_group = lax.axis_index("expert")
    column = lax.axis_index("dp")

    shifts = list(range(1, groups)) + [0]
    whole = groups == seqs
    rows_shape, square = (length, width), (width, width)
    mem_shape, heads_shape = (mem_rows, width), (HEADS, length)
    turned = (width, length)
    in_smem = pl.BlockSpec(memory_space=pltpu.SMEM)
    order, picks, used, slot_of, spot_of, *grads = pl.pallas_call(
        functools.partial(plan_kernel, shifts, local_count),
        in_specs=[in_smem] * 3 + [pl.BlockSpec(memory_space=pltpu.VMEM)],
        out_specs=[in_smem] * 5 + [pl.BlockSpec(memory_space=pltpu.VMEM)] * groups,
        out_shape=[
            struct((seqs + 1,), jnp.int32),
            struct((groups,), jnp.int32),
            struct((groups,), jnp.int32),
            struct((seqs,), jnp.int32),
            struct((groups,), jnp.int32),
        ]
        + [struct(rows_shape, BF16)] * groups,
        compiler_params=pltpu.CompilerParams(vmem_limit_bytes=VMEM_LIMIT),
        name="plan",
    )(
        jnp.stack([own_group, column, jnp.int32(places)]).astype(jnp.int32),
        expert_of,
        target_length,
        cotangent,
    )

    def move(rows, slot, back=False):
        shift = shifts[slot]
        if shift == 0:
            return rows
        turn = -shift if back else shift
        return lax.ppermute(rows, "expert", [(g, (g + turn) % groups) for g in range(groups)])

    def arranged(per_slot):
        if whole:
            return per_slot
        stack = jnp.stack(per_slot)
        return [lax.dynamic_index_in_dim(stack, slot_of[at], 0, False) for at in range(seqs)]

    position = lambda shape, start=0: at_position(shape, start, seqs)
    sequence = lambda shape, start=0: at_sequence(shape, start, seqs)
    vectors = jnp.stack(
        [
            self_norm_gain,
            self_norm_bias,
            self_query_bias,
            self_value_bias,
            self_out_bias,
            cross_norm_gain,
            cross_norm_bias,
            cross_attention_query_bias,
            cross_value_bias,
            cross_out_bias,
            expert_norm_gain,
            expert_norm_bias,
        ]
        + [jnp.zeros_like(self_norm_gain)] * 4
    )
    self_matrices = (self_query, self_key, self_value, self_out)
    cross_matrices = (cross_query, cross_key, cross_value, cross_out)
    half = seqs // 2
    high = (column % 2).astype(jnp.int32).reshape(1)
    grads_in = [move(grads[slot], slot) for slot in range(groups)]

    saved = [
        (rows_shape, F32),
        (rows_shape, F32),
        (rows_shape, BF16),
        (rows_shape, BF16),
        (rows_shape, BF16),
        (turned, BF16),
        (heads_shape, F32),
        (rows_shape, BF16),
        (mem_shape, BF16),
        (mem_shape, BF16),
        (turned, BF16),
        (heads_shape, F32),
    ]

    def forward(start, steps, kept, after):
        results = launch(
            functools.partial(forward_kernel, start, steps),
            "forward",
            (steps,),
            (order, target_length, memory_length),
            (tokens, memory, vectors) + self_matrices + cross_matrices,
            [sequence(rows_shape, start), sequence(mem_shape, start), fixed(vectors.shape)]
            + [fixed(square)] * 8,
            [(rows_shape, BF16)] * steps + [((seqs,) + shape, kind) for shape, kind in saved],
            [fixed(rows_shape)] * steps + [position(shape, start) for shape, _ in saved],
            [pltpu.VMEM(turned, BF16)],
            micros=12 * steps,
            after=after,
            into={at + steps: item for at, item in enumerate(kept)},
        )
        return results[:steps], results[steps:]

    normed_one, kept = forward(0, half, [], [])
    normed_two, kept = forward(half, seqs - half, kept, [grads_in[0]])
    normed = list(normed_one) + list(normed_two)
    (
        later,
        middle,
        query_one,
        key_one,
        value_one,
        context_one,
        logsum_one,
        query_two,
        key_two,
        value_two,
        context_two,
        logsum_two,
    ) = kept

    if whole:
        rows_in = [move(normed[slot], slot) for slot in range(groups)]
    else:
        joined = jnp.stack(normed)
        rows_in = [
            move(lax.dynamic_index_in_dim(joined, spot_of[slot], 0, False), slot)
            for slot in range(groups)
        ]
    tiles = 4
    tile_width = hidden_width // tiles
    hidden_tile = pl.BlockSpec((length, tile_width), lambda t, *_: (0, t))
    line_tile = pl.BlockSpec((1, tile_width), lambda t, *_: (0, t))
    hidden, grad_pre, made, grad_rows, pre_sum, grads_sum = {}, {}, {}, {}, {}, {}

    def expert(slot, after):
        results = launch(
            functools.partial(expert_kernel, slot),
            "expert",
            (tiles,),
            (picks, used),
            (rows_in[slot], grads_in[slot], expert_in, expert_in_bias, expert_out, expert_out_bias),
            [
                fixed(rows_shape),
                fixed(rows_shape),
                pl.BlockSpec((1, width, tile_width), lambda t, pick, _: (pick[slot], 0, t)),
                pl.BlockSpec((local_count, tile_width), lambda t, *_: (0, t)),
                pl.BlockSpec((1, tile_width, width), lambda t, pick, _: (pick[slot], t, 0)),
                fixed((local_count, width)),
            ],
            [((length, hidden_width), BF16)] * 2
            + [(rows_shape, BF16)] * 2
            + [((1, hidden_width), F32), ((1, width), F32)],
            [hidden_tile, hidden_tile, fixed(rows_shape), fixed(rows_shape), line_tile]
            + [fixed((1, width))],
            [pltpu.VMEM(rows_shape, F32)] * 2,
            micros=1,
            after=after,
        )
        for table, result in zip((hidden, grad_pre, made, grad_rows, pre_sum, grads_sum), results):
            table[slot] = result

    back_scratch = [
        pltpu.VMEM((width, mem_rows), BF16),
        pltpu.VMEM(rows_shape, BF16),
        pltpu.VMEM(heads_shape, F32),
        pltpu.VMEM(turned, BF16),
    ]

    def sums_shape(count, final, lines=0):
        if final:
            return [((count * width // 2 + lines, width), BF16)] * 2
        return [((count,) + square, F32)]

    def cross_back(start, steps, grads, given, filled, final, after, carry=()):
        first = given is None
        total = sums_shape(5, final)
        return launch(
            functools.partial(cross_back_kernel, start, first, final, steps),
            "cross_back",
            (steps,),
            (order, target_length, memory_length, high),
            tuple(grads)
            + (() if first else tuple(given))
            + (cotangent, memory, later, middle, query_two, key_two, value_two, context_two)
            + (logsum_two, context_one, vectors)
            + cross_matrices,
            [once(rows_shape)] * steps
            + ([] if first else [once((5,) + square), once((8, width))])
            + [
                sequence(rows_shape, start),
                sequence(mem_shape, start),
                position(rows_shape, start),
                position(rows_shape, start),
                position(rows_shape, start),
                position(mem_shape, start),
                position(mem_shape, start),
                position(turned, start),
                position(heads_shape, start),
                position(turned, start),
                fixed(vectors.shape),
            ]
            + [once(square)] * 4,
            [((seqs,) + rows_shape, F32)]
            + [((seqs,) + mem_shape, BF16)] * 2
            + total
            + [((8, width), F32)],
            [position(rows_shape, start), position(mem_shape, start), position(mem_shape, start)]
            + [fixed(shape) for shape, _ in total]
            + [fixed((8, width))],
            [pltpu.VMEM((5,) + square, F32), pltpu.VMEM((8, width), F32), pltpu.VMEM(rows_shape, BF16)]
            + back_scratch,
            micros=13 * steps,
            after=after,
            into={at: item for at, item in enumerate(filled)},
            carry=carry,
        )

    def self_back(start, steps, given, filled, final, after):
        first = given is None
        total = sums_shape(3, final, LINES) if final else sums_shape(3, final) + [((8, width), F32)]
        return launch(
            functools.partial(self_back_kernel, start, first, final),
            "self_back",
            (steps,),
            (order, target_length, high),
            (() if first else tuple(given))
            + (cross_lines, expert_lines)
            + (tokens, grad_middle, query_one, key_one, value_one, context_one, logsum_one, columns)
            + self_matrices,
            ([] if first else [once((3,) + square), once((8, width))])
            + [fixed((8, width)), fixed((EXPERT_LINES, width))]
            + [
                sequence(rows_shape, start),
                position(rows_shape, start),
                position(rows_shape, start),
                position(rows_shape, start),
                position(rows_shape, start),
                position(turned, start),
                position(heads_shape, start),
                fixed(columns.shape),
            ]
            + [once(square)] * 4,
            [((seqs,) + rows_shape, BF16)] * 3 + total,
            [position(rows_shape, start)] * 3 + [fixed(shape) for shape, _ in total],
            [pltpu.VMEM((3,) + square, F32), pltpu.VMEM((8, width), F32)] + back_scratch,
            micros=10 * steps,
            after=after,
            into={at: item for at, item in enumerate(filled)},
        )

    back = {}

    def send_back(slot):
        back[slot] = move(grad_rows[slot], slot, True)

    if whole:
        expert(3, [])
        expert(0, [made[3]])
        expert(1, [made[0]])
        expert(2, [made[1]])
        for slot in range(groups):
            send_back(slot)
    else:
        for slot in range(groups):
            expert(slot, [])
            send_back(slot)

    in_sums, out_sums, expert_lines = launch(
        functools.partial(expert_weights_kernel, groups),
        "expert_weights",
        (tiles,),
        (picks, used),
        tuple(rows_in)
        + tuple(grads_in)
        + tuple(table[slot] for table in (hidden, grad_pre, pre_sum, grads_sum) for slot in range(groups)),
        [once(rows_shape)] * (2 * groups)
        + [hidden_tile] * (2 * groups)
        + [line_tile] * groups
        + [fixed((1, width))] * groups,
        [
            ((local_count, width, hidden_width), BF16),
            ((local_count, hidden_width, width), BF16),
            ((EXPERT_LINES, width), F32),
        ],
        [
            pl.BlockSpec((local_count, width, tile_width), lambda t, *_: (0, 0, t)),
            pl.BlockSpec((local_count, tile_width, width), lambda t, *_: (0, t, 0)),
            fixed((EXPERT_LINES, width)),
        ],
        [
            pltpu.VMEM((local_count, width, tile_width), F32),
            pltpu.VMEM((local_count, tile_width, width), F32),
            pltpu.VMEM((local_count, 1, tile_width), F32),
            pltpu.VMEM((local_count, 1, width), F32),
        ],
        micros=17,
        after=[back[0]] if whole else [],
    )
    expert_in_grad = lax.psum_scatter(in_sums, "dp", scatter_dimension=1, tiled=True)
    expert_out_grad = lax.psum_scatter(out_sums, "dp", scatter_dimension=1, tiled=True)

    if whole:
        away = [slot for slot in range(groups) if shifts[slot]]
        results = cross_back(
            3, 2, [back[3], back[0]], None, [], False, [in_sums], [made[slot] for slot in away]
        )
        filled, (weights_run, vectors_run) = results[:3], results[3:5]
        for at, slot in enumerate(away):
            made[slot] = results[5 + at]
        made_home = [move(made[slot], slot, True) for slot in range(groups)]
        *results, cross_keep, cross_give, cross_lines = cross_back(
            1, 2, [back[1], back[2]], (weights_run, vectors_run), filled, True, []
        )
    else:
        *results, cross_keep, cross_give, cross_lines = cross_back(
            0, seqs, arranged([back[slot] for slot in range(groups)]), None, [], True, []
        )
        made_home = arranged([move(made[slot], slot, True) for slot in range(groups)])
    grad_middle, grad_key_two, grad_value_two = results

    chips = places // 2
    core, plane, line = ("dp", 1, 2), ("dp", 2, chips), ("expert", 1, groups)
    columns = jnp.concatenate([vectors.T, jnp.zeros((width, 128 - vectors.shape[0]), F32)], axis=1)

    cross_got = exchange(cross_give, core, 1)
    *filled, weights_run, vectors_run = self_back(0, half, None, [], False, made_home[:2])
    cross_parts = swap(fold([cross_keep, cross_got], 0, plane, after=filled[:1]), plane)
    *results, self_keep, self_give = self_back(
        half, seqs - half, (weights_run, vectors_run), filled, True, cross_parts[:1] + made_home[2:3]
    )
    grad_query_one, grad_key_one, grad_value_one = results

    def tokens_back(start, steps, filled, after):
        return launch(
            functools.partial(tokens_back_kernel, start),
            "tokens_back",
            (steps,),
            (order, target_length),
            (tokens, grad_middle, grad_query_one, grad_key_one, grad_value_one, vectors)
            + self_matrices[:3],
            [sequence(rows_shape, start)]
            + [position(rows_shape, start)] * 4
            + [fixed(vectors.shape)]
            + [once(square)] * 3,
            [((seqs,) + rows_shape, F32)],
            [sequence(rows_shape, start)],
            micros=4 * steps,
            after=after,
            into={at: item for at, item in enumerate(filled)},
        )

    self_got = exchange(self_give, core, 1)
    cross_line = swap(fold(cross_parts, 0, line, after=[self_give]), line)
    filled = tokens_back(0, half, [], cross_line[:1])

    self_parts = swap(fold([self_keep, self_got], LINES, plane, LINES, after=filled), plane)
    cross_share = fold(cross_line, 0, None, after=filled)[0]
    cross_got = fetch(cross_share, line)
    (tokens_grad,) = tokens_back(half, seqs - half, filled, [cross_share, self_parts[0]])

    *self_gives, own_lines = fold(self_parts, LINES, line, SHARED_LINES, after=[tokens_grad])
    self_line = swap(self_gives, line)
    cross_plane = spread(cross_got, line, after=[tokens_grad])
    cross_got = fetch(cross_plane, plane)
    (memory_grad,) = launch(
        memory_back_kernel,
        "memory_back",
        (seqs,),
        (order,),
        (grad_key_two, grad_value_two, cross_key, cross_value),
        [position(mem_shape)] * 2 + [once(square)] * 2,
        [((seqs,) + mem_shape, F32)],
        [sequence(mem_shape)],
        micros=5,
        after=[self_line[0], cross_plane],
    )

    self_share, totals = fold(self_line, SHARED_LINES, None, after=[memory_grad])
    self_got = fetch(self_share, line)
    cross_half = spread(cross_got, plane, after=[memory_grad])
    cross_got = exchange(cross_half, core, 1)
    (output,) = launch(
        functools.partial(output_kernel, seqs),
        "output",
        (seqs,),
        (order, target_length),
        (later, *made_home),
        [position(rows_shape)] + [once(rows_shape)] * seqs,
        [((seqs,) + rows_shape, BF16)],
        [sequence(rows_shape)],
        micros=5,
        after=[self_share, cross_half],
    )

    self_plane = spread(self_got, line, after=[output])
    self_got = fetch(self_plane, plane)
    cross_q, cross_k, cross_v, cross_o, self_o = finish(cross_half, cross_got, width, 5, [self_plane])
    shares = (expert_in_grad, expert_out_grad)
    expert_in_grad, expert_out_grad = launch(
        cast_kernel,
        "cast",
        (1,),
        (),
        shares,
        [fixed(item.shape) for item in shares],
        [(item.shape, F32) for item in shares],
        [fixed(item.shape) for item in shares],
        micros=3,
        after=[self_plane],
    )
    self_half = spread(self_got, plane, after=[cross_q, expert_in_grad])
    self_q, self_k, self_v = finish(self_half, exchange(self_half, core, 1), width, 3, [])

    in_count = local_count * hidden_width // width
    in_bias = own_lines[:in_count].reshape(local_count, hidden_width)
    out_bias = own_lines[in_count : in_count + local_count]
    in_share, out_share = hidden_width // places, width // places
    return (
        output,
        tokens_grad,
        memory_grad,
        totals[2],
        totals[3],
        self_q,
        self_k,
        self_v,
        self_o,
        totals[0],
        totals[1],
        totals[15],
        totals[13],
        totals[14],
        cross_q,
        cross_k,
        cross_v,
        cross_o,
        totals[12],
        totals[11],
        totals[10],
        totals[8],
        totals[9],
        expert_in_grad,
        lax.dynamic_slice_in_dim(in_bias, column * in_share, in_share, 1),
        expert_out_grad,
        lax.dynamic_slice_in_dim(out_bias, column * out_share, out_share, 1),
    )


def solution(mesh):
    rows = P(("expert", "dp"), None, None)
    counts = P(("expert", "dp"))
    split = (P("expert", None, None), P("expert", None)) * 2
    shares = (P("expert", "dp", None), P("expert", "dp")) * 2
    return jax.shard_map(
        on_device,
        mesh=mesh,
        in_specs=(rows,) * 3 + (counts,) * 2 + (P(),) * 21 + split,
        out_specs=(rows,) * 3 + (P(),) * 20 + shares,
        check_vma=False,
    )
```

```python
import functools

import jax
import jax.numpy as jnp
from jax import lax
from jax.experimental import pallas as pl
from jax.experimental.pallas import tpu as pltpu
from jax.sharding import PartitionSpec as P

HEADS = 8
HEAD_DIM = 64
PAIR = 2 * HEAD_DIM
EPSILON = 1e-05
SCORE_SCALE = 0.125
NEGATIVE = -1e30
SAFE_SCORE = 80.0
SHARED_LINES = 16
EXPERT_LINES = 16
LINES = SHARED_LINES + EXPERT_LINES
LOG2E = 1.4426950408889634
LN2 = 0.6931471805599453
VMEM_LIMIT = 64 * 1024 * 1024
F32 = jnp.float32
BF16 = jnp.bfloat16


def contract(left, right, left_dim, right_dim):
    return lax.dot_general(
        left, right, (((left_dim,), (right_dim,)), ((), ())), preferred_element_type=F32
    )


def nn(left, right):
    return contract(left, right, 1, 0)


def nt(left, right):
    return contract(left, right, 1, 1)


def tn(left, right):
    return contract(left, right, 0, 0)


def normalise(rows):
    centre = rows - jnp.mean(rows, axis=-1, keepdims=True)
    inverse = lax.rsqrt(jnp.mean(centre * centre, axis=-1, keepdims=True) + EPSILON)
    return centre * inverse, inverse


def normalise_back(grad, normed, inverse, gain):
    scaled = grad * gain
    return inverse * (
        scaled
        - jnp.mean(scaled, axis=-1, keepdims=True)
        - normed * jnp.mean(scaled * normed, axis=-1, keepdims=True)
    )


def column_sum(rows):
    return jnp.sum(rows.astype(F32), axis=0, keepdims=True)


def head_masks():
    lane = lax.broadcasted_iota(jnp.int32, (1, PAIR), 1)
    mine = [(lane // HEAD_DIM == half).astype(F32).astype(BF16) for half in (0, 1)]
    spare = [(lane == HEAD_DIM * (1 - half)).astype(F32).astype(BF16) for half in (0, 1)]
    return mine, spare


def key_bias(count, mem_rows):
    place = lax.broadcasted_iota(jnp.int32, (mem_rows, PAIR), 0)
    return jnp.where(place < count, 0.0, NEGATIVE).astype(BF16)


def score_operands(keys, queries, half, mine, spare, bias):
    picked = queries * mine[half]
    if bias is None:
        return keys, picked
    return keys * (1 - spare[half]) + bias * spare[half], picked + spare[half]


def causal(scores, block):
    key_at = lax.broadcasted_iota(jnp.int32, (scores.shape[0], block), 0)
    query_at = lax.broadcasted_iota(jnp.int32, (scores.shape[0], block), 1)
    return jnp.where(key_at <= query_at, scores, NEGATIVE)


def lower(items, block):
    return jnp.concatenate([item[block:] for item in items], axis=0)


def lower_columns(items, block):
    return jnp.concatenate([item[:, block:] for item in items], axis=1)


def span(start, size):
    return slice(start, start + size) if isinstance(start, int) else pl.ds(pl.multiple_of(start, size), size)


def head_rows(pair, half):
    return span(pair * PAIR + half * HEAD_DIM, HEAD_DIM)


def pair_span(pair):
    return span(pair * PAIR, PAIR)


def each_pair(pair_step, unrolled):
    if unrolled:
        for pair in range(HEADS // 2):
            pair_step(pair, 0)
    else:
        lax.fori_loop(0, HEADS // 2, pair_step, 0)


def head_part(both, half, block):
    return both[half * HEAD_DIM : (half + 1) * HEAD_DIM, half * block : (half + 1) * block]


def causal_pair_scores(keys, picked, block):
    upper = []
    for half in (0, 1):
        scores = nt(keys[:block], picked[half])
        upper.append(
            jnp.concatenate([causal(scores[:, :block], block), scores[:, block:]], axis=1)
        )
    scores = nt(keys[block:], lower(picked, block))
    low = jnp.concatenate([causal(scores[:, :block], block), causal(scores[:, block:], block)], axis=1)
    return upper, low


def head_blocks():
    feature = lax.broadcasted_iota(jnp.int32, (HEADS * HEAD_DIM, 128), 0)
    return (feature // HEAD_DIM == lax.broadcasted_iota(jnp.int32, (HEADS * HEAD_DIM, 128), 1)).astype(BF16)


def scores_small(query_ref, key_ref):
    blocks = head_blocks()
    squares = [nn(ref[...] * ref[...], blocks) for ref in (query_ref, key_ref)]
    most = [jnp.max(item, axis=0, keepdims=True) for item in squares]
    return jnp.max(most[0] * most[1]) < SAFE_SCORE * SAFE_SCORE


def attend_cross(plain, query_ref, key_ref, value_t_ref, context_t_ref, logsum_ref, bias):
    mine, spare = head_masks()

    def pair_step(pair, carry):
        columns = pair_span(pair)
        keys, queries = key_ref[:, columns], query_ref[:, columns]
        for half in (0, 1):
            rows = head_rows(pair, half)
            left, right = score_operands(keys, queries, half, mine, spare, bias)
            scores = nt(left, right)
            highest = 0.0 if plain else jnp.max(scores, axis=0, keepdims=True)
            raised = jnp.exp2(scores if plain else scores - highest)
            summed = jnp.sum(raised, axis=0, keepdims=True)
            context = nn(value_t_ref[rows, :], raised.astype(BF16))
            context_t_ref[rows, :] = (context * (1.0 / summed)).astype(BF16)
            logsum_ref[pl.ds(2 * pair + half, 1), :] = highest + LOG2E * jnp.log(summed)
        return carry

    each_pair(pair_step, plain)


def attend_self(plain, query_ref, key_ref, value_t_ref, context_t_ref, logsum_ref):
    block = query_ref.shape[0] // 2
    mine, _ = head_masks()

    def pair_step(pair, carry):
        columns = pair_span(pair)
        keys, queries = key_ref[:, columns], query_ref[:, columns]
        upper, low = causal_pair_scores(keys, [queries * mine[0], queries * mine[1]], block)
        if plain:
            highest = [0.0, 0.0]
            low = jnp.exp2(low)
        else:
            low_top = jnp.max(low, axis=0, keepdims=True)
            highest = []
            for half in (0, 1):
                top = jnp.max(upper[half], axis=0, keepdims=True)
                other = low_top[:, half * block : (half + 1) * block]
                highest.append(
                    jnp.concatenate([top[:, :block], jnp.maximum(top[:, block:], other)], axis=1)
                )
            low = jnp.exp2(low - lower_columns(highest, block))
        low_sum = jnp.sum(low, axis=0, keepdims=True)
        low_context = nn(value_t_ref[columns, block:], low.astype(BF16))
        for half in (0, 1):
            rows = head_rows(pair, half)
            raised = jnp.exp2(upper[half] if plain else upper[half] - highest[half])
            summed = jnp.sum(raised, axis=0, keepdims=True)
            part = low_sum[:, half * block : (half + 1) * block]
            summed = jnp.concatenate([summed[:, :block], summed[:, block:] + part], axis=1)
            context = nn(value_t_ref[rows, :block], raised.astype(BF16))
            context = jnp.concatenate(
                [context[:, :block], context[:, block:] + head_part(low_context, half, block)],
                axis=1,
            )
            context_t_ref[rows, :] = (context * (1.0 / summed)).astype(BF16)
            logsum_ref[pl.ds(2 * pair + half, 1), :] = highest[half] + LOG2E * jnp.log(summed)
        return carry

    each_pair(pair_step, plain)


def attend(kind, query_ref, key_ref, *refs):
    small = scores_small(query_ref, key_ref)

    @pl.when(small)
    def _():
        kind(True, query_ref, key_ref, *refs)

    @pl.when(jnp.logical_not(small))
    def _():
        kind(False, query_ref, key_ref, *refs)


def attend_cross_back(
    query_ref,
    key_ref,
    value_ref,
    key_t_ref,
    grad_ref,
    delta_ref,
    logsum_ref,
    grad_query_t_ref,
    grad_key_ref,
    grad_value_ref,
    bias,
):
    mine, spare = head_masks()

    def pair_step(pair, carry):
        columns = pair_span(pair)
        keys, queries, values = key_ref[:, columns], query_ref[:, columns], value_ref[:, columns]
        grads = grad_ref[:, columns]
        chances, slopes, picked_grads, picked_queries = [], [], [], []
        for half in (0, 1):
            head, rows = pl.ds(2 * pair + half, 1), head_rows(pair, half)
            left, right = score_operands(keys, queries, half, mine, spare, bias)
            picked_grads.append(grads * mine[half])
            picked_queries.append(queries * mine[half])
            chance = jnp.exp2(nt(left, right) - logsum_ref[head, :])
            slope = chance * (nt(values, picked_grads[half]) - delta_ref[head, :])
            chances.append(chance.astype(BF16))
            slopes.append(slope.astype(BF16))
            grad_query_t_ref[rows, :] = (nn(key_t_ref[rows, :], slopes[half]) * SCORE_SCALE).astype(
                BF16
            )
        grad_value_ref[:, columns] = nn(
            jnp.concatenate(chances, axis=1), jnp.concatenate(picked_grads, axis=0)
        ).astype(BF16)
        grad_key_ref[:, columns] = (
            nn(jnp.concatenate(slopes, axis=1), jnp.concatenate(picked_queries, axis=0)) * LN2
        ).astype(BF16)
        return carry

    each_pair(pair_step, True)


def attend_self_back(
    query_ref,
    key_ref,
    value_ref,
    key_t_ref,
    grad_ref,
    delta_ref,
    logsum_ref,
    grad_query_t_ref,
    grad_key_ref,
    grad_value_ref,
):
    block = query_ref.shape[0] // 2
    mine, _ = head_masks()

    def pair_step(pair, carry):
        columns = pair_span(pair)
        keys, queries, values = key_ref[:, columns], query_ref[:, columns], value_ref[:, columns]
        grads = grad_ref[:, columns]
        picked = [queries * mine[0], queries * mine[1]]
        picked_grads = [grads * mine[0], grads * mine[1]]
        upper, low = causal_pair_scores(keys, picked, block)
        logsum = [logsum_ref[pl.ds(2 * pair + half, 1), :] for half in (0, 1)]
        delta = [delta_ref[pl.ds(2 * pair + half, 1), :] for half in (0, 1)]
        low_grads = lower(picked_grads, block)
        low = jnp.exp2(low - lower_columns(logsum, block))
        low_slope = (
            low * (nt(values[block:], low_grads) - lower_columns(delta, block))
        ).astype(BF16)
        low_query = nn(key_t_ref[columns, block:], low_slope)
        chances, slopes = [], []
        for half in (0, 1):
            chance = jnp.exp2(upper[half] - logsum[half])
            slope = chance * (nt(values[:block], picked_grads[half]) - delta[half])
            chances.append(chance.astype(BF16))
            slopes.append(slope.astype(BF16))
            rows = head_rows(pair, half)
            grad = nn(key_t_ref[rows, :block], slopes[half])
            grad = jnp.concatenate(
                [grad[:, :block], grad[:, block:] + head_part(low_query, half, block)], axis=1
            )
            grad_query_t_ref[rows, :] = (grad * SCORE_SCALE).astype(BF16)
        grad_value_ref[:block, columns] = nn(
            jnp.concatenate(chances, axis=1), jnp.concatenate(picked_grads, axis=0)
        ).astype(BF16)
        grad_value_ref[block:, columns] = nn(low.astype(BF16), low_grads).astype(BF16)
        grad_key_ref[:block, columns] = (
            nn(jnp.concatenate(slopes, axis=1), jnp.concatenate(picked, axis=0)) * LN2
        ).astype(BF16)
        grad_key_ref[block:, columns] = (nn(low_slope, lower(picked, block)) * LN2).astype(BF16)
        return carry

    each_pair(pair_step, True)


def head_sums(grad, context_t):
    product = grad.T.astype(F32) * context_t.astype(F32)
    return jnp.sum(product.reshape(HEADS, HEAD_DIM, product.shape[1]), axis=1)


def valid_rows_of(count, length):
    return (lax.broadcasted_iota(jnp.int32, (length, 1), 0) < count).astype(F32)


def forward_kernel(
    start_at,
    steps,
    order_ref,
    target_ref,
    memory_length_ref,
    tokens_ref,
    memory_ref,
    vectors_ref,
    self_query,
    self_key,
    self_value,
    self_out,
    cross_query,
    cross_key,
    cross_value,
    cross_out,
    *refs,
):
    normed_refs, refs = refs[:steps], refs[steps:]
    (
    later_ref,
    middle_ref,
    query_one_ref,
    key_one_ref,
    value_one_ref,
    context_one_ref,
    logsum_one_ref,
    query_two_ref,
    key_two_ref,
    value_two_ref,
    context_two_ref,
    logsum_two_ref,
    value_t_ref,
    ) = refs
    step = pl.program_id(0)
    sequence = order_ref[start_at + step]
    length = tokens_ref.shape[1]
    vector = lambda at: vectors_ref[at : at + 1, :]
    start = tokens_ref[0].astype(F32) * valid_rows_of(target_ref[sequence], length)
    normed = (normalise(start)[0] * vector(0) + vector(1)).astype(BF16)
    scale = SCORE_SCALE * LOG2E
    query_one_ref[0] = ((nn(normed, self_query[...]) + vector(2)) * scale).astype(BF16)
    key_one_ref[0] = nn(normed, self_key[...]).astype(BF16)
    value = (nn(normed, self_value[...]) + vector(3)).astype(BF16)
    value_one_ref[0] = value
    value_t_ref[...] = value.T
    attend(
        attend_self,
        query_one_ref.at[0],
        key_one_ref.at[0],
        value_t_ref,
        context_one_ref.at[0],
        logsum_one_ref.at[0],
    )
    middle = start + tn(context_one_ref[0], self_out[...]) + vector(4)
    middle_ref[0] = middle
    normed = (normalise(middle)[0] * vector(5) + vector(6)).astype(BF16)
    memory = memory_ref[0]
    query_two_ref[0] = ((nn(normed, cross_query[...]) + vector(7)) * scale).astype(BF16)
    key_two_ref[0] = nn(memory, cross_key[...]).astype(BF16)
    value = (nn(memory, cross_value[...]) + vector(8)).astype(BF16)
    value_two_ref[0] = value
    value_t_ref[...] = value.T
    attend(
        attend_cross,
        query_two_ref.at[0],
        key_two_ref.at[0],
        value_t_ref,
        context_two_ref.at[0],
        logsum_two_ref.at[0],
        key_bias(memory_length_ref[sequence], memory.shape[0]),
    )
    later = middle_ref[0] + tn(context_two_ref[0], cross_out[...]) + vector(9)
    later_ref[0] = later
    normed = (normalise(later)[0] * vector(10) + vector(11)).astype(BF16)
    for at in range(steps):

        @pl.when(step == at)
        def _():
            normed_refs[at][...] = normed


def expert_kernel(
    slot,
    pick_ref,
    used_ref,
    rows_ref,
    grads_ref,
    weight_in,
    bias_in,
    weight_out,
    bias_out,
    hidden_ref,
    grad_pre_ref,
    made_ref,
    grad_rows_ref,
    pre_sum_ref,
    grads_sum_ref,
    made_sum,
    grad_sum,
):
    tile = pl.program_id(0)
    last = pl.num_programs(0) - 1
    used = used_ref[slot] > 0
    pick = pl.ds(pick_ref[slot], 1)

    @pl.when(used)
    def _():
        pre = nn(rows_ref[...], weight_in[0]) + bias_in[pick, :]
        grad_hidden = nt(grads_ref[...], weight_out[0])
        gate = 0.5 * jnp.tanh(0.5 * pre) + 0.5
        active = pre * gate
        hidden = active.astype(BF16)
        hidden_ref[...] = hidden
        grad_pre = grad_hidden * (gate + active * (1.0 - gate))
        pre_sum_ref[...] = jnp.sum(grad_pre, axis=0, keepdims=True)
        grad_pre = grad_pre.astype(BF16)
        grad_pre_ref[...] = grad_pre
        made = nn(hidden, weight_out[0])
        grad_rows = nt(grad_pre, weight_in[0])

        @pl.when(tile == 0)
        def _():
            made_sum[...] = made
            grad_sum[...] = grad_rows
            grads_sum_ref[...] = column_sum(grads_ref[...])

        @pl.when(tile > 0)
        def _():
            made_sum[...] += made
            grad_sum[...] += grad_rows

        @pl.when(tile == last)
        def _():
            made_ref[...] = (made_sum[...] + bias_out[pick, :]).astype(BF16)
            grad_rows_ref[...] = grad_sum[...].astype(BF16)

    @pl.when(jnp.logical_not(used))
    def _():
        for ref in (hidden_ref, grad_pre_ref, made_ref, grad_rows_ref, pre_sum_ref, grads_sum_ref):
            ref[...] = jnp.zeros_like(ref)


def expert_weights_kernel(slots, pick_ref, used_ref, *refs):
    rows, grads, hidden, grad_pre, pre_sum, grads_sum = [
        refs[at * slots : (at + 1) * slots] for at in range(6)
    ]
    in_ref, out_ref, lines_ref, in_sum, out_sum, in_bias, out_bias = refs[6 * slots :]
    for total in (in_sum, out_sum, in_bias, out_bias):
        total[...] = jnp.zeros_like(total)
    for slot in range(slots):

        @pl.when(used_ref[slot] > 0)
        def _():
            pick = pick_ref[slot]
            in_sum[pick] += tn(rows[slot][...], grad_pre[slot][...])
            out_sum[pick] += tn(hidden[slot][...], grads[slot][...])
            in_bias[pick] += pre_sum[slot][...]
            out_bias[pick] += grads_sum[slot][...]

    in_ref[...] = in_sum[...].astype(BF16)
    out_ref[...] = out_sum[...].astype(BF16)
    tile, tiles = pl.program_id(0), pl.num_programs(0)
    count = in_bias.shape[0]

    @pl.when(tile == 0)
    def _():
        lines_ref[...] = jnp.zeros_like(lines_ref)

    for pick in range(count):
        lines_ref[pl.ds(pick * tiles + tile, 1), :] = in_bias[pick]
        lines_ref[pl.ds(count * tiles + pick, 1), :] = out_bias[pick]


def plan_kernel(
    shifts,
    local_count,
    place_ref,
    expert_ref,
    target_ref,
    cotangent_ref,
    order_ref,
    pick_ref,
    used_ref,
    slot_ref,
    spot_ref,
    *grads_refs,
):
    groups, seqs = len(shifts), cotangent_ref.shape[0]
    own, column, places = place_ref[0], place_ref[1], place_ref[2]
    own_ids = [expert_ref[(own * places + column) * seqs + at] for at in range(seqs)]
    distance = [lax.rem(lax.div(item, local_count) - own + groups, groups) for item in own_ids]
    slots = [
        sum((jnp.where(item == shift, at, 0) for at, shift in enumerate(shifts)), jnp.int32(0))
        for item in distance
    ]
    for slot in range(groups):
        spot_ref[slot] = 0
        source = lax.rem(own - shifts[slot] + groups, groups)
        pick, used = jnp.int32(0), jnp.int32(0)
        for at in range(seqs):
            item = expert_ref[(source * places + column) * seqs + at]
            here = lax.div(item, local_count) == own
            pick = jnp.where(here, lax.rem(item, local_count), pick)
            used = jnp.where(here, 1, used)
        pick_ref[slot] = pick
        used_ref[slot] = used
    for at in range(seqs):
        spot = sum((jnp.where(other < slots[at], 1, 0) for other in slots), jnp.int32(0))
        order_ref[spot] = at
        slot_ref[spot] = slots[at]
        spot_ref[slots[at]] = spot
    order_ref[seqs] = order_ref[0]
    length = cotangent_ref.shape[1]
    for slot in range(groups):
        sequence = order_ref[spot_ref[slot]]
        valid = valid_rows_of(target_ref[sequence], length)
        grads_refs[slot][...] = (cotangent_ref[sequence].astype(F32) * valid).astype(BF16)


def output_kernel(slots, order_ref, target_ref, later_ref, *refs):
    made, output_ref = refs[:slots], refs[slots]
    position = pl.program_id(0)
    valid = valid_rows_of(target_ref[order_ref[position]], later_ref.shape[1])
    for at in range(slots):

        @pl.when(position == at)
        def _():
            output_ref[0] = ((later_ref[0] + made[at][...].astype(F32)) * valid).astype(BF16)


def open_sums(first, weight_sum, vector_sum, given):
    @pl.when(pl.program_id(0) == 0)
    def _():
        if first:
            weight_sum[...] = jnp.zeros_like(weight_sum)
            vector_sum[...] = jnp.zeros_like(vector_sum)
        else:
            weight_sum[...] = given[0][...]
            vector_sum[...] = given[1][...]


def put_halves(squares, lines, high, keep_ref, give_ref):
    height = squares[0].shape[0]
    half = height * len(squares) // 2
    for top, (low_ref, high_ref) in ((0, (keep_ref, give_ref)), (1, (give_ref, keep_ref))):

        @pl.when(high == top)
        def _():
            for at, square in enumerate(squares):
                for part, ref in enumerate((low_ref, high_ref)):
                    start, stop = max(at * height, part * half), min((at + 1) * height, (part + 1) * half)
                    if start < stop:
                        rows = square[start - at * height : stop - at * height]
                        ref[start - part * half : stop - part * half] = rows.astype(BF16)

    if lines is not None:
        keep_ref[half:] = lines.astype(BF16)
        give_ref[half:] = lines.astype(BF16)


def close_sums(final, weight_sum, vector_sum, high, outs):
    @pl.when(pl.program_id(0) == pl.num_programs(0) - 1)
    def _():
        outs[-1][...] = vector_sum[...]
        if final:
            squares = [weight_sum[0].T] + [weight_sum[at] for at in range(1, weight_sum.shape[0])]
            put_halves(squares, None, high, outs[0], outs[1])
        else:
            outs[0][...] = weight_sum[...]


def cross_back_kernel(
    start_at, first, final, slots, order_ref, target_ref, memory_length_ref, high_ref, *refs
):
    grad_normed, refs = refs[:slots], refs[slots:]
    given, refs = (None, refs) if first else (refs[:2], refs[2:])
    (
        cotangent_ref,
        memory_ref,
        later_ref,
        middle_ref,
        query_ref,
        key_ref,
        value_ref,
        context_ref,
        logsum_ref,
        context_one_ref,
        vectors_ref,
        cross_query,
        cross_key,
        cross_value,
        cross_out,
        grad_middle_ref,
        grad_key_ref,
        grad_value_ref,
        *outs,
        weight_sum,
        vector_sum,
        grad_expert,
        key_t,
        grad_context,
        delta,
        grad_query_t,
    ) = refs
    step = pl.program_id(0)
    sequence = order_ref[lax.rem(start_at + step, order_ref.shape[0] - 1)]
    length = cotangent_ref.shape[1]
    vector = lambda at: vectors_ref[at : at + 1, :]
    open_sums(first, weight_sum, vector_sum, given)

    for at in range(slots):

        @pl.when(step == at)
        def _():
            grad_expert[...] = grad_normed[at][...]

    def add_vector(at, value):
        vector_sum[at : at + 1, :] += value

    valid = valid_rows_of(target_ref[sequence], length)
    normed, inverse = normalise(later_ref[0])
    grad = grad_expert[...].astype(F32)
    add_vector(0, column_sum(grad * normed))
    add_vector(1, column_sum(grad))
    grad_later = cotangent_ref[0].astype(F32) * valid + normalise_back(
        grad, normed, inverse, vector(10)
    )
    branch = grad_later.astype(BF16)
    grad_middle_ref[0] = grad_later
    add_vector(2, column_sum(branch))
    weight_sum[3] += nn(context_ref[0], branch)
    context_grad = nt(branch, cross_out[...]).astype(BF16)
    grad_context[...] = context_grad
    delta[...] = head_sums(context_grad, context_ref[0])
    key_t[...] = key_ref[0].T
    attend_cross_back(
        query_ref.at[0],
        key_ref.at[0],
        value_ref.at[0],
        key_t,
        grad_context,
        delta,
        logsum_ref.at[0],
        grad_query_t,
        grad_key_ref.at[0],
        grad_value_ref.at[0],
        key_bias(memory_length_ref[sequence], memory_ref.shape[1]),
    )
    memory_t = memory_ref[0].T
    weight_sum[1] += nn(memory_t, grad_key_ref[0])
    weight_sum[2] += nn(memory_t, grad_value_ref[0])
    add_vector(3, column_sum(grad_value_ref[0]))
    normed, inverse = normalise(middle_ref[0])
    weight_sum[0] += nn(grad_query_t[...], (normed * vector(5) + vector(6)).astype(BF16))
    grad_query = grad_query_t[...].T
    add_vector(4, column_sum(grad_query))
    grad = nt(grad_query, cross_query[...])
    add_vector(5, column_sum(grad * normed))
    add_vector(6, column_sum(grad))
    grad_middle = grad_middle_ref[0] + normalise_back(grad, normed, inverse, vector(5))
    grad_middle_ref[0] = grad_middle
    branch = grad_middle.astype(BF16)
    add_vector(7, column_sum(branch))
    weight_sum[4] += nn(context_one_ref[0], branch)
    close_sums(final, weight_sum, vector_sum, high_ref[0], outs)


def self_back_kernel(start_at, first, final, order_ref, target_ref, high_ref, *refs):
    given, refs = (None, refs) if first else (refs[:2], refs[2:])
    cross_lines_ref, expert_lines_ref = refs[:2]
    refs = refs[2:]
    (
        tokens_ref,
        grad_middle_ref,
        query_ref,
        key_ref,
        value_ref,
        context_ref,
        logsum_ref,
        columns_ref,
        self_query,
        self_key,
        self_value,
        self_out,
        grad_query_ref,
        grad_key_ref,
        grad_value_ref,
        first_ref,
        second_ref,
        weight_sum,
        vector_sum,
        key_t,
        grad_context,
        delta,
        grad_query_t,
    ) = refs
    step = pl.program_id(0)
    sequence = order_ref[lax.rem(start_at + step, order_ref.shape[0] - 1)]
    length = tokens_ref.shape[1]
    open_sums(first, weight_sum, vector_sum, given)

    valid = valid_rows_of(target_ref[sequence], length)
    context_grad = nt(grad_middle_ref[0].astype(BF16), self_out[...]).astype(BF16)
    grad_context[...] = context_grad
    delta[...] = head_sums(context_grad, context_ref[0])
    key_t[...] = key_ref[0].T
    attend_self_back(
        query_ref.at[0],
        key_ref.at[0],
        value_ref.at[0],
        key_t,
        grad_context,
        delta,
        logsum_ref.at[0],
        grad_query_t,
        grad_key_ref.at[0],
        grad_value_ref.at[0],
    )
    normed = normalise(tokens_ref[0].astype(F32) * valid)[0].astype(BF16)
    normed_t = normed.T
    weight_sum[0] += nn(grad_query_t[...], normed)
    weight_sum[1] += nn(normed_t, grad_key_ref[0])
    weight_sum[2] += nn(normed_t, grad_value_ref[0])
    grad_query = grad_query_t[...].T
    grad_query_ref[0] = grad_query
    for at, item in enumerate((grad_query, grad_key_ref[0], grad_value_ref[0])):
        vector_sum[at : at + 1, :] += column_sum(item)

    @pl.when(step == pl.num_programs(0) - 1)
    def _():
        if not final:
            first_ref[...] = weight_sum[...]
            second_ref[...] = vector_sum[...]
            return
        width = weight_sum.shape[1]
        gain, shift = columns_ref[:, 0:1], columns_ref[:, 1:2]
        gain_grad = jnp.zeros((width, 1), F32)
        shift_grad = jnp.zeros((width, 1), F32)
        squares = []
        for at, matrix in enumerate((self_query, self_key, self_value)):
            total = weight_sum[at].T if at == 0 else weight_sum[at]
            column = vector_sum[at : at + 1, :]
            weights = matrix[...].astype(F32)
            gain_grad += jnp.sum(weights * total, axis=1, keepdims=True)
            shift_grad += jnp.sum(weights * column, axis=1, keepdims=True)
            squares.append((total * gain + shift * column).astype(BF16))
        lane = lax.broadcasted_iota(jnp.int32, (width, 128), 1)
        both = jnp.where(lane == 0, gain_grad, jnp.where(lane == 1, shift_grad, 0.0)).T
        lines = jnp.concatenate(
            [
                vector_sum[0:1, :],
                vector_sum[2:3, :],
                both[0:2, :],
                jnp.zeros((4, width), F32),
                cross_lines_ref[...],
                expert_lines_ref[...],
            ],
            axis=0,
        )
        put_halves(squares, lines, high_ref[0], first_ref, second_ref)


def tokens_back_kernel(
    start_at,
    order_ref,
    target_ref,
    tokens_ref,
    grad_middle_ref,
    grad_query_ref,
    grad_key_ref,
    grad_value_ref,
    vectors_ref,
    self_query,
    self_key,
    self_value,
    tokens_grad_ref,
):
    sequence = order_ref[lax.rem(start_at + pl.program_id(0), order_ref.shape[0] - 1)]
    valid = valid_rows_of(target_ref[sequence], tokens_ref.shape[1])
    normed, inverse = normalise(tokens_ref[0].astype(F32) * valid)
    grad = (
        nt(grad_query_ref[0], self_query[...])
        + nt(grad_key_ref[0], self_key[...])
        + nt(grad_value_ref[0], self_value[...])
    )
    tokens_grad_ref[0] = (
        grad_middle_ref[0] + normalise_back(grad, normed, inverse, vectors_ref[0:1, :])
    ) * valid


def memory_back_kernel(order_ref, grad_key_ref, grad_value_ref, cross_key, cross_value, memory_grad_ref):
    memory_grad_ref[0] = nt(grad_key_ref[0], cross_key[...]) + nt(
        grad_value_ref[0], cross_value[...]
    )


def apart(at, count, turn):
    return at ^ turn if count & (count - 1) == 0 else lax.rem(at + turn, count)


def heard(at, count, turn):
    return at ^ turn if count & (count - 1) == 0 else lax.rem(at + count - turn, count)


def fold_kernel(sizes, lines, shared, count, at_ref, *refs):
    items = sum(sizes)
    parts, outs = refs[:items], refs[items:]
    totals = []
    for size in sizes:
        total = parts[0][...].astype(F32)
        for part in parts[1:size]:
            total = total + part[...].astype(F32)
        totals.append(total)
        parts = parts[size:]
    heights = [total.shape[0] for total in totals]
    heights[-1] -= lines
    if count == 1:
        outs[0][...] = totals[0][: heights[0]].astype(BF16)
        if lines:
            outs[1][...] = totals[0][heights[0] :]
        return
    at, stacks, start = at_ref[0], refs[-len(sizes) :], 0
    for total, height, stack in zip(totals, heights, stacks):
        share = height // count
        stack[...] = total[:height].astype(BF16)
        for turn in range(count):
            which = pl.multiple_of(apart(at, count, turn) * share, 16)
            outs[turn][start : start + share] = stack[pl.ds(which, share), :]
        start += share
    last = heights[-1]
    if shared:
        for turn in range(count):
            outs[turn][start:] = totals[-1][last : last + shared].astype(BF16)
    if lines > shared:
        outs[count][...] = totals[-1][last + shared :]


def spread_kernel(count, at_ref, *refs):
    parts, out = refs[:count], refs[count]
    share = parts[0].shape[0]
    for turn in range(count):
        place = pl.multiple_of(heard(at_ref[0], count, turn) * share, 16)
        out[pl.ds(place, share), :] = parts[turn][...]


def finish_kernel(places, counts, high_ref, own_ref, got_ref, *outs):
    own, got = own_ref[...].astype(F32), got_ref[...].astype(F32)
    top = high_ref[0] > 0
    halves = [jnp.where(top, got, own), jnp.where(top, own, got)]
    height = outs[0].shape[0]
    shares = [height * count // (2 * places) for count in counts]
    block = sum(shares)
    for half in (0, 1):
        for place in range(places):
            source, first = place * block, 0
            for count, share in zip(counts, shares):
                row, left = (half * places + place) * share, share
                while left:
                    at, inside = divmod(row, height)
                    size = min(left, height - inside)
                    outs[first + at][inside : inside + size] = halves[half][source : source + size]
                    row, source, left = row + size, source + size, left - size
                first += count


def cast_kernel(*refs):
    count = len(refs) // 2
    for source, out in zip(refs[:count], refs[count:]):
        out[...] = source[...].astype(F32)


def fixed(shape):
    return pl.BlockSpec(shape, lambda *_: (0,) * len(shape))


def once(shape):
    return pl.BlockSpec(shape, lambda *_: (0,) * len(shape), pipeline_mode=pl.Buffered(1))


def at_position(shape, start, count):
    return pl.BlockSpec(
        (1,) + shape, lambda step, *_: (lax.rem(start + step, count),) + (0,) * len(shape)
    )


def at_sequence(shape, start, count):
    return pl.BlockSpec(
        (1,) + shape,
        lambda step, order, *_: (order[lax.rem(start + step, count)],) + (0,) * len(shape),
    )


def struct(shape, kind):
    return jax.ShapeDtypeStruct(shape, kind)


def launch(
    kernel,
    name,
    grid,
    scalars,
    inputs,
    in_specs,
    outs,
    out_specs,
    scratch=(),
    micros=10,
    after=(),
    into=None,
    carry=(),
):
    into = into or {}
    extra = list(after) + list(into.values()) + list(carry)
    lead, made = len(scalars) + len(inputs), len(outs)
    anywhere = pl.BlockSpec(memory_space=pl.ANY)

    def body(*refs):
        rest = refs[lead + len(extra) :]
        kernel(*refs[:lead], *rest[:made], *rest[made + len(carry) :])

    aliases = {lead + len(after) + at: out for at, out in enumerate(into)}
    first = lead + len(after) + len(into)
    aliases.update({first + at: made + at for at in range(len(carry))})
    return pl.pallas_call(
        body,
        grid_spec=pltpu.PrefetchScalarGridSpec(
            num_scalar_prefetch=len(scalars),
            grid=grid,
            in_specs=list(in_specs) + [anywhere] * len(extra),
            out_specs=list(out_specs) + [anywhere] * len(carry),
            scratch_shapes=list(scratch),
        ),
        out_shape=[struct(shape, kind) for shape, kind in outs]
        + [struct(item.shape, item.dtype) for item in carry],
        input_output_aliases=aliases,
        compiler_params=pltpu.CompilerParams(
            dimension_semantics=("arbitrary",) * len(grid), vmem_limit_bytes=VMEM_LIMIT
        ),
        cost_estimate=pl.CostEstimate(
            flops=int(micros * 1.0e9), bytes_accessed=int(micros * 2.0e6), transcendentals=0
        ),
        name=name,
    )(*scalars, *inputs, *extra)


def gate(item, after):
    (item,) = launch(
        lambda *_: None, "gate", (1,), (), (), [], [], [], micros=1, after=after, carry=[item]
    )
    return item


def exchange(rows, way, turn):
    axis, stride, count = way
    route = []
    for place in range(lax.axis_size(axis)):
        at = (place // stride) % count
        other = at ^ turn if count & (count - 1) == 0 else (at + turn) % count
        route.append((place, place + (other - at) * stride))
    return lax.ppermute(rows, axis, route)


def coordinate(way):
    axis, stride, count = way
    return ((lax.axis_index(axis) // stride) % count).astype(jnp.int32)


def fold(stacks, lines, way, shared=0, after=()):
    count = 1 if way is None else way[2]
    heights, width = [parts[0].shape[0] for parts in stacks], stacks[0][0].shape[1]
    heights[-1] -= lines
    shares = [height // count for height in heights]
    outs = [((sum(shares) + shared, width), BF16)] * count
    if way is None:
        outs += [((lines, width), F32)] if lines else []
    elif lines > shared:
        outs += [((lines - shared, width), F32)]
    parts = [part for stack in stacks for part in stack]
    if all(share % 16 == 0 for share in shares):
        at = coordinate(way).reshape(1) if way else jnp.zeros((1,), jnp.int32)
        return launch(
            functools.partial(fold_kernel, [len(stack) for stack in stacks], lines, shared, count),
            "fold",
            (1,),
            (at,),
            tuple(parts),
            [fixed(part.shape) for part in parts],
            outs,
            [fixed(shape) for shape, _ in outs],
            [pltpu.VMEM((height, width), BF16) for height in heights] if count > 1 else [],
            micros=2,
            after=after,
        )
    (height,), (share,) = heights, shares
    total = sum(part.astype(F32) for part in parts)
    if way is None:
        return [total[:height].astype(BF16)] + ([total[height:]] if lines else [])
    at = coordinate(way)
    results = [
        jnp.concatenate(
            [
                lax.dynamic_slice_in_dim(total, apart(at, count, turn) * share, share, 0),
                total[height : height + shared],
            ],
            axis=0,
        ).astype(BF16)
        for turn in range(count)
    ]
    return results + ([total[height + shared :]] if lines > shared else [])


def swap(gives, way):
    return [gives[0]] + [exchange(gives[turn], way, turn) for turn in range(1, way[2])]


def fetch(own, way):
    return [own] + [exchange(own, way, turn) for turn in range(1, way[2])]


def spread(parts, way, after=(), carry=()):
    own, count = parts[0], way[2]
    share, width = own.shape
    at = coordinate(way)
    if share % 16 == 0:
        whole, *carry = launch(
            functools.partial(spread_kernel, count),
            "spread",
            (1,),
            (at.reshape(1),),
            tuple(parts),
            [fixed(own.shape)] * count,
            [((share * count, width), BF16)],
            [fixed((share * count, width))],
            micros=2,
            after=after,
            carry=carry,
        )
        return (whole, *carry) if carry else whole
    stack = jnp.stack(parts)
    turns = [at ^ place if count & (count - 1) == 0 else (at - place) % count for place in range(count)]
    whole = jnp.concatenate(
        [lax.dynamic_index_in_dim(stack, turn, 0, False) for turn in turns], axis=0
    )
    return (whole, *carry) if carry else whole


def finish(own, got, width, places, counts, after=()):
    high = (lax.axis_index("dp") % 2).astype(jnp.int32).reshape(1)
    squares = sum(counts)
    return launch(
        functools.partial(finish_kernel, places, counts),
        "finish",
        (1,),
        (high,),
        (own, got),
        [fixed(own.shape)] * 2,
        [((width, width), F32)] * squares,
        [fixed((width, width))] * squares,
        micros=2,
        after=after,
    )


def on_device(
    tokens,
    memory,
    cotangent,
    target_length,
    memory_length,
    expert_of,
    self_norm_gain,
    self_norm_bias,
    self_query,
    self_key,
    self_value,
    self_out,
    self_query_bias,
    self_value_bias,
    self_out_bias,
    cross_norm_gain,
    cross_norm_bias,
    cross_query,
    cross_key,
    cross_value,
    cross_out,
    cross_attention_query_bias,
    cross_value_bias,
    cross_out_bias,
    expert_norm_gain,
    expert_norm_bias,
    expert_in,
    expert_in_bias,
    expert_out,
    expert_out_bias,
):
    seqs, length, width = tokens.shape
    mem_rows = memory.shape[1]
    local_count, _, hidden_width = expert_in.shape
    groups = lax.axis_size("expert")
    places = lax.axis_size("dp")
    own_group = lax.axis_index("expert")
    column = lax.axis_index("dp")

    shifts = list(range(1, groups)) + [0]
    whole = groups == seqs
    rows_shape, square = (length, width), (width, width)
    mem_shape, heads_shape = (mem_rows, width), (HEADS, length)
    turned = (width, length)
    in_smem = pl.BlockSpec(memory_space=pltpu.SMEM)
    order, picks, used, slot_of, spot_of, *grads = pl.pallas_call(
        functools.partial(plan_kernel, shifts, local_count),
        in_specs=[in_smem] * 3 + [pl.BlockSpec(memory_space=pltpu.VMEM)],
        out_specs=[in_smem] * 5 + [pl.BlockSpec(memory_space=pltpu.VMEM)] * groups,
        out_shape=[
            struct((seqs + 1,), jnp.int32),
            struct((groups,), jnp.int32),
            struct((groups,), jnp.int32),
            struct((seqs,), jnp.int32),
            struct((groups,), jnp.int32),
        ]
        + [struct(rows_shape, BF16)] * groups,
        compiler_params=pltpu.CompilerParams(vmem_limit_bytes=VMEM_LIMIT),
        name="plan",
    )(
        jnp.stack([own_group, column, jnp.int32(places)]).astype(jnp.int32),
        expert_of,
        target_length,
        cotangent,
    )

    def move(rows, slot, back=False):
        shift = shifts[slot]
        if shift == 0:
            return rows
        turn = -shift if back else shift
        return lax.ppermute(rows, "expert", [(g, (g + turn) % groups) for g in range(groups)])

    def arranged(per_slot):
        if whole:
            return per_slot
        stack = jnp.stack(per_slot)
        return [lax.dynamic_index_in_dim(stack, slot_of[at], 0, False) for at in range(seqs)]

    position = lambda shape, start=0: at_position(shape, start, seqs)
    sequence = lambda shape, start=0: at_sequence(shape, start, seqs)
    vectors = jnp.stack(
        [
            self_norm_gain,
            self_norm_bias,
            self_query_bias,
            self_value_bias,
            self_out_bias,
            cross_norm_gain,
            cross_norm_bias,
            cross_attention_query_bias,
            cross_value_bias,
            cross_out_bias,
            expert_norm_gain,
            expert_norm_bias,
        ]
        + [jnp.zeros_like(self_norm_gain)] * 4
    )
    self_matrices = (self_query, self_key, self_value, self_out)
    cross_matrices = (cross_query, cross_key, cross_value, cross_out)
    half = seqs // 2
    high = (column % 2).astype(jnp.int32).reshape(1)
    grads_in = [move(grads[slot], slot) for slot in range(groups)]

    saved = [
        (rows_shape, F32),
        (rows_shape, F32),
        (rows_shape, BF16),
        (rows_shape, BF16),
        (rows_shape, BF16),
        (turned, BF16),
        (heads_shape, F32),
        (rows_shape, BF16),
        (mem_shape, BF16),
        (mem_shape, BF16),
        (turned, BF16),
        (heads_shape, F32),
    ]

    def forward(start, steps, kept, after):
        results = launch(
            functools.partial(forward_kernel, start, steps),
            "forward",
            (steps,),
            (order, target_length, memory_length),
            (tokens, memory, vectors) + self_matrices + cross_matrices,
            [sequence(rows_shape, start), sequence(mem_shape, start), fixed(vectors.shape)]
            + [fixed(square)] * 8,
            [(rows_shape, BF16)] * steps + [((seqs,) + shape, kind) for shape, kind in saved],
            [fixed(rows_shape)] * steps + [position(shape, start) for shape, _ in saved],
            [pltpu.VMEM(turned, BF16)],
            micros=12 * steps,
            after=after,
            into={at + steps: item for at, item in enumerate(kept)},
        )
        return results[:steps], results[steps:]

    normed_one, kept = forward(0, half, [], [])
    normed_two, kept = forward(half, seqs - half, kept, [grads_in[0]])
    normed = list(normed_one) + list(normed_two)
    (
        later,
        middle,
        query_one,
        key_one,
        value_one,
        context_one,
        logsum_one,
        query_two,
        key_two,
        value_two,
        context_two,
        logsum_two,
    ) = kept

    if whole:
        rows_in = [move(normed[slot], slot) for slot in range(groups)]
    else:
        joined = jnp.stack(normed)
        rows_in = [
            move(lax.dynamic_index_in_dim(joined, spot_of[slot], 0, False), slot)
            for slot in range(groups)
        ]
    tiles = 4
    tile_width = hidden_width // tiles
    hidden_tile = pl.BlockSpec((length, tile_width), lambda t, *_: (0, t))
    line_tile = pl.BlockSpec((1, tile_width), lambda t, *_: (0, t))
    hidden, grad_pre, made, grad_rows, pre_sum, grads_sum = {}, {}, {}, {}, {}, {}

    def expert(slot, after):
        results = launch(
            functools.partial(expert_kernel, slot),
            "expert",
            (tiles,),
            (picks, used),
            (rows_in[slot], grads_in[slot], expert_in, expert_in_bias, expert_out, expert_out_bias),
            [
                fixed(rows_shape),
                fixed(rows_shape),
                pl.BlockSpec((1, width, tile_width), lambda t, pick, _: (pick[slot], 0, t)),
                pl.BlockSpec((local_count, tile_width), lambda t, *_: (0, t)),
                pl.BlockSpec((1, tile_width, width), lambda t, pick, _: (pick[slot], t, 0)),
                fixed((local_count, width)),
            ],
            [((length, hidden_width), BF16)] * 2
            + [(rows_shape, BF16)] * 2
            + [((1, hidden_width), F32), ((1, width), F32)],
            [hidden_tile, hidden_tile, fixed(rows_shape), fixed(rows_shape), line_tile]
            + [fixed((1, width))],
            [pltpu.VMEM(rows_shape, F32)] * 2,
            micros=1,
            after=after,
        )
        for table, result in zip((hidden, grad_pre, made, grad_rows, pre_sum, grads_sum), results):
            table[slot] = result

    back_scratch = [
        pltpu.VMEM((width, mem_rows), BF16),
        pltpu.VMEM(rows_shape, BF16),
        pltpu.VMEM(heads_shape, F32),
        pltpu.VMEM(turned, BF16),
    ]

    def sums_shape(count, final, lines=0):
        if final:
            return [((count * width // 2 + lines, width), BF16)] * 2
        return [((count,) + square, F32)]

    def cross_back(start, steps, grads, given, filled, final, after, carry=()):
        first = given is None
        total = sums_shape(5, final)
        return launch(
            functools.partial(cross_back_kernel, start, first, final, steps),
            "cross_back",
            (steps,),
            (order, target_length, memory_length, high),
            tuple(grads)
            + (() if first else tuple(given))
            + (cotangent, memory, later, middle, query_two, key_two, value_two, context_two)
            + (logsum_two, context_one, vectors)
            + cross_matrices,
            [once(rows_shape)] * steps
            + ([] if first else [once((5,) + square), once((8, width))])
            + [
                sequence(rows_shape, start),
                sequence(mem_shape, start),
                position(rows_shape, start),
                position(rows_shape, start),
                position(rows_shape, start),
                position(mem_shape, start),
                position(mem_shape, start),
                position(turned, start),
                position(heads_shape, start),
                position(turned, start),
                fixed(vectors.shape),
            ]
            + [once(square)] * 4,
            [((seqs,) + rows_shape, F32)]
            + [((seqs,) + mem_shape, BF16)] * 2
            + total
            + [((8, width), F32)],
            [position(rows_shape, start), position(mem_shape, start), position(mem_shape, start)]
            + [fixed(shape) for shape, _ in total]
            + [fixed((8, width))],
            [pltpu.VMEM((5,) + square, F32), pltpu.VMEM((8, width), F32), pltpu.VMEM(rows_shape, BF16)]
            + back_scratch,
            micros=13 * steps,
            after=after,
            into={at: item for at, item in enumerate(filled)},
            carry=carry,
        )

    def self_back(start, steps, given, filled, final, after):
        first = given is None
        total = sums_shape(3, final, LINES) if final else sums_shape(3, final) + [((8, width), F32)]
        return launch(
            functools.partial(self_back_kernel, start, first, final),
            "self_back",
            (steps,),
            (order, target_length, high),
            (() if first else tuple(given))
            + (cross_lines, expert_lines)
            + (tokens, grad_middle, query_one, key_one, value_one, context_one, logsum_one, columns)
            + self_matrices,
            ([] if first else [once((3,) + square), once((8, width))])
            + [fixed((8, width)), fixed((EXPERT_LINES, width))]
            + [
                sequence(rows_shape, start),
                position(rows_shape, start),
                position(rows_shape, start),
                position(rows_shape, start),
                position(rows_shape, start),
                position(turned, start),
                position(heads_shape, start),
                fixed(columns.shape),
            ]
            + [once(square)] * 4,
            [((seqs,) + rows_shape, BF16)] * 3 + total,
            [position(rows_shape, start)] * 3 + [fixed(shape) for shape, _ in total],
            [pltpu.VMEM((3,) + square, F32), pltpu.VMEM((8, width), F32)] + back_scratch,
            micros=10 * steps,
            after=after,
            into={at: item for at, item in enumerate(filled)},
        )

    back = {}

    def send_back(slot):
        back[slot] = move(grad_rows[slot], slot, True)

    if whole:
        expert(3, [])
        expert(0, [made[3]])
        expert(1, [made[0]])
        expert(2, [made[1]])
        for slot in range(groups):
            send_back(slot)
    else:
        for slot in range(groups):
            expert(slot, [])
            send_back(slot)

    in_sums, out_sums, expert_lines = launch(
        functools.partial(expert_weights_kernel, groups),
        "expert_weights",
        (tiles,),
        (picks, used),
        tuple(rows_in)
        + tuple(grads_in)
        + tuple(table[slot] for table in (hidden, grad_pre, pre_sum, grads_sum) for slot in range(groups)),
        [once(rows_shape)] * (2 * groups)
        + [hidden_tile] * (2 * groups)
        + [line_tile] * groups
        + [fixed((1, width))] * groups,
        [
            ((local_count, width, hidden_width), BF16),
            ((local_count, hidden_width, width), BF16),
            ((EXPERT_LINES, width), F32),
        ],
        [
            pl.BlockSpec((local_count, width, tile_width), lambda t, *_: (0, 0, t)),
            pl.BlockSpec((local_count, tile_width, width), lambda t, *_: (0, t, 0)),
            fixed((EXPERT_LINES, width)),
        ],
        [
            pltpu.VMEM((local_count, width, tile_width), F32),
            pltpu.VMEM((local_count, tile_width, width), F32),
            pltpu.VMEM((local_count, 1, tile_width), F32),
            pltpu.VMEM((local_count, 1, width), F32),
        ],
        micros=17,
        after=[back[0]] if whole else [],
    )
    expert_in_grad = lax.psum_scatter(in_sums, "dp", scatter_dimension=1, tiled=True)
    expert_out_grad = lax.psum_scatter(out_sums, "dp", scatter_dimension=1, tiled=True)

    if whole:
        away = [slot for slot in range(groups) if shifts[slot]]
        results = cross_back(
            3, 2, [back[3], back[0]], None, [], False, [in_sums], [made[slot] for slot in away]
        )
        filled, (weights_run, vectors_run) = results[:3], results[3:5]
        for at, slot in enumerate(away):
            made[slot] = results[5 + at]
        made_home = [move(made[slot], slot, True) for slot in range(groups)]
        *results, cross_keep, cross_give, cross_lines = cross_back(
            1, 2, [back[1], back[2]], (weights_run, vectors_run), filled, True, []
        )
    else:
        *results, cross_keep, cross_give, cross_lines = cross_back(
            0, seqs, arranged([back[slot] for slot in range(groups)]), None, [], True, []
        )
        made_home = arranged([move(made[slot], slot, True) for slot in range(groups)])
    grad_middle, grad_key_two, grad_value_two = results

    chips = places // 2
    core, plane, line = ("dp", 1, 2), ("dp", 2, chips), ("expert", 1, groups)
    columns = jnp.concatenate([vectors.T, jnp.zeros((width, 128 - vectors.shape[0]), F32)], axis=1)

    def tokens_back(start, steps, grads, filled, after):
        return launch(
            functools.partial(tokens_back_kernel, start),
            "tokens_back",
            (steps,),
            (order, target_length),
            (tokens, grad_middle, *grads, vectors)
            + self_matrices[:3],
            [sequence(rows_shape, start)]
            + [position(rows_shape, start)] * 4
            + [fixed(vectors.shape)]
            + [once(square)] * 3,
            [((seqs,) + rows_shape, F32)],
            [sequence(rows_shape, start)],
            micros=4 * steps,
            after=after,
            into={at: item for at, item in enumerate(filled)},
        )

    def memory_back(after):
        return launch(
            memory_back_kernel,
            "memory_back",
            (seqs,),
            (order,),
            (grad_key_two, grad_value_two, cross_key, cross_value),
            [position(mem_shape)] * 2 + [once(square)] * 2,
            [((seqs,) + mem_shape, F32)],
            [sequence(mem_shape)],
            micros=5,
            after=after,
        )[0]

    def output_rows(after):
        return launch(
            functools.partial(output_kernel, seqs),
            "output",
            (seqs,),
            (order, target_length),
            (later, *made_home),
            [position(rows_shape)] + [once(rows_shape)] * seqs,
            [((seqs,) + rows_shape, BF16)],
            [sequence(rows_shape)],
            micros=5,
            after=after,
        )[0]

    def casts(items, after):
        return launch(
            cast_kernel,
            "cast",
            (1,),
            (),
            tuple(items),
            [fixed(item.shape) for item in items],
            [(item.shape, F32) for item in items],
            [fixed(item.shape) for item in items],
            micros=3,
            after=after,
        )

    cross_got = exchange(gate(cross_give, made_home[:2]), core, 1)
    memory_grad = memory_back([])
    cross_parts = swap(fold([[cross_keep, cross_got]], 0, plane, after=[memory_grad]), plane)
    *grads_one, weights_run, vectors_run = self_back(
        0, half, None, [], False, [cross_parts[0]]
    )
    cross_line = swap(fold([cross_parts], 0, line, after=grads_one[:1]), line)
    filled = tokens_back(0, half, grads_one, [], cross_line[:1])
    (cross_share,) = fold([cross_line], 0, None, after=filled)
    cross_fetched = fetch(cross_share, line)
    *grads_one, self_keep, self_give = self_back(
        half,
        seqs - half,
        (weights_run, vectors_run),
        grads_one,
        True,
        [*made_home[2:3], cross_share, *filled],
    )

    cross_rows, self_give = spread(cross_fetched, line, after=[self_keep], carry=[self_give])
    self_got = exchange(self_give, core, 1)
    cross_fetched = fetch(cross_rows, plane)
    expert_in_grad, expert_out_grad = casts([expert_in_grad, expert_out_grad], [cross_rows])

    self_parts = swap(
        fold([[self_keep, self_got]], LINES, plane, LINES, after=[expert_in_grad]), plane
    )
    output = output_rows([self_parts[0]])

    *gives, own_lines = fold([self_parts], LINES, line, SHARED_LINES, after=[output])
    self_line = swap(gives, line)
    cross_rows = spread(cross_fetched, plane, after=[output])
    cross_got = exchange(cross_rows, core, 1)
    filled = tokens_back(half, 1, grads_one, filled, [self_line[0], cross_rows])

    self_share, totals = fold([self_line], SHARED_LINES, None, after=filled)
    self_fetched = fetch(self_share, line)
    (tokens_grad,) = tokens_back(half + 1, seqs - half - 1, grads_one, filled, [self_share])

    self_rows = spread(self_fetched, line, after=[tokens_grad])
    self_fetched = fetch(self_rows, plane)
    cross_q, cross_k, cross_v, cross_o, self_o = finish(
        cross_rows, cross_got, width, 1, [5], [self_rows]
    )
    self_rows = spread(self_fetched, plane, after=[cross_q])
    self_q, self_k, self_v = finish(self_rows, exchange(self_rows, core, 1), width, 1, [3])

    in_count = local_count * hidden_width // width
    in_bias = own_lines[:in_count].reshape(local_count, hidden_width)
    out_bias = own_lines[in_count : in_count + local_count]
    in_share, out_share = hidden_width // places, width // places
    return (
        output,
        tokens_grad,
        memory_grad,
        totals[2],
        totals[3],
        self_q,
        self_k,
        self_v,
        self_o,
        totals[0],
        totals[1],
        totals[15],
        totals[13],
        totals[14],
        cross_q,
        cross_k,
        cross_v,
        cross_o,
        totals[12],
        totals[11],
        totals[10],
        totals[8],
        totals[9],
        expert_in_grad,
        lax.dynamic_slice_in_dim(in_bias, column * in_share, in_share, 1),
        expert_out_grad,
        lax.dynamic_slice_in_dim(out_bias, column * out_share, out_share, 1),
    )


def solution(mesh):
    rows = P(("expert", "dp"), None, None)
    counts = P(("expert", "dp"))
    split = (P("expert", None, None), P("expert", None)) * 2
    shares = (P("expert", "dp", None), P("expert", "dp")) * 2
    return jax.shard_map(
        on_device,
        mesh=mesh,
        in_specs=(rows,) * 3 + (counts,) * 2 + (P(),) * 21 + split,
        out_specs=(rows,) * 3 + (P(),) * 20 + shares,
        check_vma=False,
    )
```

```python
import functools

import jax
import jax.numpy as jnp
from jax import lax
from jax.experimental import pallas as pl
from jax.experimental.pallas import tpu as pltpu
from jax.sharding import PartitionSpec as P

HEADS = 8
HEAD_DIM = 64
PAIR = 2 * HEAD_DIM
EPSILON = 1e-05
SCORE_SCALE = 0.125
NEGATIVE = -1e30
SAFE_SCORE = 80.0
SHARED_LINES = 16
EXPERT_LINES = 16
VECTORS = 12
LINES = SHARED_LINES + EXPERT_LINES
LOG2E = 1.4426950408889634
LN2 = 0.6931471805599453
VMEM_LIMIT = 64 * 1024 * 1024
F32 = jnp.float32
BF16 = jnp.bfloat16


def contract(left, right, left_dim, right_dim):
    return lax.dot_general(
        left, right, (((left_dim,), (right_dim,)), ((), ())), preferred_element_type=F32
    )


def nn(left, right):
    return contract(left, right, 1, 0)


def nt(left, right):
    return contract(left, right, 1, 1)


def tn(left, right):
    return contract(left, right, 0, 0)


def normalise(rows):
    centre = rows - jnp.mean(rows, axis=-1, keepdims=True)
    inverse = lax.rsqrt(jnp.mean(centre * centre, axis=-1, keepdims=True) + EPSILON)
    return centre * inverse, inverse


def normalise_back(grad, normed, inverse, gain):
    scaled = grad * gain
    return inverse * (
        scaled
        - jnp.mean(scaled, axis=-1, keepdims=True)
        - normed * jnp.mean(scaled * normed, axis=-1, keepdims=True)
    )


def column_sum(rows):
    return jnp.sum(rows.astype(F32), axis=0, keepdims=True)


def head_masks():
    lane = lax.broadcasted_iota(jnp.int32, (1, PAIR), 1)
    mine = [(lane // HEAD_DIM == half).astype(F32).astype(BF16) for half in (0, 1)]
    spare = [(lane == HEAD_DIM * (1 - half)).astype(F32).astype(BF16) for half in (0, 1)]
    return mine, spare


def key_bias(count, mem_rows):
    place = lax.broadcasted_iota(jnp.int32, (mem_rows, PAIR), 0)
    return jnp.where(place < count, 0.0, NEGATIVE).astype(BF16)


def score_operands(keys, queries, half, mine, spare, bias):
    picked = queries * mine[half]
    if bias is None:
        return keys, picked
    return keys * (1 - spare[half]) + bias * spare[half], picked + spare[half]


def causal(scores, block):
    key_at = lax.broadcasted_iota(jnp.int32, (scores.shape[0], block), 0)
    query_at = lax.broadcasted_iota(jnp.int32, (scores.shape[0], block), 1)
    return jnp.where(key_at <= query_at, scores, NEGATIVE)


def lower(items, block):
    return jnp.concatenate([item[block:] for item in items], axis=0)


def lower_columns(items, block):
    return jnp.concatenate([item[:, block:] for item in items], axis=1)


def span(start, size):
    return slice(start, start + size) if isinstance(start, int) else pl.ds(pl.multiple_of(start, size), size)


def head_rows(pair, half):
    return span(pair * PAIR + half * HEAD_DIM, HEAD_DIM)


def pair_span(pair):
    return span(pair * PAIR, PAIR)


def each_pair(pair_step, unrolled):
    if unrolled:
        for pair in range(HEADS // 2):
            pair_step(pair, 0)
    else:
        lax.fori_loop(0, HEADS // 2, pair_step, 0)


def head_part(both, half, block):
    return both[half * HEAD_DIM : (half + 1) * HEAD_DIM, half * block : (half + 1) * block]


def causal_pair_scores(keys, picked, block):
    upper = []
    for half in (0, 1):
        scores = nt(keys[:block], picked[half])
        upper.append(
            jnp.concatenate([causal(scores[:, :block], block), scores[:, block:]], axis=1)
        )
    scores = nt(keys[block:], lower(picked, block))
    low = jnp.concatenate([causal(scores[:, :block], block), causal(scores[:, block:], block)], axis=1)
    return upper, low


def head_blocks():
    feature = lax.broadcasted_iota(jnp.int32, (HEADS * HEAD_DIM, 128), 0)
    return (feature // HEAD_DIM == lax.broadcasted_iota(jnp.int32, (HEADS * HEAD_DIM, 128), 1)).astype(BF16)


def scores_small(query_ref, key_ref):
    blocks = head_blocks()
    squares = [nn(ref[...] * ref[...], blocks) for ref in (query_ref, key_ref)]
    most = [jnp.max(item, axis=0, keepdims=True) for item in squares]
    return jnp.max(most[0] * most[1]) < SAFE_SCORE * SAFE_SCORE


def attend_cross(plain, query_ref, key_ref, value_t_ref, context_t_ref, logsum_ref, bias):
    mine, spare = head_masks()

    def pair_step(pair, carry):
        columns = pair_span(pair)
        keys, queries = key_ref[:, columns], query_ref[:, columns]
        for half in (0, 1):
            rows = head_rows(pair, half)
            left, right = score_operands(keys, queries, half, mine, spare, bias)
            scores = nt(left, right)
            highest = 0.0 if plain else jnp.max(scores, axis=0, keepdims=True)
            raised = jnp.exp2(scores if plain else scores - highest)
            summed = jnp.sum(raised, axis=0, keepdims=True)
            context = nn(value_t_ref[rows, :], raised.astype(BF16))
            context_t_ref[rows, :] = (context * (1.0 / summed)).astype(BF16)
            logsum_ref[pl.ds(2 * pair + half, 1), :] = highest + LOG2E * jnp.log(summed)
        return carry

    each_pair(pair_step, plain)


def attend_self(plain, query_ref, key_ref, value_t_ref, context_t_ref, logsum_ref):
    block = query_ref.shape[0] // 2
    mine, _ = head_masks()

    def pair_step(pair, carry):
        columns = pair_span(pair)
        keys, queries = key_ref[:, columns], query_ref[:, columns]
        upper, low = causal_pair_scores(keys, [queries * mine[0], queries * mine[1]], block)
        if plain:
            highest = [0.0, 0.0]
            low = jnp.exp2(low)
        else:
            low_top = jnp.max(low, axis=0, keepdims=True)
            highest = []
            for half in (0, 1):
                top = jnp.max(upper[half], axis=0, keepdims=True)
                other = low_top[:, half * block : (half + 1) * block]
                highest.append(
                    jnp.concatenate([top[:, :block], jnp.maximum(top[:, block:], other)], axis=1)
                )
            low = jnp.exp2(low - lower_columns(highest, block))
        low_sum = jnp.sum(low, axis=0, keepdims=True)
        low_context = nn(value_t_ref[columns, block:], low.astype(BF16))
        for half in (0, 1):
            rows = head_rows(pair, half)
            raised = jnp.exp2(upper[half] if plain else upper[half] - highest[half])
            summed = jnp.sum(raised, axis=0, keepdims=True)
            part = low_sum[:, half * block : (half + 1) * block]
            summed = jnp.concatenate([summed[:, :block], summed[:, block:] + part], axis=1)
            context = nn(value_t_ref[rows, :block], raised.astype(BF16))
            context = jnp.concatenate(
                [context[:, :block], context[:, block:] + head_part(low_context, half, block)],
                axis=1,
            )
            context_t_ref[rows, :] = (context * (1.0 / summed)).astype(BF16)
            logsum_ref[pl.ds(2 * pair + half, 1), :] = highest[half] + LOG2E * jnp.log(summed)
        return carry

    each_pair(pair_step, plain)


def attend(kind, query_ref, key_ref, *refs):
    small = scores_small(query_ref, key_ref)

    @pl.when(small)
    def _():
        kind(True, query_ref, key_ref, *refs)

    @pl.when(jnp.logical_not(small))
    def _():
        kind(False, query_ref, key_ref, *refs)


def attend_cross_back(
    query_ref,
    key_ref,
    value_ref,
    key_t_ref,
    grad_ref,
    delta_ref,
    logsum_ref,
    grad_query_t_ref,
    grad_key_ref,
    grad_value_ref,
    bias,
):
    mine, spare = head_masks()

    def pair_step(pair, carry):
        columns = pair_span(pair)
        keys, queries, values = key_ref[:, columns], query_ref[:, columns], value_ref[:, columns]
        grads = grad_ref[:, columns]
        chances, slopes, picked_grads, picked_queries = [], [], [], []
        for half in (0, 1):
            head, rows = pl.ds(2 * pair + half, 1), head_rows(pair, half)
            left, right = score_operands(keys, queries, half, mine, spare, bias)
            picked_grads.append(grads * mine[half])
            picked_queries.append(queries * mine[half])
            chance = jnp.exp2(nt(left, right) - logsum_ref[head, :])
            slope = chance * (nt(values, picked_grads[half]) - delta_ref[head, :])
            chances.append(chance.astype(BF16))
            slopes.append(slope.astype(BF16))
            grad_query_t_ref[rows, :] = (nn(key_t_ref[rows, :], slopes[half]) * SCORE_SCALE).astype(
                BF16
            )
        grad_value_ref[:, columns] = nn(
            jnp.concatenate(chances, axis=1), jnp.concatenate(picked_grads, axis=0)
        ).astype(BF16)
        grad_key_ref[:, columns] = (
            nn(jnp.concatenate(slopes, axis=1), jnp.concatenate(picked_queries, axis=0)) * LN2
        ).astype(BF16)
        return carry

    each_pair(pair_step, True)


def attend_self_back(
    query_ref,
    key_ref,
    value_ref,
    key_t_ref,
    grad_ref,
    delta_ref,
    logsum_ref,
    grad_query_t_ref,
    grad_key_ref,
    grad_value_ref,
):
    block = query_ref.shape[0] // 2
    mine, _ = head_masks()

    def pair_step(pair, carry):
        columns = pair_span(pair)
        keys, queries, values = key_ref[:, columns], query_ref[:, columns], value_ref[:, columns]
        grads = grad_ref[:, columns]
        picked = [queries * mine[0], queries * mine[1]]
        picked_grads = [grads * mine[0], grads * mine[1]]
        upper, low = causal_pair_scores(keys, picked, block)
        logsum = [logsum_ref[pl.ds(2 * pair + half, 1), :] for half in (0, 1)]
        delta = [delta_ref[pl.ds(2 * pair + half, 1), :] for half in (0, 1)]
        low_grads = lower(picked_grads, block)
        low = jnp.exp2(low - lower_columns(logsum, block))
        low_slope = (
            low * (nt(values[block:], low_grads) - lower_columns(delta, block))
        ).astype(BF16)
        low_query = nn(key_t_ref[columns, block:], low_slope)
        chances, slopes = [], []
        for half in (0, 1):
            chance = jnp.exp2(upper[half] - logsum[half])
            slope = chance * (nt(values[:block], picked_grads[half]) - delta[half])
            chances.append(chance.astype(BF16))
            slopes.append(slope.astype(BF16))
            rows = head_rows(pair, half)
            grad = nn(key_t_ref[rows, :block], slopes[half])
            grad = jnp.concatenate(
                [grad[:, :block], grad[:, block:] + head_part(low_query, half, block)], axis=1
            )
            grad_query_t_ref[rows, :] = (grad * SCORE_SCALE).astype(BF16)
        grad_value_ref[:block, columns] = nn(
            jnp.concatenate(chances, axis=1), jnp.concatenate(picked_grads, axis=0)
        ).astype(BF16)
        grad_value_ref[block:, columns] = nn(low.astype(BF16), low_grads).astype(BF16)
        grad_key_ref[:block, columns] = (
            nn(jnp.concatenate(slopes, axis=1), jnp.concatenate(picked, axis=0)) * LN2
        ).astype(BF16)
        grad_key_ref[block:, columns] = (nn(low_slope, lower(picked, block)) * LN2).astype(BF16)
        return carry

    each_pair(pair_step, True)


def head_sums(grad, context_t):
    product = grad.T.astype(F32) * context_t.astype(F32)
    return jnp.sum(product.reshape(HEADS, HEAD_DIM, product.shape[1]), axis=1)


def valid_rows_of(count, length):
    return (lax.broadcasted_iota(jnp.int32, (length, 1), 0) < count).astype(F32)


def forward_kernel(
    start_at,
    steps,
    order_ref,
    target_ref,
    memory_length_ref,
    tokens_ref,
    memory_ref,
    vectors_ref,
    self_query,
    self_key,
    self_value,
    self_out,
    cross_query,
    cross_key,
    cross_value,
    cross_out,
    *refs,
):
    normed_refs, refs = refs[:steps], refs[steps:]
    (
    later_ref,
    middle_ref,
    query_one_ref,
    key_one_ref,
    value_one_ref,
    context_one_ref,
    logsum_one_ref,
    query_two_ref,
    key_two_ref,
    value_two_ref,
    context_two_ref,
    logsum_two_ref,
    value_t_ref,
    ) = refs
    step = pl.program_id(0)
    sequence = order_ref[start_at + step]
    length = tokens_ref.shape[1]
    vector = lambda at: vectors_ref[at : at + 1, :]
    start = tokens_ref[0].astype(F32) * valid_rows_of(target_ref[sequence], length)
    normed = (normalise(start)[0] * vector(0) + vector(1)).astype(BF16)
    scale = SCORE_SCALE * LOG2E
    query_one_ref[0] = ((nn(normed, self_query[...]) + vector(2)) * scale).astype(BF16)
    key_one_ref[0] = nn(normed, self_key[...]).astype(BF16)
    value = (nn(normed, self_value[...]) + vector(3)).astype(BF16)
    value_one_ref[0] = value
    value_t_ref[...] = value.T
    attend(
        attend_self,
        query_one_ref.at[0],
        key_one_ref.at[0],
        value_t_ref,
        context_one_ref.at[0],
        logsum_one_ref.at[0],
    )
    middle = start + tn(context_one_ref[0], self_out[...]) + vector(4)
    middle_ref[0] = middle
    normed = (normalise(middle)[0] * vector(5) + vector(6)).astype(BF16)
    memory = memory_ref[0]
    query_two_ref[0] = ((nn(normed, cross_query[...]) + vector(7)) * scale).astype(BF16)
    key_two_ref[0] = nn(memory, cross_key[...]).astype(BF16)
    value = (nn(memory, cross_value[...]) + vector(8)).astype(BF16)
    value_two_ref[0] = value
    value_t_ref[...] = value.T
    attend(
        attend_cross,
        query_two_ref.at[0],
        key_two_ref.at[0],
        value_t_ref,
        context_two_ref.at[0],
        logsum_two_ref.at[0],
        key_bias(memory_length_ref[sequence], memory.shape[0]),
    )
    later = middle_ref[0] + tn(context_two_ref[0], cross_out[...]) + vector(9)
    later_ref[0] = later
    normed = (normalise(later)[0] * vector(10) + vector(11)).astype(BF16)
    for at in range(steps):

        @pl.when(step == at)
        def _():
            normed_refs[at][...] = normed


def expert_kernel(
    slot,
    pick_ref,
    used_ref,
    rows_ref,
    grads_ref,
    weight_in,
    bias_in,
    weight_out,
    bias_out,
    hidden_ref,
    grad_pre_ref,
    made_ref,
    grad_rows_ref,
    pre_sum_ref,
    grads_sum_ref,
    made_sum,
    grad_sum,
):
    tile = pl.program_id(0)
    last = pl.num_programs(0) - 1
    used = used_ref[slot] > 0
    pick = pl.ds(pick_ref[slot], 1)

    @pl.when(used)
    def _():
        pre = nn(rows_ref[...], weight_in[0]) + bias_in[pick, :]
        grad_hidden = nt(grads_ref[...], weight_out[0])
        gate = 0.5 * jnp.tanh(0.5 * pre) + 0.5
        active = pre * gate
        hidden = active.astype(BF16)
        hidden_ref[...] = hidden
        grad_pre = grad_hidden * (gate + active * (1.0 - gate))
        pre_sum_ref[...] = jnp.sum(grad_pre, axis=0, keepdims=True)
        grad_pre = grad_pre.astype(BF16)
        grad_pre_ref[...] = grad_pre
        made = nn(hidden, weight_out[0])
        grad_rows = nt(grad_pre, weight_in[0])

        @pl.when(tile == 0)
        def _():
            made_sum[...] = made
            grad_sum[...] = grad_rows
            grads_sum_ref[...] = column_sum(grads_ref[...])

        @pl.when(tile > 0)
        def _():
            made_sum[...] += made
            grad_sum[...] += grad_rows

        @pl.when(tile == last)
        def _():
            made_ref[...] = (made_sum[...] + bias_out[pick, :]).astype(BF16)
            grad_rows_ref[...] = grad_sum[...].astype(BF16)

    @pl.when(jnp.logical_not(used))
    def _():
        for ref in (hidden_ref, grad_pre_ref, made_ref, grad_rows_ref, pre_sum_ref, grads_sum_ref):
            ref[...] = jnp.zeros_like(ref)


def expert_weights_kernel(slots, pick_ref, used_ref, *refs):
    rows, grads, hidden, grad_pre, pre_sum, grads_sum = [
        refs[at * slots : (at + 1) * slots] for at in range(6)
    ]
    in_ref, out_ref, lines_ref, in_sum, out_sum, in_bias, out_bias = refs[6 * slots :]
    for total in (in_sum, out_sum, in_bias, out_bias):
        total[...] = jnp.zeros_like(total)
    for slot in range(slots):

        @pl.when(used_ref[slot] > 0)
        def _():
            pick = pick_ref[slot]
            in_sum[pick] += tn(rows[slot][...], grad_pre[slot][...])
            out_sum[pick] += tn(hidden[slot][...], grads[slot][...])
            in_bias[pick] += pre_sum[slot][...]
            out_bias[pick] += grads_sum[slot][...]

    in_ref[...] = in_sum[...].astype(BF16)
    out_ref[...] = out_sum[...].astype(BF16)
    tile, tiles = pl.program_id(0), pl.num_programs(0)
    count = in_bias.shape[0]

    @pl.when(tile == 0)
    def _():
        lines_ref[...] = jnp.zeros_like(lines_ref)

    for pick in range(count):
        lines_ref[pl.ds(pick * tiles + tile, 1), :] = in_bias[pick]
        lines_ref[pl.ds(count * tiles + pick, 1), :] = out_bias[pick]


def plan_kernel(
    shifts,
    local_count,
    place_ref,
    expert_ref,
    target_ref,
    cotangent_ref,
    *refs,
):
    lines, refs = refs[:VECTORS], refs[VECTORS:]
    order_ref, pick_ref, used_ref, slot_ref, spot_ref, vectors_ref, *grads_refs = refs
    vectors_ref[...] = jnp.zeros_like(vectors_ref)
    for at, line in enumerate(lines):
        vectors_ref[at : at + 1, :] = line[...]

    groups, seqs = len(shifts), cotangent_ref.shape[0]
    own, column, places = place_ref[0], place_ref[1], place_ref[2]
    own_ids = [expert_ref[(own * places + column) * seqs + at] for at in range(seqs)]
    distance = [lax.rem(lax.div(item, local_count) - own + groups, groups) for item in own_ids]
    slots = [
        sum((jnp.where(item == shift, at, 0) for at, shift in enumerate(shifts)), jnp.int32(0))
        for item in distance
    ]
    for slot in range(groups):
        spot_ref[slot] = 0
        source = lax.rem(own - shifts[slot] + groups, groups)
        pick, used = jnp.int32(0), jnp.int32(0)
        for at in range(seqs):
            item = expert_ref[(source * places + column) * seqs + at]
            here = lax.div(item, local_count) == own
            pick = jnp.where(here, lax.rem(item, local_count), pick)
            used = jnp.where(here, 1, used)
        pick_ref[slot] = pick
        used_ref[slot] = used
    for at in range(seqs):
        spot = sum((jnp.where(other < slots[at], 1, 0) for other in slots), jnp.int32(0))
        order_ref[spot] = at
        slot_ref[spot] = slots[at]
        spot_ref[slots[at]] = spot
    order_ref[seqs] = order_ref[0]
    length = cotangent_ref.shape[1]
    for slot in range(groups):
        sequence = order_ref[spot_ref[slot]]
        valid = valid_rows_of(target_ref[sequence], length)
        grads_refs[slot][...] = (cotangent_ref[sequence].astype(F32) * valid).astype(BF16)


def output_kernel(slots, order_ref, target_ref, later_ref, *refs):
    made, output_ref = refs[:slots], refs[slots]
    position = pl.program_id(0)
    valid = valid_rows_of(target_ref[order_ref[position]], later_ref.shape[1])
    for at in range(slots):

        @pl.when(position == at)
        def _():
            output_ref[0] = ((later_ref[0] + made[at][...].astype(F32)) * valid).astype(BF16)


def open_sums(first, weight_sum, vector_sum, given):
    @pl.when(pl.program_id(0) == 0)
    def _():
        if first:
            weight_sum[...] = jnp.zeros_like(weight_sum)
            vector_sum[...] = jnp.zeros_like(vector_sum)
        else:
            weight_sum[...] = given[0][...]
            vector_sum[...] = given[1][...]


def put_halves(squares, lines, high, keep_ref, give_ref):
    height = squares[0].shape[0]
    half = height * len(squares) // 2
    for top, (low_ref, high_ref) in ((0, (keep_ref, give_ref)), (1, (give_ref, keep_ref))):

        @pl.when(high == top)
        def _():
            for at, square in enumerate(squares):
                for part, ref in enumerate((low_ref, high_ref)):
                    start, stop = max(at * height, part * half), min((at + 1) * height, (part + 1) * half)
                    if start < stop:
                        rows = square[start - at * height : stop - at * height]
                        ref[start - part * half : stop - part * half] = rows.astype(BF16)

    if lines is not None:
        keep_ref[half:] = lines.astype(BF16)
        give_ref[half:] = lines.astype(BF16)


def close_sums(final, weight_sum, vector_sum, high, outs):
    @pl.when(pl.program_id(0) == pl.num_programs(0) - 1)
    def _():
        outs[-1][...] = vector_sum[...]
        if final:
            squares = [weight_sum[0].T] + [weight_sum[at] for at in range(1, weight_sum.shape[0])]
            put_halves(squares, None, high, outs[0], outs[1])
        else:
            outs[0][...] = weight_sum[...]


def cross_back_kernel(
    start_at, first, final, slots, order_ref, target_ref, memory_length_ref, high_ref, *refs
):
    grad_normed, refs = refs[:slots], refs[slots:]
    given, refs = (None, refs) if first else (refs[:2], refs[2:])
    (
        cotangent_ref,
        memory_ref,
        later_ref,
        middle_ref,
        query_ref,
        key_ref,
        value_ref,
        context_ref,
        logsum_ref,
        context_one_ref,
        vectors_ref,
        cross_query,
        cross_key,
        cross_value,
        cross_out,
        grad_middle_ref,
        grad_key_ref,
        grad_value_ref,
        *outs,
        weight_sum,
        vector_sum,
        grad_expert,
        key_t,
        grad_context,
        delta,
        grad_query_t,
    ) = refs
    step = pl.program_id(0)
    sequence = order_ref[lax.rem(start_at + step, order_ref.shape[0] - 1)]
    length = cotangent_ref.shape[1]
    vector = lambda at: vectors_ref[at : at + 1, :]
    open_sums(first, weight_sum, vector_sum, given)

    for at in range(slots):

        @pl.when(step == at)
        def _():
            grad_expert[...] = grad_normed[at][...]

    def add_vector(at, value):
        vector_sum[at : at + 1, :] += value

    valid = valid_rows_of(target_ref[sequence], length)
    normed, inverse = normalise(later_ref[0])
    grad = grad_expert[...].astype(F32)
    add_vector(0, column_sum(grad * normed))
    add_vector(1, column_sum(grad))
    grad_later = cotangent_ref[0].astype(F32) * valid + normalise_back(
        grad, normed, inverse, vector(10)
    )
    branch = grad_later.astype(BF16)
    grad_middle_ref[0] = grad_later
    add_vector(2, column_sum(branch))
    weight_sum[3] += nn(context_ref[0], branch)
    context_grad = nt(branch, cross_out[...]).astype(BF16)
    grad_context[...] = context_grad
    delta[...] = head_sums(context_grad, context_ref[0])
    key_t[...] = key_ref[0].T
    attend_cross_back(
        query_ref.at[0],
        key_ref.at[0],
        value_ref.at[0],
        key_t,
        grad_context,
        delta,
        logsum_ref.at[0],
        grad_query_t,
        grad_key_ref.at[0],
        grad_value_ref.at[0],
        key_bias(memory_length_ref[sequence], memory_ref.shape[1]),
    )
    memory_t = memory_ref[0].T
    weight_sum[1] += nn(memory_t, grad_key_ref[0])
    weight_sum[2] += nn(memory_t, grad_value_ref[0])
    add_vector(3, column_sum(grad_value_ref[0]))
    normed, inverse = normalise(middle_ref[0])
    weight_sum[0] += nn(grad_query_t[...], (normed * vector(5) + vector(6)).astype(BF16))
    grad_query = grad_query_t[...].T
    add_vector(4, column_sum(grad_query))
    grad = nt(grad_query, cross_query[...])
    add_vector(5, column_sum(grad * normed))
    add_vector(6, column_sum(grad))
    grad_middle = grad_middle_ref[0] + normalise_back(grad, normed, inverse, vector(5))
    grad_middle_ref[0] = grad_middle
    branch = grad_middle.astype(BF16)
    add_vector(7, column_sum(branch))
    weight_sum[4] += nn(context_one_ref[0], branch)
    close_sums(final, weight_sum, vector_sum, high_ref[0], outs)


def self_back_kernel(start_at, first, final, order_ref, target_ref, high_ref, *refs):
    given, refs = (None, refs) if first else (refs[:2], refs[2:])
    cross_lines_ref, expert_lines_ref = refs[:2]
    refs = refs[2:]
    (
        tokens_ref,
        grad_middle_ref,
        query_ref,
        key_ref,
        value_ref,
        context_ref,
        logsum_ref,
        columns_ref,
        self_query,
        self_key,
        self_value,
        self_out,
        grad_query_ref,
        grad_key_ref,
        grad_value_ref,
        first_ref,
        second_ref,
        weight_sum,
        vector_sum,
        key_t,
        grad_context,
        delta,
        grad_query_t,
    ) = refs
    step = pl.program_id(0)
    sequence = order_ref[lax.rem(start_at + step, order_ref.shape[0] - 1)]
    length = tokens_ref.shape[1]
    open_sums(first, weight_sum, vector_sum, given)

    valid = valid_rows_of(target_ref[sequence], length)
    context_grad = nt(grad_middle_ref[0].astype(BF16), self_out[...]).astype(BF16)
    grad_context[...] = context_grad
    delta[...] = head_sums(context_grad, context_ref[0])
    key_t[...] = key_ref[0].T
    attend_self_back(
        query_ref.at[0],
        key_ref.at[0],
        value_ref.at[0],
        key_t,
        grad_context,
        delta,
        logsum_ref.at[0],
        grad_query_t,
        grad_key_ref.at[0],
        grad_value_ref.at[0],
    )
    normed = normalise(tokens_ref[0].astype(F32) * valid)[0].astype(BF16)
    normed_t = normed.T
    weight_sum[0] += nn(grad_query_t[...], normed)
    weight_sum[1] += nn(normed_t, grad_key_ref[0])
    weight_sum[2] += nn(normed_t, grad_value_ref[0])
    grad_query = grad_query_t[...].T
    grad_query_ref[0] = grad_query
    for at, item in enumerate((grad_query, grad_key_ref[0], grad_value_ref[0])):
        vector_sum[at : at + 1, :] += column_sum(item)

    @pl.when(step == pl.num_programs(0) - 1)
    def _():
        if not final:
            first_ref[...] = weight_sum[...]
            second_ref[...] = vector_sum[...]
            return
        width = weight_sum.shape[1]
        gain, shift = columns_ref[:, 0:1], columns_ref[:, 1:2]
        gain_grad = jnp.zeros((width, 1), F32)
        shift_grad = jnp.zeros((width, 1), F32)
        squares = []
        for at, matrix in enumerate((self_query, self_key, self_value)):
            total = weight_sum[at].T if at == 0 else weight_sum[at]
            column = vector_sum[at : at + 1, :]
            weights = matrix[...].astype(F32)
            gain_grad += jnp.sum(weights * total, axis=1, keepdims=True)
            shift_grad += jnp.sum(weights * column, axis=1, keepdims=True)
            squares.append((total * gain + shift * column).astype(BF16))
        lane = lax.broadcasted_iota(jnp.int32, (width, 128), 1)
        both = jnp.where(lane == 0, gain_grad, jnp.where(lane == 1, shift_grad, 0.0)).T
        lines = jnp.concatenate(
            [
                vector_sum[0:1, :],
                vector_sum[2:3, :],
                both[0:2, :],
                jnp.zeros((4, width), F32),
                cross_lines_ref[...],
                expert_lines_ref[...],
            ],
            axis=0,
        )
        put_halves(squares, lines, high_ref[0], first_ref, second_ref)


def tokens_back_kernel(
    start_at,
    order_ref,
    target_ref,
    tokens_ref,
    grad_middle_ref,
    grad_query_ref,
    grad_key_ref,
    grad_value_ref,
    vectors_ref,
    self_query,
    self_key,
    self_value,
    tokens_grad_ref,
):
    sequence = order_ref[lax.rem(start_at + pl.program_id(0), order_ref.shape[0] - 1)]
    valid = valid_rows_of(target_ref[sequence], tokens_ref.shape[1])
    normed, inverse = normalise(tokens_ref[0].astype(F32) * valid)
    grad = (
        nt(grad_query_ref[0], self_query[...])
        + nt(grad_key_ref[0], self_key[...])
        + nt(grad_value_ref[0], self_value[...])
    )
    tokens_grad_ref[0] = (
        grad_middle_ref[0] + normalise_back(grad, normed, inverse, vectors_ref[0:1, :])
    ) * valid


def memory_back_kernel(order_ref, grad_key_ref, grad_value_ref, cross_key, cross_value, memory_grad_ref):
    memory_grad_ref[0] = nt(grad_key_ref[0], cross_key[...]) + nt(
        grad_value_ref[0], cross_value[...]
    )


def apart(at, count, turn):
    return at ^ turn if count & (count - 1) == 0 else lax.rem(at + turn, count)


def heard(at, count, turn):
    return at ^ turn if count & (count - 1) == 0 else lax.rem(at + count - turn, count)


def fold_kernel(sizes, lines, shared, count, at_ref, *refs):
    items = sum(sizes)
    parts, outs = refs[:items], refs[items:]
    totals = []
    for size in sizes:
        total = parts[0][...].astype(F32)
        for part in parts[1:size]:
            total = total + part[...].astype(F32)
        totals.append(total)
        parts = parts[size:]
    heights = [total.shape[0] for total in totals]
    heights[-1] -= lines
    if count == 1:
        outs[0][...] = totals[0][: heights[0]].astype(BF16)
        if lines:
            outs[1][...] = totals[0][heights[0] :]
        return
    at, stacks, start = at_ref[0], refs[-len(sizes) :], 0
    for total, height, stack in zip(totals, heights, stacks):
        share = height // count
        stack[...] = total[:height].astype(BF16)
        for turn in range(count):
            which = pl.multiple_of(apart(at, count, turn) * share, 16)
            outs[turn][start : start + share] = stack[pl.ds(which, share), :]
        start += share
    last = heights[-1]
    if shared:
        for turn in range(count):
            outs[turn][start:] = totals[-1][last : last + shared].astype(BF16)
    if lines > shared:
        outs[count][...] = totals[-1][last + shared :]


def spread_kernel(count, at_ref, *refs):
    parts, out = refs[:count], refs[count]
    share = parts[0].shape[0]
    for turn in range(count):
        place = pl.multiple_of(heard(at_ref[0], count, turn) * share, 16)
        out[pl.ds(place, share), :] = parts[turn][...]


def finish_kernel(places, counts, high_ref, own_ref, got_ref, *outs):
    own, got = own_ref[...].astype(F32), got_ref[...].astype(F32)
    top = high_ref[0] > 0
    halves = [jnp.where(top, got, own), jnp.where(top, own, got)]
    height = outs[0].shape[0]
    shares = [height * count // (2 * places) for count in counts]
    block = sum(shares)
    for half in (0, 1):
        for place in range(places):
            source, first = place * block, 0
            for count, share in zip(counts, shares):
                row, left = (half * places + place) * share, share
                while left:
                    at, inside = divmod(row, height)
                    size = min(left, height - inside)
                    outs[first + at][inside : inside + size] = halves[half][source : source + size]
                    row, source, left = row + size, source + size, left - size
                first += count


def cast_kernel(*refs):
    count = len(refs) // 2
    for source, out in zip(refs[:count], refs[count:]):
        out[...] = source[...].astype(F32)


def fixed(shape):
    return pl.BlockSpec(shape, lambda *_: (0,) * len(shape))


def once(shape):
    return pl.BlockSpec(shape, lambda *_: (0,) * len(shape), pipeline_mode=pl.Buffered(1))


def at_position(shape, start, count):
    return pl.BlockSpec(
        (1,) + shape, lambda step, *_: (lax.rem(start + step, count),) + (0,) * len(shape)
    )


def at_sequence(shape, start, count):
    return pl.BlockSpec(
        (1,) + shape,
        lambda step, order, *_: (order[lax.rem(start + step, count)],) + (0,) * len(shape),
    )


def struct(shape, kind):
    return jax.ShapeDtypeStruct(shape, kind)


def launch(
    kernel,
    name,
    grid,
    scalars,
    inputs,
    in_specs,
    outs,
    out_specs,
    scratch=(),
    micros=10,
    after=(),
    into=None,
    carry=(),
):
    into = into or {}
    extra = list(after) + list(into.values()) + list(carry)
    lead, made = len(scalars) + len(inputs), len(outs)
    anywhere = pl.BlockSpec(memory_space=pl.ANY)

    def body(*refs):
        rest = refs[lead + len(extra) :]
        kernel(*refs[:lead], *rest[:made], *rest[made + len(carry) :])

    aliases = {lead + len(after) + at: out for at, out in enumerate(into)}
    first = lead + len(after) + len(into)
    aliases.update({first + at: made + at for at in range(len(carry))})
    return pl.pallas_call(
        body,
        grid_spec=pltpu.PrefetchScalarGridSpec(
            num_scalar_prefetch=len(scalars),
            grid=grid,
            in_specs=list(in_specs) + [anywhere] * len(extra),
            out_specs=list(out_specs) + [anywhere] * len(carry),
            scratch_shapes=list(scratch),
        ),
        out_shape=[struct(shape, kind) for shape, kind in outs]
        + [struct(item.shape, item.dtype) for item in carry],
        input_output_aliases=aliases,
        compiler_params=pltpu.CompilerParams(
            dimension_semantics=("arbitrary",) * len(grid), vmem_limit_bytes=VMEM_LIMIT
        ),
        cost_estimate=pl.CostEstimate(
            flops=int(micros * 1.0e9), bytes_accessed=int(micros * 2.0e6), transcendentals=0
        ),
        name=name,
    )(*scalars, *inputs, *extra)


def gate(item, after):
    (item,) = launch(
        lambda *_: None, "gate", (1,), (), (), [], [], [], micros=1, after=after, carry=[item]
    )
    return item


def exchange(rows, way, turn):
    axis, stride, count = way
    route = []
    for place in range(lax.axis_size(axis)):
        at = (place // stride) % count
        other = at ^ turn if count & (count - 1) == 0 else (at + turn) % count
        route.append((place, place + (other - at) * stride))
    return lax.ppermute(rows, axis, route)


def coordinate(way):
    axis, stride, count = way
    return ((lax.axis_index(axis) // stride) % count).astype(jnp.int32)


def fold(stacks, lines, way, shared=0, after=()):
    count = 1 if way is None else way[2]
    heights, width = [parts[0].shape[0] for parts in stacks], stacks[0][0].shape[1]
    heights[-1] -= lines
    shares = [height // count for height in heights]
    outs = [((sum(shares) + shared, width), BF16)] * count
    if way is None:
        outs += [((lines, width), F32)] if lines else []
    elif lines > shared:
        outs += [((lines - shared, width), F32)]
    parts = [part for stack in stacks for part in stack]
    if all(share % 16 == 0 for share in shares):
        at = coordinate(way).reshape(1) if way else jnp.zeros((1,), jnp.int32)
        return launch(
            functools.partial(fold_kernel, [len(stack) for stack in stacks], lines, shared, count),
            "fold",
            (1,),
            (at,),
            tuple(parts),
            [fixed(part.shape) for part in parts],
            outs,
            [fixed(shape) for shape, _ in outs],
            [pltpu.VMEM((height, width), BF16) for height in heights] if count > 1 else [],
            micros=2,
            after=after,
        )
    (height,), (share,) = heights, shares
    total = sum(part.astype(F32) for part in parts)
    if way is None:
        return [total[:height].astype(BF16)] + ([total[height:]] if lines else [])
    at = coordinate(way)
    results = [
        jnp.concatenate(
            [
                lax.dynamic_slice_in_dim(total, apart(at, count, turn) * share, share, 0),
                total[height : height + shared],
            ],
            axis=0,
        ).astype(BF16)
        for turn in range(count)
    ]
    return results + ([total[height + shared :]] if lines > shared else [])


def swap(gives, way):
    return [gives[0]] + [exchange(gives[turn], way, turn) for turn in range(1, way[2])]


def fetch(own, way):
    return [own] + [exchange(own, way, turn) for turn in range(1, way[2])]


def spread(parts, way, after=(), carry=()):
    own, count = parts[0], way[2]
    share, width = own.shape
    at = coordinate(way)
    if share % 16 == 0:
        whole, *carry = launch(
            functools.partial(spread_kernel, count),
            "spread",
            (1,),
            (at.reshape(1),),
            tuple(parts),
            [fixed(own.shape)] * count,
            [((share * count, width), BF16)],
            [fixed((share * count, width))],
            micros=2,
            after=after,
            carry=carry,
        )
        return (whole, *carry) if carry else whole
    stack = jnp.stack(parts)
    turns = [at ^ place if count & (count - 1) == 0 else (at - place) % count for place in range(count)]
    whole = jnp.concatenate(
        [lax.dynamic_index_in_dim(stack, turn, 0, False) for turn in turns], axis=0
    )
    return (whole, *carry) if carry else whole


def finish(own, got, width, places, counts, after=()):
    high = (lax.axis_index("dp") % 2).astype(jnp.int32).reshape(1)
    squares = sum(counts)
    return launch(
        functools.partial(finish_kernel, places, counts),
        "finish",
        (1,),
        (high,),
        (own, got),
        [fixed(own.shape)] * 2,
        [((width, width), F32)] * squares,
        [fixed((width, width))] * squares,
        micros=2,
        after=after,
    )


def on_device(
    tokens,
    memory,
    cotangent,
    target_length,
    memory_length,
    expert_of,
    self_norm_gain,
    self_norm_bias,
    self_query,
    self_key,
    self_value,
    self_out,
    self_query_bias,
    self_value_bias,
    self_out_bias,
    cross_norm_gain,
    cross_norm_bias,
    cross_query,
    cross_key,
    cross_value,
    cross_out,
    cross_attention_query_bias,
    cross_value_bias,
    cross_out_bias,
    expert_norm_gain,
    expert_norm_bias,
    expert_in,
    expert_in_bias,
    expert_out,
    expert_out_bias,
):
    seqs, length, width = tokens.shape
    mem_rows = memory.shape[1]
    local_count, _, hidden_width = expert_in.shape
    groups = lax.axis_size("expert")
    places = lax.axis_size("dp")
    own_group = lax.axis_index("expert")
    column = lax.axis_index("dp")

    shifts = list(range(1, groups)) + [0]
    whole = groups == seqs
    rows_shape, square = (length, width), (width, width)
    mem_shape, heads_shape = (mem_rows, width), (HEADS, length)
    turned = (width, length)
    in_smem = pl.BlockSpec(memory_space=pltpu.SMEM)
    lines = [
        self_norm_gain,
        self_norm_bias,
        self_query_bias,
        self_value_bias,
        self_out_bias,
        cross_norm_gain,
        cross_norm_bias,
        cross_attention_query_bias,
        cross_value_bias,
        cross_out_bias,
        expert_norm_gain,
        expert_norm_bias,
    ]
    in_vmem = pl.BlockSpec(memory_space=pltpu.VMEM)
    order, picks, used, slot_of, spot_of, vectors, *grads = pl.pallas_call(
        functools.partial(plan_kernel, shifts, local_count),
        in_specs=[in_smem] * 3 + [in_vmem] * (1 + VECTORS),
        out_specs=[in_smem] * 5 + [in_vmem] * (1 + groups),
        out_shape=[
            struct((seqs + 1,), jnp.int32),
            struct((groups,), jnp.int32),
            struct((groups,), jnp.int32),
            struct((seqs,), jnp.int32),
            struct((groups,), jnp.int32),
            struct((16, width), F32),
        ]
        + [struct(rows_shape, BF16)] * groups,
        compiler_params=pltpu.CompilerParams(vmem_limit_bytes=VMEM_LIMIT),
        name="plan",
    )(
        jnp.stack([own_group, column, jnp.int32(places)]).astype(jnp.int32),
        expert_of,
        target_length,
        cotangent,
        *[line.reshape(1, width) for line in lines],
    )

    def move(rows, slot, back=False):
        shift = shifts[slot]
        if shift == 0:
            return rows
        turn = -shift if back else shift
        return lax.ppermute(rows, "expert", [(g, (g + turn) % groups) for g in range(groups)])

    def arranged(per_slot):
        if whole:
            return per_slot
        stack = jnp.stack(per_slot)
        return [lax.dynamic_index_in_dim(stack, slot_of[at], 0, False) for at in range(seqs)]

    position = lambda shape, start=0: at_position(shape, start, seqs)
    sequence = lambda shape, start=0: at_sequence(shape, start, seqs)
    self_matrices = (self_query, self_key, self_value, self_out)
    cross_matrices = (cross_query, cross_key, cross_value, cross_out)
    half = seqs // 2
    high = (column % 2).astype(jnp.int32).reshape(1)

    saved = [
        (rows_shape, F32),
        (rows_shape, F32),
        (rows_shape, BF16),
        (rows_shape, BF16),
        (rows_shape, BF16),
        (turned, BF16),
        (heads_shape, F32),
        (rows_shape, BF16),
        (mem_shape, BF16),
        (mem_shape, BF16),
        (turned, BF16),
        (heads_shape, F32),
    ]

    def forward(start, steps, kept, after):
        results = launch(
            functools.partial(forward_kernel, start, steps),
            "forward",
            (steps,),
            (order, target_length, memory_length),
            (tokens, memory, vectors) + self_matrices + cross_matrices,
            [sequence(rows_shape, start), sequence(mem_shape, start), fixed(vectors.shape)]
            + [fixed(square)] * 8,
            [(rows_shape, BF16)] * steps + [((seqs,) + shape, kind) for shape, kind in saved],
            [fixed(rows_shape)] * steps + [position(shape, start) for shape, _ in saved],
            [pltpu.VMEM(turned, BF16)],
            micros=0.01,
            after=after,
            into={at + steps: item for at, item in enumerate(kept)},
        )
        return results[:steps], results[steps:]

    grads_in = [move(grads[slot], slot) for slot in range(groups)]
    normed_one, kept = forward(0, half, [], [])
    normed_two, kept = forward(half, seqs - half, kept, [grads_in[0]])
    normed = list(normed_one) + list(normed_two)
    (
        later,
        middle,
        query_one,
        key_one,
        value_one,
        context_one,
        logsum_one,
        query_two,
        key_two,
        value_two,
        context_two,
        logsum_two,
    ) = kept

    if whole:
        rows_in = [move(normed[slot], slot) for slot in range(groups)]
    else:
        joined = jnp.stack(normed)
        rows_in = [
            move(lax.dynamic_index_in_dim(joined, spot_of[slot], 0, False), slot)
            for slot in range(groups)
        ]
    tiles = 4
    tile_width = hidden_width // tiles
    hidden_tile = pl.BlockSpec((length, tile_width), lambda t, *_: (0, t))
    line_tile = pl.BlockSpec((1, tile_width), lambda t, *_: (0, t))
    hidden, grad_pre, made, grad_rows, pre_sum, grads_sum = {}, {}, {}, {}, {}, {}

    def expert(slot, after):
        results = launch(
            functools.partial(expert_kernel, slot),
            "expert",
            (tiles,),
            (picks, used),
            (rows_in[slot], grads_in[slot], expert_in, expert_in_bias, expert_out, expert_out_bias),
            [
                fixed(rows_shape),
                fixed(rows_shape),
                pl.BlockSpec((1, width, tile_width), lambda t, pick, _: (pick[slot], 0, t)),
                pl.BlockSpec((local_count, tile_width), lambda t, *_: (0, t)),
                pl.BlockSpec((1, tile_width, width), lambda t, pick, _: (pick[slot], t, 0)),
                fixed((local_count, width)),
            ],
            [((length, hidden_width), BF16)] * 2
            + [(rows_shape, BF16)] * 2
            + [((1, hidden_width), F32), ((1, width), F32)],
            [hidden_tile, hidden_tile, fixed(rows_shape), fixed(rows_shape), line_tile]
            + [fixed((1, width))],
            [pltpu.VMEM(rows_shape, F32)] * 2,
            micros=0.01,
            after=after,
        )
        for table, result in zip((hidden, grad_pre, made, grad_rows, pre_sum, grads_sum), results):
            table[slot] = result

    back_scratch = [
        pltpu.VMEM((width, mem_rows), BF16),
        pltpu.VMEM(rows_shape, BF16),
        pltpu.VMEM(heads_shape, F32),
        pltpu.VMEM(turned, BF16),
    ]

    def sums_shape(count, final, lines=0):
        if final:
            return [((count * width // 2 + lines, width), BF16)] * 2
        return [((count,) + square, F32)]

    def cross_back(start, steps, grads, given, filled, final, after, carry=(), micros=26):
        first = given is None
        total = sums_shape(5, final)
        return launch(
            functools.partial(cross_back_kernel, start, first, final, steps),
            "cross_back",
            (steps,),
            (order, target_length, memory_length, high),
            tuple(grads)
            + (() if first else tuple(given))
            + (cotangent, memory, later, middle, query_two, key_two, value_two, context_two)
            + (logsum_two, context_one, vectors)
            + cross_matrices,
            [once(rows_shape)] * steps
            + ([] if first else [once((5,) + square), once((8, width))])
            + [
                sequence(rows_shape, start),
                sequence(mem_shape, start),
                position(rows_shape, start),
                position(rows_shape, start),
                position(rows_shape, start),
                position(mem_shape, start),
                position(mem_shape, start),
                position(turned, start),
                position(heads_shape, start),
                position(turned, start),
                fixed(vectors.shape),
            ]
            + [once(square)] * 4,
            [((seqs,) + rows_shape, F32)]
            + [((seqs,) + mem_shape, BF16)] * 2
            + total
            + [((8, width), F32)],
            [position(rows_shape, start), position(mem_shape, start), position(mem_shape, start)]
            + [fixed(shape) for shape, _ in total]
            + [fixed((8, width))],
            [pltpu.VMEM((5,) + square, F32), pltpu.VMEM((8, width), F32), pltpu.VMEM(rows_shape, BF16)]
            + back_scratch,
            micros=micros,
            after=after,
            into={at: item for at, item in enumerate(filled)},
            carry=carry,
        )

    def self_back(start, steps, given, filled, final, after):
        first = given is None
        total = sums_shape(3, final, LINES) if final else sums_shape(3, final) + [((8, width), F32)]
        return launch(
            functools.partial(self_back_kernel, start, first, final),
            "self_back",
            (steps,),
            (order, target_length, high),
            (() if first else tuple(given))
            + (cross_lines, expert_lines)
            + (tokens, grad_middle, query_one, key_one, value_one, context_one, logsum_one, columns)
            + self_matrices,
            ([] if first else [once((3,) + square), once((8, width))])
            + [fixed((8, width)), fixed((EXPERT_LINES, width))]
            + [
                sequence(rows_shape, start),
                position(rows_shape, start),
                position(rows_shape, start),
                position(rows_shape, start),
                position(rows_shape, start),
                position(turned, start),
                position(heads_shape, start),
                fixed(columns.shape),
            ]
            + [once(square)] * 4,
            [((seqs,) + rows_shape, BF16)] * 3 + total,
            [position(rows_shape, start)] * 3 + [fixed(shape) for shape, _ in total],
            [pltpu.VMEM((3,) + square, F32), pltpu.VMEM((8, width), F32)] + back_scratch,
            micros=10 * steps,
            after=after,
            into={at: item for at, item in enumerate(filled)},
        )

    back = {}

    def send_back(slot):
        back[slot] = move(grad_rows[slot], slot, True)

    if whole:
        expert(3, [])
        send_back(3)
        results = cross_back(
            3, 1, [back[3]], None, [], False, grads_in[1:3], micros=0.01
        )
        filled, running = results[:3], results[3:5]
        expert(0, running[1:])
        expert(1, [made[0]])
        expert(2, [made[1]])
        for slot in range(3):
            send_back(slot)
    else:
        for slot in range(groups):
            expert(slot, [])
            send_back(slot)

    in_sums, out_sums, expert_lines = launch(
        functools.partial(expert_weights_kernel, groups),
        "expert_weights",
        (tiles,),
        (picks, used),
        tuple(rows_in)
        + tuple(grads_in)
        + tuple(table[slot] for table in (hidden, grad_pre, pre_sum, grads_sum) for slot in range(groups)),
        [once(rows_shape)] * (2 * groups)
        + [hidden_tile] * (2 * groups)
        + [line_tile] * groups
        + [fixed((1, width))] * groups,
        [
            ((local_count, width, hidden_width), BF16),
            ((local_count, hidden_width, width), BF16),
            ((EXPERT_LINES, width), F32),
        ],
        [
            pl.BlockSpec((local_count, width, tile_width), lambda t, *_: (0, 0, t)),
            pl.BlockSpec((local_count, tile_width, width), lambda t, *_: (0, t, 0)),
            fixed((EXPERT_LINES, width)),
        ],
        [
            pltpu.VMEM((local_count, width, tile_width), F32),
            pltpu.VMEM((local_count, tile_width, width), F32),
            pltpu.VMEM((local_count, 1, tile_width), F32),
            pltpu.VMEM((local_count, 1, width), F32),
        ],
        micros=17,
        after=[back[0]] if whole else [],
    )
    expert_in_grad = lax.psum_scatter(in_sums, "dp", scatter_dimension=1, tiled=True)
    expert_out_grad = lax.psum_scatter(out_sums, "dp", scatter_dimension=1, tiled=True)

    if whole:
        away = [slot for slot in range(groups) if shifts[slot]]
        results = cross_back(
            0, 2, [back[0], back[1]], running, filled, False, [in_sums], [made[slot] for slot in away]
        )
        filled, running = results[:3], results[3:5]
        for at, slot in enumerate(away):
            made[slot] = results[5 + at]
        made_home = [move(made[slot], slot, True) for slot in range(groups)]
        *results, cross_keep, cross_give, cross_lines = cross_back(
            2, 1, [back[2]], running, filled, True, []
        )
    else:
        *results, cross_keep, cross_give, cross_lines = cross_back(
            0, seqs, arranged([back[slot] for slot in range(groups)]), None, [], True, []
        )
        made_home = arranged([move(made[slot], slot, True) for slot in range(groups)])
    grad_middle, grad_key_two, grad_value_two = results

    chips = places // 2
    core, plane, line = ("dp", 1, 2), ("dp", 2, chips), ("expert", 1, groups)
    columns = jnp.concatenate([vectors.T, jnp.zeros((width, 128 - vectors.shape[0]), F32)], axis=1)

    def tokens_back(start, steps, grads, filled, after):
        return launch(
            functools.partial(tokens_back_kernel, start),
            "tokens_back",
            (steps,),
            (order, target_length),
            (tokens, grad_middle, *grads, vectors)
            + self_matrices[:3],
            [sequence(rows_shape, start)]
            + [position(rows_shape, start)] * 4
            + [fixed(vectors.shape)]
            + [once(square)] * 3,
            [((seqs,) + rows_shape, F32)],
            [sequence(rows_shape, start)],
            micros=4 * steps,
            after=after,
            into={at: item for at, item in enumerate(filled)},
        )

    def memory_back(after):
        return launch(
            memory_back_kernel,
            "memory_back",
            (seqs,),
            (order,),
            (grad_key_two, grad_value_two, cross_key, cross_value),
            [position(mem_shape)] * 2 + [once(square)] * 2,
            [((seqs,) + mem_shape, F32)],
            [sequence(mem_shape)],
            micros=5,
            after=after,
        )[0]

    def output_rows(after):
        return launch(
            functools.partial(output_kernel, seqs),
            "output",
            (seqs,),
            (order, target_length),
            (later, *made_home),
            [position(rows_shape)] + [once(rows_shape)] * seqs,
            [((seqs,) + rows_shape, BF16)],
            [sequence(rows_shape)],
            micros=5,
            after=after,
        )[0]

    def casts(items, after):
        return launch(
            cast_kernel,
            "cast",
            (1,),
            (),
            tuple(items),
            [fixed(item.shape) for item in items],
            [(item.shape, F32) for item in items],
            [fixed(item.shape) for item in items],
            micros=3,
            after=after,
        )

    cross_got = exchange(gate(cross_give, made_home[:1]), core, 1)
    memory_grad = memory_back([])
    cross_parts = swap(fold([[cross_keep, cross_got]], 0, plane, after=[memory_grad]), plane)
    *grads_one, weights_run, vectors_run = self_back(
        0, half, None, [], False, [cross_parts[0]]
    )
    cross_line = swap(fold([cross_parts], 0, line, after=grads_one[:1]), line)
    filled = tokens_back(0, half, grads_one, [], [cross_line[0], *made_home[1:2]])
    (cross_share,) = fold([cross_line], 0, None, after=filled)
    cross_fetched = fetch(cross_share, line)
    *grads_one, self_keep, self_give = self_back(
        half,
        seqs - half,
        (weights_run, vectors_run),
        grads_one,
        True,
        [cross_share, *filled],
    )

    cross_rows, self_give = spread(
        cross_fetched, line, after=[self_keep, *made_home[2:3]], carry=[self_give]
    )
    self_got = exchange(self_give, core, 1)
    cross_fetched = fetch(cross_rows, plane)
    expert_in_grad, expert_out_grad = casts([expert_in_grad, expert_out_grad], [cross_rows])

    self_parts = swap(
        fold([[self_keep, self_got]], LINES, plane, LINES, after=[expert_in_grad]), plane
    )
    output = output_rows([self_parts[0]])

    *gives, own_lines = fold([self_parts], LINES, line, SHARED_LINES, after=[output])
    self_line = swap(gives, line)
    cross_rows = spread(cross_fetched, plane, after=[output])
    cross_got = exchange(cross_rows, core, 1)
    filled = tokens_back(half, 1, grads_one, filled, [self_line[0], cross_rows])

    self_share, totals = fold([self_line], SHARED_LINES, None, after=filled)
    self_fetched = fetch(self_share, line)
    (tokens_grad,) = tokens_back(half + 1, seqs - half - 1, grads_one, filled, [self_share])

    self_rows = spread(self_fetched, line, after=[tokens_grad])
    self_fetched = fetch(self_rows, plane)
    cross_q, cross_k, cross_v, cross_o, self_o = finish(
        cross_rows, cross_got, width, 1, [5], [self_rows]
    )
    self_rows = spread(self_fetched, plane, after=[cross_q])
    self_q, self_k, self_v = finish(self_rows, exchange(self_rows, core, 1), width, 1, [3])

    in_count = local_count * hidden_width // width
    in_bias = own_lines[:in_count].reshape(local_count, hidden_width)
    out_bias = own_lines[in_count : in_count + local_count]
    in_share, out_share = hidden_width // places, width // places
    return (
        output,
        tokens_grad,
        memory_grad,
        totals[2],
        totals[3],
        self_q,
        self_k,
        self_v,
        self_o,
        totals[0],
        totals[1],
        totals[15],
        totals[13],
        totals[14],
        cross_q,
        cross_k,
        cross_v,
        cross_o,
        totals[12],
        totals[11],
        totals[10],
        totals[8],
        totals[9],
        expert_in_grad,
        lax.dynamic_slice_in_dim(in_bias, column * in_share, in_share, 1),
        expert_out_grad,
        lax.dynamic_slice_in_dim(out_bias, column * out_share, out_share, 1),
    )


def solution(mesh):
    rows = P(("expert", "dp"), None, None)
    counts = P(("expert", "dp"))
    split = (P("expert", None, None), P("expert", None)) * 2
    shares = (P("expert", "dp", None), P("expert", "dp")) * 2
    return jax.shard_map(
        on_device,
        mesh=mesh,
        in_specs=(rows,) * 3 + (counts,) * 2 + (P(),) * 21 + split,
        out_specs=(rows,) * 3 + (P(),) * 20 + shares,
        check_vma=False,
    )
```

```python
import functools

import jax
import jax.numpy as jnp
from jax import lax
from jax.experimental import pallas as pl
from jax.experimental.pallas import tpu as pltpu
from jax.sharding import PartitionSpec as P

HEADS = 8
HEAD_DIM = 64
PAIR = 2 * HEAD_DIM
EPSILON = 1e-05
SCORE_SCALE = 0.125
NEGATIVE = -1e30
SAFE_SCORE = 80.0
SHARED_LINES = 16
EXPERT_LINES = 16
VECTORS = 12
LINES = SHARED_LINES + EXPERT_LINES
LOG2E = 1.4426950408889634
LN2 = 0.6931471805599453
VMEM_LIMIT = 64 * 1024 * 1024
F32 = jnp.float32
BF16 = jnp.bfloat16


def contract(left, right, left_dim, right_dim):
    return lax.dot_general(
        left, right, (((left_dim,), (right_dim,)), ((), ())), preferred_element_type=F32
    )


def nn(left, right):
    return contract(left, right, 1, 0)


def nt(left, right):
    return contract(left, right, 1, 1)


def tn(left, right):
    return contract(left, right, 0, 0)


def normalise(rows):
    centre = rows - jnp.mean(rows, axis=-1, keepdims=True)
    inverse = lax.rsqrt(jnp.mean(centre * centre, axis=-1, keepdims=True) + EPSILON)
    return centre * inverse, inverse


def normalise_back(grad, normed, inverse, gain):
    scaled = grad * gain
    return inverse * (
        scaled
        - jnp.mean(scaled, axis=-1, keepdims=True)
        - normed * jnp.mean(scaled * normed, axis=-1, keepdims=True)
    )


def column_sum(rows):
    return jnp.sum(rows.astype(F32), axis=0, keepdims=True)


def head_masks():
    lane = lax.broadcasted_iota(jnp.int32, (1, PAIR), 1)
    mine = [(lane // HEAD_DIM == half).astype(F32).astype(BF16) for half in (0, 1)]
    spare = [(lane == HEAD_DIM * (1 - half)).astype(F32).astype(BF16) for half in (0, 1)]
    return mine, spare


def key_bias(count, mem_rows):
    place = lax.broadcasted_iota(jnp.int32, (mem_rows, PAIR), 0)
    return jnp.where(place < count, 0.0, NEGATIVE).astype(BF16)


def score_operands(keys, queries, half, mine, spare, bias):
    picked = queries * mine[half]
    if bias is None:
        return keys, picked
    return keys * (1 - spare[half]) + bias * spare[half], picked + spare[half]


def causal(scores, block):
    key_at = lax.broadcasted_iota(jnp.int32, (scores.shape[0], block), 0)
    query_at = lax.broadcasted_iota(jnp.int32, (scores.shape[0], block), 1)
    return jnp.where(key_at <= query_at, scores, NEGATIVE)


def lower(items, block):
    return jnp.concatenate([item[block:] for item in items], axis=0)


def lower_columns(items, block):
    return jnp.concatenate([item[:, block:] for item in items], axis=1)


def span(start, size):
    return slice(start, start + size) if isinstance(start, int) else pl.ds(pl.multiple_of(start, size), size)


def head_rows(pair, half):
    return span(pair * PAIR + half * HEAD_DIM, HEAD_DIM)


def pair_span(pair):
    return span(pair * PAIR, PAIR)


def each_pair(pair_step, unrolled):
    if unrolled:
        for pair in range(HEADS // 2):
            pair_step(pair, 0)
    else:
        lax.fori_loop(0, HEADS // 2, pair_step, 0)


def head_part(both, half, block):
    return both[half * HEAD_DIM : (half + 1) * HEAD_DIM, half * block : (half + 1) * block]


def causal_pair_scores(keys, picked, block):
    upper = []
    for half in (0, 1):
        scores = nt(keys[:block], picked[half])
        upper.append(
            jnp.concatenate([causal(scores[:, :block], block), scores[:, block:]], axis=1)
        )
    scores = nt(keys[block:], lower(picked, block))
    low = jnp.concatenate([causal(scores[:, :block], block), causal(scores[:, block:], block)], axis=1)
    return upper, low


def head_blocks():
    feature = lax.broadcasted_iota(jnp.int32, (HEADS * HEAD_DIM, 128), 0)
    return (feature // HEAD_DIM == lax.broadcasted_iota(jnp.int32, (HEADS * HEAD_DIM, 128), 1)).astype(BF16)


def scores_small(query_ref, key_ref):
    blocks = head_blocks()
    squares = [nn(ref[...] * ref[...], blocks) for ref in (query_ref, key_ref)]
    most = [jnp.max(item, axis=0, keepdims=True) for item in squares]
    return jnp.max(most[0] * most[1]) < SAFE_SCORE * SAFE_SCORE


def attend_cross(plain, query_ref, key_ref, value_t_ref, context_t_ref, logsum_ref, bias):
    mine, spare = head_masks()

    def pair_step(pair, carry):
        columns = pair_span(pair)
        keys, queries = key_ref[:, columns], query_ref[:, columns]
        for half in (0, 1):
            rows = head_rows(pair, half)
            left, right = score_operands(keys, queries, half, mine, spare, bias)
            scores = nt(left, right)
            highest = 0.0 if plain else jnp.max(scores, axis=0, keepdims=True)
            raised = jnp.exp2(scores if plain else scores - highest)
            summed = jnp.sum(raised, axis=0, keepdims=True)
            context = nn(value_t_ref[rows, :], raised.astype(BF16))
            context_t_ref[rows, :] = (context * (1.0 / summed)).astype(BF16)
            logsum_ref[pl.ds(2 * pair + half, 1), :] = highest + LOG2E * jnp.log(summed)
        return carry

    each_pair(pair_step, plain)


def attend_self(plain, query_ref, key_ref, value_t_ref, context_t_ref, logsum_ref):
    block = query_ref.shape[0] // 2
    mine, _ = head_masks()

    def pair_step(pair, carry):
        columns = pair_span(pair)
        keys, queries = key_ref[:, columns], query_ref[:, columns]
        upper, low = causal_pair_scores(keys, [queries * mine[0], queries * mine[1]], block)
        if plain:
            highest = [0.0, 0.0]
            low = jnp.exp2(low)
        else:
            low_top = jnp.max(low, axis=0, keepdims=True)
            highest = []
            for half in (0, 1):
                top = jnp.max(upper[half], axis=0, keepdims=True)
                other = low_top[:, half * block : (half + 1) * block]
                highest.append(
                    jnp.concatenate([top[:, :block], jnp.maximum(top[:, block:], other)], axis=1)
                )
            low = jnp.exp2(low - lower_columns(highest, block))
        low_sum = jnp.sum(low, axis=0, keepdims=True)
        low_context = nn(value_t_ref[columns, block:], low.astype(BF16))
        for half in (0, 1):
            rows = head_rows(pair, half)
            raised = jnp.exp2(upper[half] if plain else upper[half] - highest[half])
            summed = jnp.sum(raised, axis=0, keepdims=True)
            part = low_sum[:, half * block : (half + 1) * block]
            summed = jnp.concatenate([summed[:, :block], summed[:, block:] + part], axis=1)
            context = nn(value_t_ref[rows, :block], raised.astype(BF16))
            context = jnp.concatenate(
                [context[:, :block], context[:, block:] + head_part(low_context, half, block)],
                axis=1,
            )
            context_t_ref[rows, :] = (context * (1.0 / summed)).astype(BF16)
            logsum_ref[pl.ds(2 * pair + half, 1), :] = highest[half] + LOG2E * jnp.log(summed)
        return carry

    each_pair(pair_step, plain)


def attend(kind, query_ref, key_ref, *refs):
    small = scores_small(query_ref, key_ref)

    @pl.when(small)
    def _():
        kind(True, query_ref, key_ref, *refs)

    @pl.when(jnp.logical_not(small))
    def _():
        kind(False, query_ref, key_ref, *refs)


def attend_cross_back(
    query_ref,
    key_ref,
    value_ref,
    key_t_ref,
    grad_ref,
    delta_ref,
    logsum_ref,
    grad_query_t_ref,
    grad_key_ref,
    grad_value_ref,
    bias,
):
    mine, spare = head_masks()

    def pair_step(pair, carry):
        columns = pair_span(pair)
        keys, queries, values = key_ref[:, columns], query_ref[:, columns], value_ref[:, columns]
        grads = grad_ref[:, columns]
        chances, slopes, picked_grads, picked_queries = [], [], [], []
        for half in (0, 1):
            head, rows = pl.ds(2 * pair + half, 1), head_rows(pair, half)
            left, right = score_operands(keys, queries, half, mine, spare, bias)
            picked_grads.append(grads * mine[half])
            picked_queries.append(queries * mine[half])
            chance = jnp.exp2(nt(left, right) - logsum_ref[head, :])
            slope = chance * (nt(values, picked_grads[half]) - delta_ref[head, :])
            chances.append(chance.astype(BF16))
            slopes.append(slope.astype(BF16))
            grad_query_t_ref[rows, :] = (nn(key_t_ref[rows, :], slopes[half]) * SCORE_SCALE).astype(
                BF16
            )
        grad_value_ref[:, columns] = nn(
            jnp.concatenate(chances, axis=1), jnp.concatenate(picked_grads, axis=0)
        ).astype(BF16)
        grad_key_ref[:, columns] = (
            nn(jnp.concatenate(slopes, axis=1), jnp.concatenate(picked_queries, axis=0)) * LN2
        ).astype(BF16)
        return carry

    each_pair(pair_step, True)


def attend_self_back(
    query_ref,
    key_ref,
    value_ref,
    key_t_ref,
    grad_ref,
    delta_ref,
    logsum_ref,
    grad_query_t_ref,
    grad_key_ref,
    grad_value_ref,
):
    block = query_ref.shape[0] // 2
    mine, _ = head_masks()

    def pair_step(pair, carry):
        columns = pair_span(pair)
        keys, queries, values = key_ref[:, columns], query_ref[:, columns], value_ref[:, columns]
        grads = grad_ref[:, columns]
        picked = [queries * mine[0], queries * mine[1]]
        picked_grads = [grads * mine[0], grads * mine[1]]
        upper, low = causal_pair_scores(keys, picked, block)
        logsum = [logsum_ref[pl.ds(2 * pair + half, 1), :] for half in (0, 1)]
        delta = [delta_ref[pl.ds(2 * pair + half, 1), :] for half in (0, 1)]
        low_grads = lower(picked_grads, block)
        low = jnp.exp2(low - lower_columns(logsum, block))
        low_slope = (
            low * (nt(values[block:], low_grads) - lower_columns(delta, block))
        ).astype(BF16)
        low_query = nn(key_t_ref[columns, block:], low_slope)
        chances, slopes = [], []
        for half in (0, 1):
            chance = jnp.exp2(upper[half] - logsum[half])
            slope = chance * (nt(values[:block], picked_grads[half]) - delta[half])
            chances.append(chance.astype(BF16))
            slopes.append(slope.astype(BF16))
            rows = head_rows(pair, half)
            grad = nn(key_t_ref[rows, :block], slopes[half])
            grad = jnp.concatenate(
                [grad[:, :block], grad[:, block:] + head_part(low_query, half, block)], axis=1
            )
            grad_query_t_ref[rows, :] = (grad * SCORE_SCALE).astype(BF16)
        grad_value_ref[:block, columns] = nn(
            jnp.concatenate(chances, axis=1), jnp.concatenate(picked_grads, axis=0)
        ).astype(BF16)
        grad_value_ref[block:, columns] = nn(low.astype(BF16), low_grads).astype(BF16)
        grad_key_ref[:block, columns] = (
            nn(jnp.concatenate(slopes, axis=1), jnp.concatenate(picked, axis=0)) * LN2
        ).astype(BF16)
        grad_key_ref[block:, columns] = (nn(low_slope, lower(picked, block)) * LN2).astype(BF16)
        return carry

    each_pair(pair_step, True)


def head_sums(grad, context_t):
    product = grad.T.astype(F32) * context_t.astype(F32)
    return jnp.sum(product.reshape(HEADS, HEAD_DIM, product.shape[1]), axis=1)


def valid_rows_of(count, length):
    return (lax.broadcasted_iota(jnp.int32, (length, 1), 0) < count).astype(F32)


def forward_kernel(
    start_at,
    steps,
    order_ref,
    target_ref,
    memory_length_ref,
    tokens_ref,
    memory_ref,
    vectors_ref,
    self_query,
    self_key,
    self_value,
    self_out,
    cross_query,
    cross_key,
    cross_value,
    cross_out,
    *refs,
):
    normed_refs, refs = refs[:steps], refs[steps:]
    (
    later_ref,
    middle_ref,
    query_one_ref,
    key_one_ref,
    value_one_ref,
    context_one_ref,
    logsum_one_ref,
    query_two_ref,
    key_two_ref,
    value_two_ref,
    context_two_ref,
    logsum_two_ref,
    value_t_ref,
    ) = refs
    step = pl.program_id(0)
    sequence = order_ref[start_at + step]
    length = tokens_ref.shape[1]
    vector = lambda at: vectors_ref[at : at + 1, :]
    start = tokens_ref[0].astype(F32) * valid_rows_of(target_ref[sequence], length)
    normed = (normalise(start)[0] * vector(0) + vector(1)).astype(BF16)
    scale = SCORE_SCALE * LOG2E
    query_one_ref[0] = ((nn(normed, self_query[...]) + vector(2)) * scale).astype(BF16)
    key_one_ref[0] = nn(normed, self_key[...]).astype(BF16)
    value = (nn(normed, self_value[...]) + vector(3)).astype(BF16)
    value_one_ref[0] = value
    value_t_ref[...] = value.T
    attend(
        attend_self,
        query_one_ref.at[0],
        key_one_ref.at[0],
        value_t_ref,
        context_one_ref.at[0],
        logsum_one_ref.at[0],
    )
    middle = start + tn(context_one_ref[0], self_out[...]) + vector(4)
    middle_ref[0] = middle
    normed = (normalise(middle)[0] * vector(5) + vector(6)).astype(BF16)
    memory = memory_ref[0]
    query_two_ref[0] = ((nn(normed, cross_query[...]) + vector(7)) * scale).astype(BF16)
    key_two_ref[0] = nn(memory, cross_key[...]).astype(BF16)
    value = (nn(memory, cross_value[...]) + vector(8)).astype(BF16)
    value_two_ref[0] = value
    value_t_ref[...] = value.T
    attend(
        attend_cross,
        query_two_ref.at[0],
        key_two_ref.at[0],
        value_t_ref,
        context_two_ref.at[0],
        logsum_two_ref.at[0],
        key_bias(memory_length_ref[sequence], memory.shape[0]),
    )
    later = middle_ref[0] + tn(context_two_ref[0], cross_out[...]) + vector(9)
    later_ref[0] = later
    normed = (normalise(later)[0] * vector(10) + vector(11)).astype(BF16)
    for at in range(steps):

        @pl.when(step == at)
        def _():
            normed_refs[at][...] = normed


def expert_kernel(
    slot,
    pick_ref,
    used_ref,
    rows_ref,
    grads_ref,
    weight_in,
    bias_in,
    weight_out,
    bias_out,
    hidden_ref,
    grad_pre_ref,
    made_ref,
    grad_rows_ref,
    pre_sum_ref,
    grads_sum_ref,
    made_sum,
    grad_sum,
):
    tile = pl.program_id(0)
    last = pl.num_programs(0) - 1
    used = used_ref[slot] > 0
    pick = pl.ds(pick_ref[slot], 1)

    @pl.when(used)
    def _():
        pre = nn(rows_ref[...], weight_in[0]) + bias_in[pick, :]
        grad_hidden = nt(grads_ref[...], weight_out[0])
        gate = 0.5 * jnp.tanh(0.5 * pre) + 0.5
        active = pre * gate
        hidden = active.astype(BF16)
        hidden_ref[...] = hidden
        grad_pre = grad_hidden * (gate + active * (1.0 - gate))
        pre_sum_ref[...] = jnp.sum(grad_pre, axis=0, keepdims=True)
        grad_pre = grad_pre.astype(BF16)
        grad_pre_ref[...] = grad_pre
        made = nn(hidden, weight_out[0])
        grad_rows = nt(grad_pre, weight_in[0])

        @pl.when(tile == 0)
        def _():
            made_sum[...] = made
            grad_sum[...] = grad_rows
            grads_sum_ref[...] = column_sum(grads_ref[...])

        @pl.when(tile > 0)
        def _():
            made_sum[...] += made
            grad_sum[...] += grad_rows

        @pl.when(tile == last)
        def _():
            made_ref[...] = (made_sum[...] + bias_out[pick, :]).astype(BF16)
            grad_rows_ref[...] = grad_sum[...].astype(BF16)

    @pl.when(jnp.logical_not(used))
    def _():
        for ref in (hidden_ref, grad_pre_ref, made_ref, grad_rows_ref, pre_sum_ref, grads_sum_ref):
            ref[...] = jnp.zeros_like(ref)


def expert_weights_kernel(slots, pick_ref, used_ref, *refs):
    rows, grads, hidden, grad_pre, pre_sum, grads_sum = [
        refs[at * slots : (at + 1) * slots] for at in range(6)
    ]
    in_ref, out_ref, lines_ref, in_sum, out_sum, in_bias, out_bias = refs[6 * slots :]
    for total in (in_sum, out_sum, in_bias, out_bias):
        total[...] = jnp.zeros_like(total)
    for slot in range(slots):

        @pl.when(used_ref[slot] > 0)
        def _():
            pick = pick_ref[slot]
            in_sum[pick] += tn(rows[slot][...], grad_pre[slot][...])
            out_sum[pick] += tn(hidden[slot][...], grads[slot][...])
            in_bias[pick] += pre_sum[slot][...]
            out_bias[pick] += grads_sum[slot][...]

    in_ref[...] = in_sum[...].astype(BF16)
    out_ref[...] = out_sum[...].astype(BF16)
    tile, tiles = pl.program_id(0), pl.num_programs(0)
    count = in_bias.shape[0]

    @pl.when(tile == 0)
    def _():
        lines_ref[...] = jnp.zeros_like(lines_ref)

    for pick in range(count):
        lines_ref[pl.ds(pick * tiles + tile, 1), :] = in_bias[pick]
        lines_ref[pl.ds(count * tiles + pick, 1), :] = out_bias[pick]


def plan_kernel(
    shifts,
    local_count,
    place_ref,
    expert_ref,
    target_ref,
    cotangent_ref,
    *refs,
):
    lines, refs = refs[:VECTORS], refs[VECTORS:]
    order_ref, pick_ref, used_ref, slot_ref, spot_ref, vectors_ref, *grads_refs = refs
    vectors_ref[...] = jnp.zeros_like(vectors_ref)
    for at, line in enumerate(lines):
        vectors_ref[at : at + 1, :] = line[...]

    groups, seqs = len(shifts), cotangent_ref.shape[0]
    own, column, places = place_ref[0], place_ref[1], place_ref[2]
    own_ids = [expert_ref[(own * places + column) * seqs + at] for at in range(seqs)]
    distance = [lax.rem(lax.div(item, local_count) - own + groups, groups) for item in own_ids]
    slots = [
        sum((jnp.where(item == shift, at, 0) for at, shift in enumerate(shifts)), jnp.int32(0))
        for item in distance
    ]
    for slot in range(groups):
        spot_ref[slot] = 0
        source = lax.rem(own - shifts[slot] + groups, groups)
        pick, used = jnp.int32(0), jnp.int32(0)
        for at in range(seqs):
            item = expert_ref[(source * places + column) * seqs + at]
            here = lax.div(item, local_count) == own
            pick = jnp.where(here, lax.rem(item, local_count), pick)
            used = jnp.where(here, 1, used)
        pick_ref[slot] = pick
        used_ref[slot] = used
    for at in range(seqs):
        spot = sum((jnp.where(other < slots[at], 1, 0) for other in slots), jnp.int32(0))
        order_ref[spot] = at
        slot_ref[spot] = slots[at]
        spot_ref[slots[at]] = spot
    order_ref[seqs] = order_ref[0]
    length = cotangent_ref.shape[1]
    for slot in range(groups):
        sequence = order_ref[spot_ref[slot]]
        valid = valid_rows_of(target_ref[sequence], length)
        grads_refs[slot][...] = (cotangent_ref[sequence].astype(F32) * valid).astype(BF16)


def output_kernel(slots, order_ref, target_ref, later_ref, *refs):
    made, output_ref = refs[:slots], refs[slots]
    position = pl.program_id(0)
    valid = valid_rows_of(target_ref[order_ref[position]], later_ref.shape[1])
    for at in range(slots):

        @pl.when(position == at)
        def _():
            output_ref[0] = ((later_ref[0] + made[at][...].astype(F32)) * valid).astype(BF16)


def open_sums(first, weight_sum, vector_sum, given):
    @pl.when(pl.program_id(0) == 0)
    def _():
        if first:
            weight_sum[...] = jnp.zeros_like(weight_sum)
            vector_sum[...] = jnp.zeros_like(vector_sum)
        else:
            weight_sum[...] = given[0][...].astype(F32)
            vector_sum[...] = given[1][...]


def put_halves(squares, lines, high, keep_ref, give_ref):
    height = squares[0].shape[0]
    half = height * len(squares) // 2
    for top, (low_ref, high_ref) in ((0, (keep_ref, give_ref)), (1, (give_ref, keep_ref))):

        @pl.when(high == top)
        def _():
            for at, square in enumerate(squares):
                for part, ref in enumerate((low_ref, high_ref)):
                    start, stop = max(at * height, part * half), min((at + 1) * height, (part + 1) * half)
                    if start < stop:
                        rows = square[start - at * height : stop - at * height]
                        ref[start - part * half : stop - part * half] = rows.astype(BF16)

    if lines is not None:
        keep_ref[half:] = lines.astype(BF16)
        give_ref[half:] = lines.astype(BF16)


def close_sums(final, weight_sum, vector_sum, high, outs):
    @pl.when(pl.program_id(0) == pl.num_programs(0) - 1)
    def _():
        outs[-1][...] = vector_sum[...]
        if final:
            squares = [weight_sum[0].T] + [weight_sum[at] for at in range(1, weight_sum.shape[0])]
            put_halves(squares, None, high, outs[0], outs[1])
        else:
            outs[0][...] = weight_sum[...].astype(BF16)


def cross_back_kernel(
    start_at, first, final, slots, order_ref, target_ref, memory_length_ref, high_ref, *refs
):
    grad_normed, refs = refs[:slots], refs[slots:]
    given, refs = (None, refs) if first else (refs[:2], refs[2:])
    (
        cotangent_ref,
        memory_ref,
        later_ref,
        middle_ref,
        query_ref,
        key_ref,
        value_ref,
        context_ref,
        logsum_ref,
        context_one_ref,
        vectors_ref,
        cross_query,
        cross_key,
        cross_value,
        cross_out,
        grad_middle_ref,
        grad_key_ref,
        grad_value_ref,
        *outs,
        weight_sum,
        vector_sum,
        grad_expert,
        key_t,
        grad_context,
        delta,
        grad_query_t,
    ) = refs
    step = pl.program_id(0)
    sequence = order_ref[lax.rem(start_at + step, order_ref.shape[0] - 1)]
    length = cotangent_ref.shape[1]
    vector = lambda at: vectors_ref[at : at + 1, :]
    open_sums(first, weight_sum, vector_sum, given)

    for at in range(slots):

        @pl.when(step == at)
        def _():
            grad_expert[...] = grad_normed[at][...]

    def add_vector(at, value):
        vector_sum[at : at + 1, :] += value

    valid = valid_rows_of(target_ref[sequence], length)
    normed, inverse = normalise(later_ref[0])
    grad = grad_expert[...].astype(F32)
    add_vector(0, column_sum(grad * normed))
    add_vector(1, column_sum(grad))
    grad_later = cotangent_ref[0].astype(F32) * valid + normalise_back(
        grad, normed, inverse, vector(10)
    )
    branch = grad_later.astype(BF16)
    grad_middle_ref[0] = grad_later
    add_vector(2, column_sum(branch))
    weight_sum[3] += nn(context_ref[0], branch)
    context_grad = nt(branch, cross_out[...]).astype(BF16)
    grad_context[...] = context_grad
    delta[...] = head_sums(context_grad, context_ref[0])
    key_t[...] = key_ref[0].T
    attend_cross_back(
        query_ref.at[0],
        key_ref.at[0],
        value_ref.at[0],
        key_t,
        grad_context,
        delta,
        logsum_ref.at[0],
        grad_query_t,
        grad_key_ref.at[0],
        grad_value_ref.at[0],
        key_bias(memory_length_ref[sequence], memory_ref.shape[1]),
    )
    memory_t = memory_ref[0].T
    weight_sum[1] += nn(memory_t, grad_key_ref[0])
    weight_sum[2] += nn(memory_t, grad_value_ref[0])
    add_vector(3, column_sum(grad_value_ref[0]))
    normed, inverse = normalise(middle_ref[0])
    weight_sum[0] += nn(grad_query_t[...], (normed * vector(5) + vector(6)).astype(BF16))
    grad_query = grad_query_t[...].T
    add_vector(4, column_sum(grad_query))
    grad = nt(grad_query, cross_query[...])
    add_vector(5, column_sum(grad * normed))
    add_vector(6, column_sum(grad))
    grad_middle = grad_middle_ref[0] + normalise_back(grad, normed, inverse, vector(5))
    grad_middle_ref[0] = grad_middle
    branch = grad_middle.astype(BF16)
    add_vector(7, column_sum(branch))
    weight_sum[4] += nn(context_one_ref[0], branch)
    close_sums(final, weight_sum, vector_sum, high_ref[0], outs)


def self_back_kernel(start_at, first, final, order_ref, target_ref, high_ref, *refs):
    given, refs = (None, refs) if first else (refs[:2], refs[2:])
    cross_lines_ref, expert_lines_ref = refs[:2]
    refs = refs[2:]
    (
        tokens_ref,
        grad_middle_ref,
        query_ref,
        key_ref,
        value_ref,
        context_ref,
        logsum_ref,
        columns_ref,
        self_query,
        self_key,
        self_value,
        self_out,
        grad_query_ref,
        grad_key_ref,
        grad_value_ref,
        first_ref,
        second_ref,
        weight_sum,
        vector_sum,
        key_t,
        grad_context,
        delta,
        grad_query_t,
    ) = refs
    step = pl.program_id(0)
    sequence = order_ref[lax.rem(start_at + step, order_ref.shape[0] - 1)]
    length = tokens_ref.shape[1]
    open_sums(first, weight_sum, vector_sum, given)

    valid = valid_rows_of(target_ref[sequence], length)
    context_grad = nt(grad_middle_ref[0].astype(BF16), self_out[...]).astype(BF16)
    grad_context[...] = context_grad
    delta[...] = head_sums(context_grad, context_ref[0])
    key_t[...] = key_ref[0].T
    attend_self_back(
        query_ref.at[0],
        key_ref.at[0],
        value_ref.at[0],
        key_t,
        grad_context,
        delta,
        logsum_ref.at[0],
        grad_query_t,
        grad_key_ref.at[0],
        grad_value_ref.at[0],
    )
    normed = normalise(tokens_ref[0].astype(F32) * valid)[0].astype(BF16)
    normed_t = normed.T
    weight_sum[0] += nn(grad_query_t[...], normed)
    weight_sum[1] += nn(normed_t, grad_key_ref[0])
    weight_sum[2] += nn(normed_t, grad_value_ref[0])
    grad_query = grad_query_t[...].T
    grad_query_ref[0] = grad_query
    for at, item in enumerate((grad_query, grad_key_ref[0], grad_value_ref[0])):
        vector_sum[at : at + 1, :] += column_sum(item)

    @pl.when(step == pl.num_programs(0) - 1)
    def _():
        if not final:
            first_ref[...] = weight_sum[...].astype(BF16)
            second_ref[...] = vector_sum[...]
            return
        width = weight_sum.shape[1]
        gain, shift = columns_ref[:, 0:1], columns_ref[:, 1:2]
        gain_grad = jnp.zeros((width, 1), F32)
        shift_grad = jnp.zeros((width, 1), F32)
        squares = []
        for at, matrix in enumerate((self_query, self_key, self_value)):
            total = weight_sum[at].T if at == 0 else weight_sum[at]
            column = vector_sum[at : at + 1, :]
            weights = matrix[...].astype(F32)
            gain_grad += jnp.sum(weights * total, axis=1, keepdims=True)
            shift_grad += jnp.sum(weights * column, axis=1, keepdims=True)
            squares.append((total * gain + shift * column).astype(BF16))
        lane = lax.broadcasted_iota(jnp.int32, (width, 128), 1)
        both = jnp.where(lane == 0, gain_grad, jnp.where(lane == 1, shift_grad, 0.0)).T
        lines = jnp.concatenate(
            [
                vector_sum[0:1, :],
                vector_sum[2:3, :],
                both[0:2, :],
                jnp.zeros((4, width), F32),
                cross_lines_ref[...],
                expert_lines_ref[...],
            ],
            axis=0,
        )
        put_halves(squares, lines, high_ref[0], first_ref, second_ref)


def tokens_back_kernel(
    start_at,
    order_ref,
    target_ref,
    tokens_ref,
    grad_middle_ref,
    grad_query_ref,
    grad_key_ref,
    grad_value_ref,
    vectors_ref,
    self_query,
    self_key,
    self_value,
    tokens_grad_ref,
):
    sequence = order_ref[lax.rem(start_at + pl.program_id(0), order_ref.shape[0] - 1)]
    valid = valid_rows_of(target_ref[sequence], tokens_ref.shape[1])
    normed, inverse = normalise(tokens_ref[0].astype(F32) * valid)
    grad = (
        nt(grad_query_ref[0], self_query[...])
        + nt(grad_key_ref[0], self_key[...])
        + nt(grad_value_ref[0], self_value[...])
    )
    tokens_grad_ref[0] = (
        grad_middle_ref[0] + normalise_back(grad, normed, inverse, vectors_ref[0:1, :])
    ) * valid


def memory_back_kernel(order_ref, grad_key_ref, grad_value_ref, cross_key, cross_value, memory_grad_ref):
    memory_grad_ref[0] = nt(grad_key_ref[0], cross_key[...]) + nt(
        grad_value_ref[0], cross_value[...]
    )


def apart(at, count, turn):
    return at ^ turn if count & (count - 1) == 0 else lax.rem(at + turn, count)


def heard(at, count, turn):
    return at ^ turn if count & (count - 1) == 0 else lax.rem(at + count - turn, count)


def fold_kernel(sizes, lines, shared, count, at_ref, *refs):
    items = sum(sizes)
    parts, outs = refs[:items], refs[items:]
    totals = []
    for size in sizes:
        total = parts[0][...].astype(F32)
        for part in parts[1:size]:
            total = total + part[...].astype(F32)
        totals.append(total)
        parts = parts[size:]
    heights = [total.shape[0] for total in totals]
    heights[-1] -= lines
    if count == 1:
        outs[0][...] = totals[0][: heights[0]].astype(BF16)
        if lines:
            outs[1][...] = totals[0][heights[0] :]
        return
    at, stacks, start = at_ref[0], refs[-len(sizes) :], 0
    for total, height, stack in zip(totals, heights, stacks):
        share = height // count
        stack[...] = total[:height].astype(BF16)
        for turn in range(count):
            which = pl.multiple_of(apart(at, count, turn) * share, 16)
            outs[turn][start : start + share] = stack[pl.ds(which, share), :]
        start += share
    last = heights[-1]
    if shared:
        for turn in range(count):
            outs[turn][start:] = totals[-1][last : last + shared].astype(BF16)
    if lines > shared:
        outs[count][...] = totals[-1][last + shared :]


def spread_kernel(count, at_ref, *refs):
    parts, out = refs[:count], refs[count]
    share = parts[0].shape[0]
    for turn in range(count):
        place = pl.multiple_of(heard(at_ref[0], count, turn) * share, 16)
        out[pl.ds(place, share), :] = parts[turn][...]


def finish_kernel(places, counts, high_ref, own_ref, got_ref, *outs):
    own, got = own_ref[...].astype(F32), got_ref[...].astype(F32)
    top = high_ref[0] > 0
    halves = [jnp.where(top, got, own), jnp.where(top, own, got)]
    height = outs[0].shape[0]
    shares = [height * count // (2 * places) for count in counts]
    block = sum(shares)
    for half in (0, 1):
        for place in range(places):
            source, first = place * block, 0
            for count, share in zip(counts, shares):
                row, left = (half * places + place) * share, share
                while left:
                    at, inside = divmod(row, height)
                    size = min(left, height - inside)
                    outs[first + at][inside : inside + size] = halves[half][source : source + size]
                    row, source, left = row + size, source + size, left - size
                first += count


def cast_kernel(*refs):
    count = len(refs) // 2
    for source, out in zip(refs[:count], refs[count:]):
        out[...] = source[...].astype(F32)


def fixed(shape):
    return pl.BlockSpec(shape, lambda *_: (0,) * len(shape))


def once(shape):
    return pl.BlockSpec(shape, lambda *_: (0,) * len(shape), pipeline_mode=pl.Buffered(1))


def at_position(shape, start, count):
    return pl.BlockSpec(
        (1,) + shape, lambda step, *_: (lax.rem(start + step, count),) + (0,) * len(shape)
    )


def at_sequence(shape, start, count):
    return pl.BlockSpec(
        (1,) + shape,
        lambda step, order, *_: (order[lax.rem(start + step, count)],) + (0,) * len(shape),
    )


def struct(shape, kind):
    return jax.ShapeDtypeStruct(shape, kind)


def launch(
    kernel,
    name,
    grid,
    scalars,
    inputs,
    in_specs,
    outs,
    out_specs,
    scratch=(),
    micros=10,
    after=(),
    into=None,
    carry=(),
):
    into = into or {}
    extra = list(after) + list(into.values()) + list(carry)
    lead, made = len(scalars) + len(inputs), len(outs)
    anywhere = pl.BlockSpec(memory_space=pl.ANY)

    def body(*refs):
        rest = refs[lead + len(extra) :]
        kernel(*refs[:lead], *rest[:made], *rest[made + len(carry) :])

    aliases = {lead + len(after) + at: out for at, out in enumerate(into)}
    first = lead + len(after) + len(into)
    aliases.update({first + at: made + at for at in range(len(carry))})
    return pl.pallas_call(
        body,
        grid_spec=pltpu.PrefetchScalarGridSpec(
            num_scalar_prefetch=len(scalars),
            grid=grid,
            in_specs=list(in_specs) + [anywhere] * len(extra),
            out_specs=list(out_specs) + [anywhere] * len(carry),
            scratch_shapes=list(scratch),
        ),
        out_shape=[struct(shape, kind) for shape, kind in outs]
        + [struct(item.shape, item.dtype) for item in carry],
        input_output_aliases=aliases,
        compiler_params=pltpu.CompilerParams(
            dimension_semantics=("arbitrary",) * len(grid), vmem_limit_bytes=VMEM_LIMIT
        ),
        cost_estimate=pl.CostEstimate(
            flops=int(micros * 1.0e9), bytes_accessed=int(micros * 2.0e6), transcendentals=0
        ),
        name=name,
    )(*scalars, *inputs, *extra)


def gate(item, after):
    (item,) = launch(
        lambda *_: None, "gate", (1,), (), (), [], [], [], micros=1, after=after, carry=[item]
    )
    return item


def exchange(rows, way, turn):
    axis, stride, count = way
    route = []
    for place in range(lax.axis_size(axis)):
        at = (place // stride) % count
        other = at ^ turn if count & (count - 1) == 0 else (at + turn) % count
        route.append((place, place + (other - at) * stride))
    return lax.ppermute(rows, axis, route)


def coordinate(way):
    axis, stride, count = way
    return ((lax.axis_index(axis) // stride) % count).astype(jnp.int32)


def fold(stacks, lines, way, shared=0, after=()):
    count = 1 if way is None else way[2]
    heights, width = [parts[0].shape[0] for parts in stacks], stacks[0][0].shape[1]
    heights[-1] -= lines
    shares = [height // count for height in heights]
    outs = [((sum(shares) + shared, width), BF16)] * count
    if way is None:
        outs += [((lines, width), F32)] if lines else []
    elif lines > shared:
        outs += [((lines - shared, width), F32)]
    parts = [part for stack in stacks for part in stack]
    if all(share % 16 == 0 for share in shares):
        at = coordinate(way).reshape(1) if way else jnp.zeros((1,), jnp.int32)
        return launch(
            functools.partial(fold_kernel, [len(stack) for stack in stacks], lines, shared, count),
            "fold",
            (1,),
            (at,),
            tuple(parts),
            [fixed(part.shape) for part in parts],
            outs,
            [fixed(shape) for shape, _ in outs],
            [pltpu.VMEM((height, width), BF16) for height in heights] if count > 1 else [],
            micros=2,
            after=after,
        )
    (height,), (share,) = heights, shares
    total = sum(part.astype(F32) for part in parts)
    if way is None:
        return [total[:height].astype(BF16)] + ([total[height:]] if lines else [])
    at = coordinate(way)
    results = [
        jnp.concatenate(
            [
                lax.dynamic_slice_in_dim(total, apart(at, count, turn) * share, share, 0),
                total[height : height + shared],
            ],
            axis=0,
        ).astype(BF16)
        for turn in range(count)
    ]
    return results + ([total[height + shared :]] if lines > shared else [])


def swap(gives, way):
    return [gives[0]] + [exchange(gives[turn], way, turn) for turn in range(1, way[2])]


def fetch(own, way):
    return [own] + [exchange(own, way, turn) for turn in range(1, way[2])]


def spread(parts, way, after=(), carry=()):
    own, count = parts[0], way[2]
    share, width = own.shape
    at = coordinate(way)
    if share % 16 == 0:
        whole, *carry = launch(
            functools.partial(spread_kernel, count),
            "spread",
            (1,),
            (at.reshape(1),),
            tuple(parts),
            [fixed(own.shape)] * count,
            [((share * count, width), BF16)],
            [fixed((share * count, width))],
            micros=2,
            after=after,
            carry=carry,
        )
        return (whole, *carry) if carry else whole
    stack = jnp.stack(parts)
    turns = [at ^ place if count & (count - 1) == 0 else (at - place) % count for place in range(count)]
    whole = jnp.concatenate(
        [lax.dynamic_index_in_dim(stack, turn, 0, False) for turn in turns], axis=0
    )
    return (whole, *carry) if carry else whole


def finish(own, got, width, places, counts, after=()):
    high = (lax.axis_index("dp") % 2).astype(jnp.int32).reshape(1)
    squares = sum(counts)
    return launch(
        functools.partial(finish_kernel, places, counts),
        "finish",
        (1,),
        (high,),
        (own, got),
        [fixed(own.shape)] * 2,
        [((width, width), F32)] * squares,
        [fixed((width, width))] * squares,
        micros=2,
        after=after,
    )


def on_device(
    tokens,
    memory,
    cotangent,
    target_length,
    memory_length,
    expert_of,
    self_norm_gain,
    self_norm_bias,
    self_query,
    self_key,
    self_value,
    self_out,
    self_query_bias,
    self_value_bias,
    self_out_bias,
    cross_norm_gain,
    cross_norm_bias,
    cross_query,
    cross_key,
    cross_value,
    cross_out,
    cross_attention_query_bias,
    cross_value_bias,
    cross_out_bias,
    expert_norm_gain,
    expert_norm_bias,
    expert_in,
    expert_in_bias,
    expert_out,
    expert_out_bias,
):
    seqs, length, width = tokens.shape
    mem_rows = memory.shape[1]
    local_count, _, hidden_width = expert_in.shape
    groups = lax.axis_size("expert")
    places = lax.axis_size("dp")
    own_group = lax.axis_index("expert")
    column = lax.axis_index("dp")

    shifts = list(range(1, groups)) + [0]
    whole = groups == seqs
    rows_shape, square = (length, width), (width, width)
    mem_shape, heads_shape = (mem_rows, width), (HEADS, length)
    turned = (width, length)
    in_smem = pl.BlockSpec(memory_space=pltpu.SMEM)
    lines = [
        self_norm_gain,
        self_norm_bias,
        self_query_bias,
        self_value_bias,
        self_out_bias,
        cross_norm_gain,
        cross_norm_bias,
        cross_attention_query_bias,
        cross_value_bias,
        cross_out_bias,
        expert_norm_gain,
        expert_norm_bias,
    ]
    in_vmem = pl.BlockSpec(memory_space=pltpu.VMEM)
    order, picks, used, slot_of, spot_of, vectors, *grads = pl.pallas_call(
        functools.partial(plan_kernel, shifts, local_count),
        in_specs=[in_smem] * 3 + [in_vmem] * (1 + VECTORS),
        out_specs=[in_smem] * 5 + [in_vmem] * (1 + groups),
        out_shape=[
            struct((seqs + 1,), jnp.int32),
            struct((groups,), jnp.int32),
            struct((groups,), jnp.int32),
            struct((seqs,), jnp.int32),
            struct((groups,), jnp.int32),
            struct((16, width), F32),
        ]
        + [struct(rows_shape, BF16)] * groups,
        compiler_params=pltpu.CompilerParams(vmem_limit_bytes=VMEM_LIMIT),
        name="plan",
    )(
        jnp.stack([own_group, column, jnp.int32(places)]).astype(jnp.int32),
        expert_of,
        target_length,
        cotangent,
        *[line.reshape(1, width) for line in lines],
    )

    def move(rows, slot, back=False):
        shift = shifts[slot]
        if shift == 0:
            return rows
        turn = -shift if back else shift
        return lax.ppermute(rows, "expert", [(g, (g + turn) % groups) for g in range(groups)])

    def arranged(per_slot):
        if whole:
            return per_slot
        stack = jnp.stack(per_slot)
        return [lax.dynamic_index_in_dim(stack, slot_of[at], 0, False) for at in range(seqs)]

    position = lambda shape, start=0: at_position(shape, start, seqs)
    sequence = lambda shape, start=0: at_sequence(shape, start, seqs)
    self_matrices = (self_query, self_key, self_value, self_out)
    cross_matrices = (cross_query, cross_key, cross_value, cross_out)
    half = seqs // 2
    high = (column % 2).astype(jnp.int32).reshape(1)

    saved = [
        (rows_shape, F32),
        (rows_shape, F32),
        (rows_shape, BF16),
        (rows_shape, BF16),
        (rows_shape, BF16),
        (turned, BF16),
        (heads_shape, F32),
        (rows_shape, BF16),
        (mem_shape, BF16),
        (mem_shape, BF16),
        (turned, BF16),
        (heads_shape, F32),
    ]

    def forward(start, steps, kept, after):
        results = launch(
            functools.partial(forward_kernel, start, steps),
            "forward",
            (steps,),
            (order, target_length, memory_length),
            (tokens, memory, vectors) + self_matrices + cross_matrices,
            [sequence(rows_shape, start), sequence(mem_shape, start), fixed(vectors.shape)]
            + [fixed(square)] * 8,
            [(rows_shape, BF16)] * steps + [((seqs,) + shape, kind) for shape, kind in saved],
            [fixed(rows_shape)] * steps + [position(shape, start) for shape, _ in saved],
            [pltpu.VMEM(turned, BF16)],
            micros=0.01,
            after=after,
            into={at + steps: item for at, item in enumerate(kept)},
        )
        return results[:steps], results[steps:]

    grads_in = [move(grads[slot], slot) for slot in range(groups)]
    normed_one, kept = forward(0, half, [], [])
    normed_two, kept = forward(half, seqs - half, kept, [grads_in[0]])
    normed = list(normed_one) + list(normed_two)
    (
        later,
        middle,
        query_one,
        key_one,
        value_one,
        context_one,
        logsum_one,
        query_two,
        key_two,
        value_two,
        context_two,
        logsum_two,
    ) = kept

    if whole:
        rows_in = [move(normed[slot], slot) for slot in range(groups)]
    else:
        joined = jnp.stack(normed)
        rows_in = [
            move(lax.dynamic_index_in_dim(joined, spot_of[slot], 0, False), slot)
            for slot in range(groups)
        ]
    tiles = 4
    tile_width = hidden_width // tiles
    hidden_tile = pl.BlockSpec((length, tile_width), lambda t, *_: (0, t))
    line_tile = pl.BlockSpec((1, tile_width), lambda t, *_: (0, t))
    hidden, grad_pre, made, grad_rows, pre_sum, grads_sum = {}, {}, {}, {}, {}, {}

    def expert(slot, after):
        results = launch(
            functools.partial(expert_kernel, slot),
            "expert",
            (tiles,),
            (picks, used),
            (rows_in[slot], grads_in[slot], expert_in, expert_in_bias, expert_out, expert_out_bias),
            [
                fixed(rows_shape),
                fixed(rows_shape),
                pl.BlockSpec((1, width, tile_width), lambda t, pick, _: (pick[slot], 0, t)),
                pl.BlockSpec((local_count, tile_width), lambda t, *_: (0, t)),
                pl.BlockSpec((1, tile_width, width), lambda t, pick, _: (pick[slot], t, 0)),
                fixed((local_count, width)),
            ],
            [((length, hidden_width), BF16)] * 2
            + [(rows_shape, BF16)] * 2
            + [((1, hidden_width), F32), ((1, width), F32)],
            [hidden_tile, hidden_tile, fixed(rows_shape), fixed(rows_shape), line_tile]
            + [fixed((1, width))],
            [pltpu.VMEM(rows_shape, F32)] * 2,
            micros=0.01,
            after=after,
        )
        for table, result in zip((hidden, grad_pre, made, grad_rows, pre_sum, grads_sum), results):
            table[slot] = result

    back_scratch = [
        pltpu.VMEM((width, mem_rows), BF16),
        pltpu.VMEM(rows_shape, BF16),
        pltpu.VMEM(heads_shape, F32),
        pltpu.VMEM(turned, BF16),
    ]

    def sums_shape(count, final, lines=0):
        if final:
            return [((count * width // 2 + lines, width), BF16)] * 2
        return [((count,) + square, BF16)]

    def cross_back(start, steps, grads, given, filled, final, after, carry=(), micros=26):
        first = given is None
        total = sums_shape(5, final)
        return launch(
            functools.partial(cross_back_kernel, start, first, final, steps),
            "cross_back",
            (steps,),
            (order, target_length, memory_length, high),
            tuple(grads)
            + (() if first else tuple(given))
            + (cotangent, memory, later, middle, query_two, key_two, value_two, context_two)
            + (logsum_two, context_one, vectors)
            + cross_matrices,
            [once(rows_shape)] * steps
            + ([] if first else [once((5,) + square), once((8, width))])
            + [
                sequence(rows_shape, start),
                sequence(mem_shape, start),
                position(rows_shape, start),
                position(rows_shape, start),
                position(rows_shape, start),
                position(mem_shape, start),
                position(mem_shape, start),
                position(turned, start),
                position(heads_shape, start),
                position(turned, start),
                fixed(vectors.shape),
            ]
            + [once(square)] * 4,
            [((seqs,) + rows_shape, F32)]
            + [((seqs,) + mem_shape, BF16)] * 2
            + total
            + [((8, width), F32)],
            [position(rows_shape, start), position(mem_shape, start), position(mem_shape, start)]
            + [fixed(shape) for shape, _ in total]
            + [fixed((8, width))],
            [pltpu.VMEM((5,) + square, F32), pltpu.VMEM((8, width), F32), pltpu.VMEM(rows_shape, BF16)]
            + back_scratch,
            micros=micros,
            after=after,
            into={at: item for at, item in enumerate(filled)},
            carry=carry,
        )

    def self_back(start, steps, given, filled, final, after):
        first = given is None
        total = sums_shape(3, final, LINES) if final else sums_shape(3, final) + [((8, width), F32)]
        return launch(
            functools.partial(self_back_kernel, start, first, final),
            "self_back",
            (steps,),
            (order, target_length, high),
            (() if first else tuple(given))
            + (cross_lines, expert_lines)
            + (tokens, grad_middle, query_one, key_one, value_one, context_one, logsum_one, columns)
            + self_matrices,
            ([] if first else [once((3,) + square), once((8, width))])
            + [fixed((8, width)), fixed((EXPERT_LINES, width))]
            + [
                sequence(rows_shape, start),
                position(rows_shape, start),
                position(rows_shape, start),
                position(rows_shape, start),
                position(rows_shape, start),
                position(turned, start),
                position(heads_shape, start),
                fixed(columns.shape),
            ]
            + [once(square)] * 4,
            [((seqs,) + rows_shape, BF16)] * 3 + total,
            [position(rows_shape, start)] * 3 + [fixed(shape) for shape, _ in total],
            [pltpu.VMEM((3,) + square, F32), pltpu.VMEM((8, width), F32)] + back_scratch,
            micros=10 * steps,
            after=after,
            into={at: item for at, item in enumerate(filled)},
        )

    back = {}

    def send_back(slot):
        back[slot] = move(grad_rows[slot], slot, True)

    if whole:
        expert(3, [])
        send_back(3)
        results = cross_back(
            3, 1, [back[3]], None, [], False, grads_in[1:3], micros=0.01
        )
        filled, running = results[:3], results[3:5]
        expert(0, running[1:])
        expert(1, [made[0]])
        expert(2, [made[1]])
        for slot in range(3):
            send_back(slot)
    else:
        for slot in range(groups):
            expert(slot, [])
            send_back(slot)

    in_sums, out_sums, expert_lines = launch(
        functools.partial(expert_weights_kernel, groups),
        "expert_weights",
        (tiles,),
        (picks, used),
        tuple(rows_in)
        + tuple(grads_in)
        + tuple(table[slot] for table in (hidden, grad_pre, pre_sum, grads_sum) for slot in range(groups)),
        [once(rows_shape)] * (2 * groups)
        + [hidden_tile] * (2 * groups)
        + [line_tile] * groups
        + [fixed((1, width))] * groups,
        [
            ((local_count, width, hidden_width), BF16),
            ((local_count, hidden_width, width), BF16),
            ((EXPERT_LINES, width), F32),
        ],
        [
            pl.BlockSpec((local_count, width, tile_width), lambda t, *_: (0, 0, t)),
            pl.BlockSpec((local_count, tile_width, width), lambda t, *_: (0, t, 0)),
            fixed((EXPERT_LINES, width)),
        ],
        [
            pltpu.VMEM((local_count, width, tile_width), F32),
            pltpu.VMEM((local_count, tile_width, width), F32),
            pltpu.VMEM((local_count, 1, tile_width), F32),
            pltpu.VMEM((local_count, 1, width), F32),
        ],
        micros=17,
        after=[back[0]] if whole else [],
    )
    expert_in_grad = lax.psum_scatter(in_sums, "dp", scatter_dimension=1, tiled=True)
    expert_out_grad = lax.psum_scatter(out_sums, "dp", scatter_dimension=1, tiled=True)

    if whole:
        away = [slot for slot in range(groups) if shifts[slot]]
        results = cross_back(
            0, 2, [back[0], back[1]], running, filled, False, [in_sums], [made[slot] for slot in away]
        )
        filled, running = results[:3], results[3:5]
        for at, slot in enumerate(away):
            made[slot] = results[5 + at]
        made_home = [move(made[slot], slot, True) for slot in range(groups)]
        *results, cross_keep, cross_give, cross_lines = cross_back(
            2, 1, [back[2]], running, filled, True, []
        )
    else:
        *results, cross_keep, cross_give, cross_lines = cross_back(
            0, seqs, arranged([back[slot] for slot in range(groups)]), None, [], True, []
        )
        made_home = arranged([move(made[slot], slot, True) for slot in range(groups)])
    grad_middle, grad_key_two, grad_value_two = results

    chips = places // 2
    core, plane, line = ("dp", 1, 2), ("dp", 2, chips), ("expert", 1, groups)
    columns = jnp.concatenate([vectors.T, jnp.zeros((width, 128 - vectors.shape[0]), F32)], axis=1)

    def tokens_back(start, steps, grads, filled, after):
        return launch(
            functools.partial(tokens_back_kernel, start),
            "tokens_back",
            (steps,),
            (order, target_length),
            (tokens, grad_middle, *grads, vectors)
            + self_matrices[:3],
            [sequence(rows_shape, start)]
            + [position(rows_shape, start)] * 4
            + [fixed(vectors.shape)]
            + [once(square)] * 3,
            [((seqs,) + rows_shape, F32)],
            [sequence(rows_shape, start)],
            micros=4 * steps,
            after=after,
            into={at: item for at, item in enumerate(filled)},
        )

    def memory_back(after):
        return launch(
            memory_back_kernel,
            "memory_back",
            (seqs,),
            (order,),
            (grad_key_two, grad_value_two, cross_key, cross_value),
            [position(mem_shape)] * 2 + [once(square)] * 2,
            [((seqs,) + mem_shape, F32)],
            [sequence(mem_shape)],
            micros=5,
            after=after,
        )[0]

    def output_rows(after):
        return launch(
            functools.partial(output_kernel, seqs),
            "output",
            (seqs,),
            (order, target_length),
            (later, *made_home),
            [position(rows_shape)] + [once(rows_shape)] * seqs,
            [((seqs,) + rows_shape, BF16)],
            [sequence(rows_shape)],
            micros=5,
            after=after,
        )[0]

    def casts(items, after):
        return launch(
            cast_kernel,
            "cast",
            (1,),
            (),
            tuple(items),
            [fixed(item.shape) for item in items],
            [(item.shape, F32) for item in items],
            [fixed(item.shape) for item in items],
            micros=3,
            after=after,
        )

    cross_got = exchange(gate(cross_give, made_home[:1]), core, 1)
    memory_grad = memory_back([])
    cross_parts = swap(fold([[cross_keep, cross_got]], 0, plane, after=[memory_grad]), plane)
    *grads_one, weights_run, vectors_run = self_back(
        0, half, None, [], False, [cross_parts[0]]
    )
    cross_line = swap(fold([cross_parts], 0, line, after=grads_one[:1]), line)
    filled = tokens_back(0, half, grads_one, [], [cross_line[0], *made_home[1:2]])
    (cross_share,) = fold([cross_line], 0, None, after=filled)
    cross_fetched = fetch(cross_share, line)
    *grads_one, self_keep, self_give = self_back(
        half,
        seqs - half,
        (weights_run, vectors_run),
        grads_one,
        True,
        [cross_share, *filled],
    )

    cross_rows, self_give = spread(
        cross_fetched, line, after=[self_keep, *made_home[2:3]], carry=[self_give]
    )
    self_got = exchange(self_give, core, 1)
    cross_fetched = fetch(cross_rows, plane)
    expert_in_grad, expert_out_grad = casts([expert_in_grad, expert_out_grad], [cross_rows])

    self_parts = swap(
        fold([[self_keep, self_got]], LINES, plane, LINES, after=[expert_in_grad]), plane
    )
    output = output_rows([self_parts[0]])

    *gives, own_lines = fold([self_parts], LINES, line, SHARED_LINES, after=[output])
    self_line = swap(gives, line)
    cross_rows = spread(cross_fetched, plane, after=[output])
    cross_got = exchange(cross_rows, core, 1)
    filled = tokens_back(half, 1, grads_one, filled, [self_line[0], cross_rows])

    self_share, totals = fold([self_line], SHARED_LINES, None, after=filled)
    self_fetched = fetch(self_share, line)
    (tokens_grad,) = tokens_back(half + 1, seqs - half - 1, grads_one, filled, [self_share])

    self_rows = spread(self_fetched, line, after=[tokens_grad])
    self_fetched = fetch(self_rows, plane)
    cross_q, cross_k, cross_v, cross_o, self_o = finish(
        cross_rows, cross_got, width, 1, [5], [self_rows]
    )
    self_rows = spread(self_fetched, plane, after=[cross_q])
    self_q, self_k, self_v = finish(self_rows, exchange(self_rows, core, 1), width, 1, [3])

    in_count = local_count * hidden_width // width
    in_bias = own_lines[:in_count].reshape(local_count, hidden_width)
    out_bias = own_lines[in_count : in_count + local_count]
    in_share, out_share = hidden_width // places, width // places
    return (
        output,
        tokens_grad,
        memory_grad,
        totals[2],
        totals[3],
        self_q,
        self_k,
        self_v,
        self_o,
        totals[0],
        totals[1],
        totals[15],
        totals[13],
        totals[14],
        cross_q,
        cross_k,
        cross_v,
        cross_o,
        totals[12],
        totals[11],
        totals[10],
        totals[8],
        totals[9],
        expert_in_grad,
        lax.dynamic_slice_in_dim(in_bias, column * in_share, in_share, 1),
        expert_out_grad,
        lax.dynamic_slice_in_dim(out_bias, column * out_share, out_share, 1),
    )


def solution(mesh):
    rows = P(("expert", "dp"), None, None)
    counts = P(("expert", "dp"))
    split = (P("expert", None, None), P("expert", None)) * 2
    shares = (P("expert", "dp", None), P("expert", "dp")) * 2
    return jax.shard_map(
        on_device,
        mesh=mesh,
        in_specs=(rows,) * 3 + (counts,) * 2 + (P(),) * 21 + split,
        out_specs=(rows,) * 3 + (P(),) * 20 + shares,
        check_vma=False,
    )
```

```python
import functools

import jax
import jax.numpy as jnp
from jax import lax
from jax.experimental import pallas as pl
from jax.experimental.pallas import tpu as pltpu
from jax.sharding import PartitionSpec as P

HEADS = 8
HEAD_DIM = 64
PAIR = 2 * HEAD_DIM
EPSILON = 1e-05
SCORE_SCALE = 0.125
NEGATIVE = -1e30
SAFE_SCORE = 80.0
SHARED_LINES = 16
EXPERT_LINES = 16
VECTORS = 12
LINES = SHARED_LINES + EXPERT_LINES
LOG2E = 1.4426950408889634
LN2 = 0.6931471805599453
VMEM_LIMIT = 64 * 1024 * 1024
F32 = jnp.float32
BF16 = jnp.bfloat16


def contract(left, right, left_dim, right_dim):
    return lax.dot_general(
        left, right, (((left_dim,), (right_dim,)), ((), ())), preferred_element_type=F32
    )


def nn(left, right):
    return contract(left, right, 1, 0)


def nt(left, right):
    return contract(left, right, 1, 1)


def tn(left, right):
    return contract(left, right, 0, 0)


def normalise(rows):
    centre = rows - jnp.mean(rows, axis=-1, keepdims=True)
    inverse = lax.rsqrt(jnp.mean(centre * centre, axis=-1, keepdims=True) + EPSILON)
    return centre * inverse, inverse


def normalise_back(grad, normed, inverse, gain):
    scaled = grad * gain
    return inverse * (
        scaled
        - jnp.mean(scaled, axis=-1, keepdims=True)
        - normed * jnp.mean(scaled * normed, axis=-1, keepdims=True)
    )


def column_sum(rows):
    return jnp.sum(rows.astype(F32), axis=0, keepdims=True)


def head_masks():
    lane = lax.broadcasted_iota(jnp.int32, (1, PAIR), 1)
    mine = [(lane // HEAD_DIM == half).astype(F32).astype(BF16) for half in (0, 1)]
    spare = [(lane == HEAD_DIM * (1 - half)).astype(F32).astype(BF16) for half in (0, 1)]
    return mine, spare


def key_bias(count, mem_rows):
    place = lax.broadcasted_iota(jnp.int32, (mem_rows, PAIR), 0)
    return jnp.where(place < count, 0.0, NEGATIVE).astype(BF16)


def score_operands(keys, queries, half, mine, spare, bias):
    picked = queries * mine[half]
    if bias is None:
        return keys, picked
    return keys * (1 - spare[half]) + bias * spare[half], picked + spare[half]


def causal(scores, block):
    key_at = lax.broadcasted_iota(jnp.int32, (scores.shape[0], block), 0)
    query_at = lax.broadcasted_iota(jnp.int32, (scores.shape[0], block), 1)
    return jnp.where(key_at <= query_at, scores, NEGATIVE)


def lower(items, block):
    return jnp.concatenate([item[block:] for item in items], axis=0)


def lower_columns(items, block):
    return jnp.concatenate([item[:, block:] for item in items], axis=1)


def span(start, size):
    return slice(start, start + size) if isinstance(start, int) else pl.ds(pl.multiple_of(start, size), size)


def head_rows(pair, half):
    return span(pair * PAIR + half * HEAD_DIM, HEAD_DIM)


def pair_span(pair):
    return span(pair * PAIR, PAIR)


def each_pair(pair_step, unrolled):
    if unrolled:
        for pair in range(HEADS // 2):
            pair_step(pair, 0)
    else:
        lax.fori_loop(0, HEADS // 2, pair_step, 0)


def head_part(both, half, block):
    return both[half * HEAD_DIM : (half + 1) * HEAD_DIM, half * block : (half + 1) * block]


def causal_pair_scores(keys, picked, block):
    upper = []
    for half in (0, 1):
        scores = nt(keys[:block], picked[half])
        upper.append(
            jnp.concatenate([causal(scores[:, :block], block), scores[:, block:]], axis=1)
        )
    scores = nt(keys[block:], lower(picked, block))
    low = jnp.concatenate([causal(scores[:, :block], block), causal(scores[:, block:], block)], axis=1)
    return upper, low


def head_blocks():
    feature = lax.broadcasted_iota(jnp.int32, (HEADS * HEAD_DIM, 128), 0)
    return (feature // HEAD_DIM == lax.broadcasted_iota(jnp.int32, (HEADS * HEAD_DIM, 128), 1)).astype(BF16)


def scores_small(query_ref, key_ref):
    blocks = head_blocks()
    squares = [nn(ref[...] * ref[...], blocks) for ref in (query_ref, key_ref)]
    most = [jnp.max(item, axis=0, keepdims=True) for item in squares]
    return jnp.max(most[0] * most[1]) < SAFE_SCORE * SAFE_SCORE


def attend_cross(plain, query_ref, key_ref, value_t_ref, context_t_ref, logsum_ref, bias):
    mine, spare = head_masks()

    def pair_step(pair, carry):
        columns = pair_span(pair)
        keys, queries = key_ref[:, columns], query_ref[:, columns]
        for half in (0, 1):
            rows = head_rows(pair, half)
            left, right = score_operands(keys, queries, half, mine, spare, bias)
            scores = nt(left, right)
            highest = 0.0 if plain else jnp.max(scores, axis=0, keepdims=True)
            raised = jnp.exp2(scores if plain else scores - highest)
            summed = jnp.sum(raised, axis=0, keepdims=True)
            context = nn(value_t_ref[rows, :], raised.astype(BF16))
            context_t_ref[rows, :] = (context * (1.0 / summed)).astype(BF16)
            logsum_ref[pl.ds(2 * pair + half, 1), :] = highest + LOG2E * jnp.log(summed)
        return carry

    each_pair(pair_step, plain)


def attend_self(plain, query_ref, key_ref, value_t_ref, context_t_ref, logsum_ref):
    block = query_ref.shape[0] // 2
    mine, _ = head_masks()

    def pair_step(pair, carry):
        columns = pair_span(pair)
        keys, queries = key_ref[:, columns], query_ref[:, columns]
        upper, low = causal_pair_scores(keys, [queries * mine[0], queries * mine[1]], block)
        if plain:
            highest = [0.0, 0.0]
            low = jnp.exp2(low)
        else:
            low_top = jnp.max(low, axis=0, keepdims=True)
            highest = []
            for half in (0, 1):
                top = jnp.max(upper[half], axis=0, keepdims=True)
                other = low_top[:, half * block : (half + 1) * block]
                highest.append(
                    jnp.concatenate([top[:, :block], jnp.maximum(top[:, block:], other)], axis=1)
                )
            low = jnp.exp2(low - lower_columns(highest, block))
        low_sum = jnp.sum(low, axis=0, keepdims=True)
        low_context = nn(value_t_ref[columns, block:], low.astype(BF16))
        for half in (0, 1):
            rows = head_rows(pair, half)
            raised = jnp.exp2(upper[half] if plain else upper[half] - highest[half])
            summed = jnp.sum(raised, axis=0, keepdims=True)
            part = low_sum[:, half * block : (half + 1) * block]
            summed = jnp.concatenate([summed[:, :block], summed[:, block:] + part], axis=1)
            context = nn(value_t_ref[rows, :block], raised.astype(BF16))
            context = jnp.concatenate(
                [context[:, :block], context[:, block:] + head_part(low_context, half, block)],
                axis=1,
            )
            context_t_ref[rows, :] = (context * (1.0 / summed)).astype(BF16)
            logsum_ref[pl.ds(2 * pair + half, 1), :] = highest[half] + LOG2E * jnp.log(summed)
        return carry

    each_pair(pair_step, plain)


def attend(kind, query_ref, key_ref, *refs):
    small = scores_small(query_ref, key_ref)

    @pl.when(small)
    def _():
        kind(True, query_ref, key_ref, *refs)

    @pl.when(jnp.logical_not(small))
    def _():
        kind(False, query_ref, key_ref, *refs)


def attend_cross_back(
    query_ref,
    key_ref,
    value_ref,
    key_t_ref,
    grad_ref,
    delta_ref,
    logsum_ref,
    grad_query_t_ref,
    grad_key_ref,
    grad_value_ref,
    bias,
):
    mine, spare = head_masks()

    def pair_step(pair, carry):
        columns = pair_span(pair)
        keys, queries, values = key_ref[:, columns], query_ref[:, columns], value_ref[:, columns]
        grads = grad_ref[:, columns]
        chances, slopes, picked_grads, picked_queries = [], [], [], []
        for half in (0, 1):
            head, rows = pl.ds(2 * pair + half, 1), head_rows(pair, half)
            left, right = score_operands(keys, queries, half, mine, spare, bias)
            picked_grads.append(grads * mine[half])
            picked_queries.append(queries * mine[half])
            chance = jnp.exp2(nt(left, right) - logsum_ref[head, :])
            slope = chance * (nt(values, picked_grads[half]) - delta_ref[head, :])
            chances.append(chance.astype(BF16))
            slopes.append(slope.astype(BF16))
            grad_query_t_ref[rows, :] = (nn(key_t_ref[rows, :], slopes[half]) * SCORE_SCALE).astype(
                BF16
            )
        grad_value_ref[:, columns] = nn(
            jnp.concatenate(chances, axis=1), jnp.concatenate(picked_grads, axis=0)
        ).astype(BF16)
        grad_key_ref[:, columns] = (
            nn(jnp.concatenate(slopes, axis=1), jnp.concatenate(picked_queries, axis=0)) * LN2
        ).astype(BF16)
        return carry

    each_pair(pair_step, True)


def attend_self_back(
    query_ref,
    key_ref,
    value_ref,
    key_t_ref,
    grad_ref,
    delta_ref,
    logsum_ref,
    grad_query_t_ref,
    grad_key_ref,
    grad_value_ref,
):
    block = query_ref.shape[0] // 2
    mine, _ = head_masks()

    def pair_step(pair, carry):
        columns = pair_span(pair)
        keys, queries, values = key_ref[:, columns], query_ref[:, columns], value_ref[:, columns]
        grads = grad_ref[:, columns]
        picked = [queries * mine[0], queries * mine[1]]
        picked_grads = [grads * mine[0], grads * mine[1]]
        upper, low = causal_pair_scores(keys, picked, block)
        logsum = [logsum_ref[pl.ds(2 * pair + half, 1), :] for half in (0, 1)]
        delta = [delta_ref[pl.ds(2 * pair + half, 1), :] for half in (0, 1)]
        low_grads = lower(picked_grads, block)
        low = jnp.exp2(low - lower_columns(logsum, block))
        low_slope = (
            low * (nt(values[block:], low_grads) - lower_columns(delta, block))
        ).astype(BF16)
        low_query = nn(key_t_ref[columns, block:], low_slope)
        chances, slopes = [], []
        for half in (0, 1):
            chance = jnp.exp2(upper[half] - logsum[half])
            slope = chance * (nt(values[:block], picked_grads[half]) - delta[half])
            chances.append(chance.astype(BF16))
            slopes.append(slope.astype(BF16))
            rows = head_rows(pair, half)
            grad = nn(key_t_ref[rows, :block], slopes[half])
            grad = jnp.concatenate(
                [grad[:, :block], grad[:, block:] + head_part(low_query, half, block)], axis=1
            )
            grad_query_t_ref[rows, :] = (grad * SCORE_SCALE).astype(BF16)
        grad_value_ref[:block, columns] = nn(
            jnp.concatenate(chances, axis=1), jnp.concatenate(picked_grads, axis=0)
        ).astype(BF16)
        grad_value_ref[block:, columns] = nn(low.astype(BF16), low_grads).astype(BF16)
        grad_key_ref[:block, columns] = (
            nn(jnp.concatenate(slopes, axis=1), jnp.concatenate(picked, axis=0)) * LN2
        ).astype(BF16)
        grad_key_ref[block:, columns] = (nn(low_slope, lower(picked, block)) * LN2).astype(BF16)
        return carry

    each_pair(pair_step, True)


def head_sums(grad, context_t):
    product = grad.T.astype(F32) * context_t.astype(F32)
    return jnp.sum(product.reshape(HEADS, HEAD_DIM, product.shape[1]), axis=1)


def valid_rows_of(count, length):
    return (lax.broadcasted_iota(jnp.int32, (length, 1), 0) < count).astype(F32)


def forward_kernel(
    start_at,
    steps,
    order_ref,
    target_ref,
    memory_length_ref,
    tokens_ref,
    memory_ref,
    vectors_ref,
    self_query,
    self_key,
    self_value,
    self_out,
    cross_query,
    cross_key,
    cross_value,
    cross_out,
    *refs,
):
    normed_refs, refs = refs[:steps], refs[steps:]
    (
    later_ref,
    middle_ref,
    query_one_ref,
    key_one_ref,
    value_one_ref,
    context_one_ref,
    logsum_one_ref,
    query_two_ref,
    key_two_ref,
    value_two_ref,
    context_two_ref,
    logsum_two_ref,
    value_t_ref,
    ) = refs
    step = pl.program_id(0)
    sequence = order_ref[start_at + step]
    length = tokens_ref.shape[1]
    vector = lambda at: vectors_ref[at : at + 1, :]
    start = tokens_ref[0].astype(F32) * valid_rows_of(target_ref[sequence], length)
    normed = (normalise(start)[0] * vector(0) + vector(1)).astype(BF16)
    scale = SCORE_SCALE * LOG2E
    query_one_ref[0] = ((nn(normed, self_query[...]) + vector(2)) * scale).astype(BF16)
    key_one_ref[0] = nn(normed, self_key[...]).astype(BF16)
    value = (nn(normed, self_value[...]) + vector(3)).astype(BF16)
    value_one_ref[0] = value
    value_t_ref[...] = value.T
    attend(
        attend_self,
        query_one_ref.at[0],
        key_one_ref.at[0],
        value_t_ref,
        context_one_ref.at[0],
        logsum_one_ref.at[0],
    )
    middle = start + tn(context_one_ref[0], self_out[...]) + vector(4)
    middle_ref[0] = middle
    normed = (normalise(middle)[0] * vector(5) + vector(6)).astype(BF16)
    memory = memory_ref[0]
    query_two_ref[0] = ((nn(normed, cross_query[...]) + vector(7)) * scale).astype(BF16)
    key_two_ref[0] = nn(memory, cross_key[...]).astype(BF16)
    value = (nn(memory, cross_value[...]) + vector(8)).astype(BF16)
    value_two_ref[0] = value
    value_t_ref[...] = value.T
    attend(
        attend_cross,
        query_two_ref.at[0],
        key_two_ref.at[0],
        value_t_ref,
        context_two_ref.at[0],
        logsum_two_ref.at[0],
        key_bias(memory_length_ref[sequence], memory.shape[0]),
    )
    later = middle_ref[0] + tn(context_two_ref[0], cross_out[...]) + vector(9)
    later_ref[0] = later
    normed = (normalise(later)[0] * vector(10) + vector(11)).astype(BF16)
    for at in range(steps):

        @pl.when(step == at)
        def _():
            normed_refs[at][...] = normed


def expert_kernel(
    slot,
    pick_ref,
    used_ref,
    rows_ref,
    grads_ref,
    weight_in,
    bias_in,
    weight_out,
    bias_out,
    hidden_ref,
    grad_pre_ref,
    made_ref,
    grad_rows_ref,
    pre_sum_ref,
    grads_sum_ref,
    made_sum,
    grad_sum,
):
    tile = pl.program_id(0)
    last = pl.num_programs(0) - 1
    used = used_ref[slot] > 0
    pick = pl.ds(pick_ref[slot], 1)

    @pl.when(used)
    def _():
        made = grad_rows = 0.0
        chunk = hidden_ref.shape[1] // 2
        for columns in (slice(0, chunk), slice(chunk, 2 * chunk)):
            pre = nn(rows_ref[...], weight_in[0, :, columns]) + bias_in[pick, columns]
            grad_hidden = nt(grads_ref[...], weight_out[0, columns, :])
            gate = 0.5 * jnp.tanh(0.5 * pre) + 0.5
            active = pre * gate
            hidden = active.astype(BF16)
            hidden_ref[:, columns] = hidden
            grad_pre = grad_hidden * (gate + active * (1.0 - gate))
            pre_sum_ref[:, columns] = jnp.sum(grad_pre, axis=0, keepdims=True)
            grad_pre = grad_pre.astype(BF16)
            grad_pre_ref[:, columns] = grad_pre
            made += nn(hidden, weight_out[0, columns, :])
            grad_rows += nt(grad_pre, weight_in[0, :, columns])

        @pl.when(tile == 0)
        def _():
            made_sum[...] = made
            grad_sum[...] = grad_rows
            grads_sum_ref[...] = column_sum(grads_ref[...])

        @pl.when(tile > 0)
        def _():
            made_sum[...] += made
            grad_sum[...] += grad_rows

        @pl.when(tile == last)
        def _():
            made_ref[...] = (made_sum[...] + bias_out[pick, :]).astype(BF16)
            grad_rows_ref[...] = grad_sum[...].astype(BF16)

    @pl.when(jnp.logical_not(used))
    def _():
        for ref in (hidden_ref, grad_pre_ref, made_ref, grad_rows_ref, pre_sum_ref, grads_sum_ref):
            ref[...] = jnp.zeros_like(ref)


def expert_weights_kernel(slots, pick_ref, used_ref, *refs):
    rows, grads, hidden, grad_pre, pre_sum, grads_sum = [
        refs[at * slots : (at + 1) * slots] for at in range(6)
    ]
    in_ref, out_ref, lines_ref, in_sum, out_sum, in_bias, out_bias = refs[6 * slots :]
    for total in (in_sum, out_sum, in_bias, out_bias):
        total[...] = jnp.zeros_like(total)
    for slot in range(slots):

        @pl.when(used_ref[slot] > 0)
        def _():
            pick = pick_ref[slot]
            in_sum[pick] += tn(rows[slot][...], grad_pre[slot][...])
            out_sum[pick] += tn(hidden[slot][...], grads[slot][...])
            in_bias[pick] += pre_sum[slot][...]
            out_bias[pick] += grads_sum[slot][...]

    in_ref[...] = in_sum[...].astype(BF16)
    out_ref[...] = out_sum[...].astype(BF16)
    tile, tiles = pl.program_id(0), pl.num_programs(0)
    count = in_bias.shape[0]

    @pl.when(tile == 0)
    def _():
        lines_ref[...] = jnp.zeros_like(lines_ref)

    for pick in range(count):
        lines_ref[pl.ds(pick * tiles + tile, 1), :] = in_bias[pick]
        lines_ref[pl.ds(count * tiles + pick, 1), :] = out_bias[pick]


def plan_kernel(
    shifts,
    local_count,
    place_ref,
    expert_ref,
    target_ref,
    cotangent_ref,
    *refs,
):
    lines, refs = refs[:VECTORS], refs[VECTORS:]
    order_ref, pick_ref, used_ref, slot_ref, spot_ref, vectors_ref, *grads_refs = refs
    vectors_ref[...] = jnp.zeros_like(vectors_ref)
    for at, line in enumerate(lines):
        vectors_ref[at : at + 1, :] = line[...]

    groups, seqs = len(shifts), cotangent_ref.shape[0]
    own, column, places = place_ref[0], place_ref[1], place_ref[2]
    own_ids = [expert_ref[(own * places + column) * seqs + at] for at in range(seqs)]
    distance = [lax.rem(lax.div(item, local_count) - own + groups, groups) for item in own_ids]
    slots = [
        sum((jnp.where(item == shift, at, 0) for at, shift in enumerate(shifts)), jnp.int32(0))
        for item in distance
    ]
    for slot in range(groups):
        spot_ref[slot] = 0
        source = lax.rem(own - shifts[slot] + groups, groups)
        pick, used = jnp.int32(0), jnp.int32(0)
        for at in range(seqs):
            item = expert_ref[(source * places + column) * seqs + at]
            here = lax.div(item, local_count) == own
            pick = jnp.where(here, lax.rem(item, local_count), pick)
            used = jnp.where(here, 1, used)
        pick_ref[slot] = pick
        used_ref[slot] = used
    for at in range(seqs):
        spot = sum((jnp.where(other < slots[at], 1, 0) for other in slots), jnp.int32(0))
        order_ref[spot] = at
        slot_ref[spot] = slots[at]
        spot_ref[slots[at]] = spot
    order_ref[seqs] = order_ref[0]
    length = cotangent_ref.shape[1]
    for slot in range(groups):
        sequence = order_ref[spot_ref[slot]]
        valid = valid_rows_of(target_ref[sequence], length)
        grads_refs[slot][...] = (cotangent_ref[sequence].astype(F32) * valid).astype(BF16)


def output_kernel(slots, order_ref, target_ref, later_ref, *refs):
    made, output_ref = refs[:slots], refs[slots]
    position = pl.program_id(0)
    valid = valid_rows_of(target_ref[order_ref[position]], later_ref.shape[1])
    for at in range(slots):

        @pl.when(position == at)
        def _():
            output_ref[0] = ((later_ref[0] + made[at][...].astype(F32)) * valid).astype(BF16)


def open_sums(first, weight_sum, vector_sum, given):
    @pl.when(pl.program_id(0) == 0)
    def _():
        if first:
            weight_sum[...] = jnp.zeros_like(weight_sum)
            vector_sum[...] = jnp.zeros_like(vector_sum)
        else:
            weight_sum[...] = given[0][...].astype(F32)
            vector_sum[...] = given[1][...]


def put_halves(squares, lines, high, keep_ref, give_ref):
    height = squares[0].shape[0]
    half = height * len(squares) // 2
    for top, (low_ref, high_ref) in ((0, (keep_ref, give_ref)), (1, (give_ref, keep_ref))):

        @pl.when(high == top)
        def _():
            for at, square in enumerate(squares):
                for part, ref in enumerate((low_ref, high_ref)):
                    start, stop = max(at * height, part * half), min((at + 1) * height, (part + 1) * half)
                    if start < stop:
                        rows = square[start - at * height : stop - at * height]
                        ref[start - part * half : stop - part * half] = rows.astype(BF16)

    if lines is not None:
        keep_ref[half:] = lines.astype(BF16)
        give_ref[half:] = lines.astype(BF16)


def close_sums(final, weight_sum, vector_sum, high, outs):
    @pl.when(pl.program_id(0) == pl.num_programs(0) - 1)
    def _():
        outs[-1][...] = vector_sum[...]
        if final:
            squares = [weight_sum[0].T] + [weight_sum[at] for at in range(1, weight_sum.shape[0])]
            put_halves(squares, None, high, outs[0], outs[1])
        else:
            outs[0][...] = weight_sum[...].astype(BF16)


def cross_back_kernel(
    start_at, first, final, slots, order_ref, target_ref, memory_length_ref, high_ref, *refs
):
    grad_normed, refs = refs[:slots], refs[slots:]
    given, refs = (None, refs) if first else (refs[:2], refs[2:])
    (
        cotangent_ref,
        memory_ref,
        later_ref,
        middle_ref,
        query_ref,
        key_ref,
        value_ref,
        context_ref,
        logsum_ref,
        context_one_ref,
        vectors_ref,
        cross_query,
        cross_key,
        cross_value,
        cross_out,
        grad_middle_ref,
        grad_key_ref,
        grad_value_ref,
        *outs,
        weight_sum,
        vector_sum,
        grad_expert,
        key_t,
        grad_context,
        delta,
        grad_query_t,
    ) = refs
    step = pl.program_id(0)
    sequence = order_ref[lax.rem(start_at + step, order_ref.shape[0] - 1)]
    length = cotangent_ref.shape[1]
    vector = lambda at: vectors_ref[at : at + 1, :]
    open_sums(first, weight_sum, vector_sum, given)

    for at in range(slots):

        @pl.when(step == at)
        def _():
            grad_expert[...] = grad_normed[at][...]

    def add_vector(at, value):
        vector_sum[at : at + 1, :] += value

    valid = valid_rows_of(target_ref[sequence], length)
    normed, inverse = normalise(later_ref[0])
    grad = grad_expert[...].astype(F32)
    add_vector(0, column_sum(grad * normed))
    add_vector(1, column_sum(grad))
    grad_later = cotangent_ref[0].astype(F32) * valid + normalise_back(
        grad, normed, inverse, vector(10)
    )
    branch = grad_later.astype(BF16)
    grad_middle_ref[0] = grad_later
    add_vector(2, column_sum(branch))
    weight_sum[3] += nn(context_ref[0], branch)
    context_grad = nt(branch, cross_out[...]).astype(BF16)
    grad_context[...] = context_grad
    delta[...] = head_sums(context_grad, context_ref[0])
    key_t[...] = key_ref[0].T
    attend_cross_back(
        query_ref.at[0],
        key_ref.at[0],
        value_ref.at[0],
        key_t,
        grad_context,
        delta,
        logsum_ref.at[0],
        grad_query_t,
        grad_key_ref.at[0],
        grad_value_ref.at[0],
        key_bias(memory_length_ref[sequence], memory_ref.shape[1]),
    )
    memory_t = memory_ref[0].T
    weight_sum[1] += nn(memory_t, grad_key_ref[0])
    weight_sum[2] += nn(memory_t, grad_value_ref[0])
    add_vector(3, column_sum(grad_value_ref[0]))
    normed, inverse = normalise(middle_ref[0])
    weight_sum[0] += nn(grad_query_t[...], (normed * vector(5) + vector(6)).astype(BF16))
    grad_query = grad_query_t[...].T
    add_vector(4, column_sum(grad_query))
    grad = nt(grad_query, cross_query[...])
    add_vector(5, column_sum(grad * normed))
    add_vector(6, column_sum(grad))
    grad_middle = grad_middle_ref[0] + normalise_back(grad, normed, inverse, vector(5))
    grad_middle_ref[0] = grad_middle
    branch = grad_middle.astype(BF16)
    add_vector(7, column_sum(branch))
    weight_sum[4] += nn(context_one_ref[0], branch)
    close_sums(final, weight_sum, vector_sum, high_ref[0], outs)


def self_back_kernel(start_at, first, final, order_ref, target_ref, high_ref, *refs):
    given, refs = (None, refs) if first else (refs[:2], refs[2:])
    cross_lines_ref, expert_lines_ref = refs[:2]
    refs = refs[2:]
    (
        tokens_ref,
        grad_middle_ref,
        query_ref,
        key_ref,
        value_ref,
        context_ref,
        logsum_ref,
        columns_ref,
        self_query,
        self_key,
        self_value,
        self_out,
        grad_query_ref,
        grad_key_ref,
        grad_value_ref,
        first_ref,
        second_ref,
        weight_sum,
        vector_sum,
        key_t,
        grad_context,
        delta,
        grad_query_t,
    ) = refs
    step = pl.program_id(0)
    sequence = order_ref[lax.rem(start_at + step, order_ref.shape[0] - 1)]
    length = tokens_ref.shape[1]
    open_sums(first, weight_sum, vector_sum, given)

    valid = valid_rows_of(target_ref[sequence], length)
    context_grad = nt(grad_middle_ref[0].astype(BF16), self_out[...]).astype(BF16)
    grad_context[...] = context_grad
    delta[...] = head_sums(context_grad, context_ref[0])
    key_t[...] = key_ref[0].T
    attend_self_back(
        query_ref.at[0],
        key_ref.at[0],
        value_ref.at[0],
        key_t,
        grad_context,
        delta,
        logsum_ref.at[0],
        grad_query_t,
        grad_key_ref.at[0],
        grad_value_ref.at[0],
    )
    normed = normalise(tokens_ref[0].astype(F32) * valid)[0].astype(BF16)
    normed_t = normed.T
    weight_sum[0] += nn(grad_query_t[...], normed)
    weight_sum[1] += nn(normed_t, grad_key_ref[0])
    weight_sum[2] += nn(normed_t, grad_value_ref[0])
    grad_query = grad_query_t[...].T
    grad_query_ref[0] = grad_query
    for at, item in enumerate((grad_query, grad_key_ref[0], grad_value_ref[0])):
        vector_sum[at : at + 1, :] += column_sum(item)

    @pl.when(step == pl.num_programs(0) - 1)
    def _():
        if not final:
            first_ref[...] = weight_sum[...].astype(BF16)
            second_ref[...] = vector_sum[...]
            return
        width = weight_sum.shape[1]
        gain, shift = columns_ref[:, 0:1], columns_ref[:, 1:2]
        gain_grad = jnp.zeros((width, 1), F32)
        shift_grad = jnp.zeros((width, 1), F32)
        squares = []
        for at, matrix in enumerate((self_query, self_key, self_value)):
            total = weight_sum[at].T if at == 0 else weight_sum[at]
            column = vector_sum[at : at + 1, :]
            weights = matrix[...].astype(F32)
            gain_grad += jnp.sum(weights * total, axis=1, keepdims=True)
            shift_grad += jnp.sum(weights * column, axis=1, keepdims=True)
            squares.append((total * gain + shift * column).astype(BF16))
        lane = lax.broadcasted_iota(jnp.int32, (width, 128), 1)
        both = jnp.where(lane == 0, gain_grad, jnp.where(lane == 1, shift_grad, 0.0)).T
        lines = jnp.concatenate(
            [
                vector_sum[0:1, :],
                vector_sum[2:3, :],
                both[0:2, :],
                jnp.zeros((4, width), F32),
                cross_lines_ref[...],
                expert_lines_ref[...],
            ],
            axis=0,
        )
        put_halves(squares, lines, high_ref[0], first_ref, second_ref)


def tokens_back_kernel(
    start_at,
    order_ref,
    target_ref,
    tokens_ref,
    grad_middle_ref,
    grad_query_ref,
    grad_key_ref,
    grad_value_ref,
    vectors_ref,
    self_query,
    self_key,
    self_value,
    tokens_grad_ref,
):
    sequence = order_ref[lax.rem(start_at + pl.program_id(0), order_ref.shape[0] - 1)]
    valid = valid_rows_of(target_ref[sequence], tokens_ref.shape[1])
    normed, inverse = normalise(tokens_ref[0].astype(F32) * valid)
    grad = (
        nt(grad_query_ref[0], self_query[...])
        + nt(grad_key_ref[0], self_key[...])
        + nt(grad_value_ref[0], self_value[...])
    )
    tokens_grad_ref[0] = (
        grad_middle_ref[0] + normalise_back(grad, normed, inverse, vectors_ref[0:1, :])
    ) * valid


def memory_back_kernel(order_ref, grad_key_ref, grad_value_ref, cross_key, cross_value, memory_grad_ref):
    memory_grad_ref[0] = nt(grad_key_ref[0], cross_key[...]) + nt(
        grad_value_ref[0], cross_value[...]
    )


def apart(at, count, turn):
    return at ^ turn if count & (count - 1) == 0 else lax.rem(at + turn, count)


def heard(at, count, turn):
    return at ^ turn if count & (count - 1) == 0 else lax.rem(at + count - turn, count)


def fold_kernel(sizes, lines, shared, count, at_ref, *refs):
    items = sum(sizes)
    parts, outs = refs[:items], refs[items:]
    totals = []
    for size in sizes:
        total = parts[0][...].astype(F32)
        for part in parts[1:size]:
            total = total + part[...].astype(F32)
        totals.append(total)
        parts = parts[size:]
    heights = [total.shape[0] for total in totals]
    heights[-1] -= lines
    if count == 1:
        outs[0][...] = totals[0][: heights[0]].astype(BF16)
        if lines:
            outs[1][...] = totals[0][heights[0] :]
        return
    at, stacks, start = at_ref[0], refs[-len(sizes) :], 0
    for total, height, stack in zip(totals, heights, stacks):
        share = height // count
        stack[...] = total[:height].astype(BF16)
        for turn in range(count):
            which = pl.multiple_of(apart(at, count, turn) * share, 16)
            outs[turn][start : start + share] = stack[pl.ds(which, share), :]
        start += share
    last = heights[-1]
    if shared:
        for turn in range(count):
            outs[turn][start:] = totals[-1][last : last + shared].astype(BF16)
    if lines > shared:
        outs[count][...] = totals[-1][last + shared :]


def spread_kernel(count, at_ref, *refs):
    parts, out = refs[:count], refs[count]
    share = parts[0].shape[0]
    for turn in range(count):
        place = pl.multiple_of(heard(at_ref[0], count, turn) * share, 16)
        out[pl.ds(place, share), :] = parts[turn][...]


def finish_kernel(places, counts, high_ref, own_ref, got_ref, *outs):
    own, got = own_ref[...].astype(F32), got_ref[...].astype(F32)
    top = high_ref[0] > 0
    halves = [jnp.where(top, got, own), jnp.where(top, own, got)]
    height = outs[0].shape[0]
    shares = [height * count // (2 * places) for count in counts]
    block = sum(shares)
    for half in (0, 1):
        for place in range(places):
            source, first = place * block, 0
            for count, share in zip(counts, shares):
                row, left = (half * places + place) * share, share
                while left:
                    at, inside = divmod(row, height)
                    size = min(left, height - inside)
                    outs[first + at][inside : inside + size] = halves[half][source : source + size]
                    row, source, left = row + size, source + size, left - size
                first += count


def cast_kernel(*refs):
    count = len(refs) // 2
    for source, out in zip(refs[:count], refs[count:]):
        out[...] = source[...].astype(F32)


def fixed(shape):
    return pl.BlockSpec(shape, lambda *_: (0,) * len(shape))


def once(shape):
    return pl.BlockSpec(shape, lambda *_: (0,) * len(shape), pipeline_mode=pl.Buffered(1))


def at_position(shape, start, count):
    return pl.BlockSpec(
        (1,) + shape, lambda step, *_: (lax.rem(start + step, count),) + (0,) * len(shape)
    )


def at_sequence(shape, start, count):
    return pl.BlockSpec(
        (1,) + shape,
        lambda step, order, *_: (order[lax.rem(start + step, count)],) + (0,) * len(shape),
    )


def struct(shape, kind):
    return jax.ShapeDtypeStruct(shape, kind)


def launch(
    kernel,
    name,
    grid,
    scalars,
    inputs,
    in_specs,
    outs,
    out_specs,
    scratch=(),
    micros=10,
    after=(),
    into=None,
    carry=(),
):
    into = into or {}
    extra = list(after) + list(into.values()) + list(carry)
    lead, made = len(scalars) + len(inputs), len(outs)
    anywhere = pl.BlockSpec(memory_space=pl.ANY)

    def body(*refs):
        rest = refs[lead + len(extra) :]
        kernel(*refs[:lead], *rest[:made], *rest[made + len(carry) :])

    aliases = {lead + len(after) + at: out for at, out in enumerate(into)}
    first = lead + len(after) + len(into)
    aliases.update({first + at: made + at for at in range(len(carry))})
    return pl.pallas_call(
        body,
        grid_spec=pltpu.PrefetchScalarGridSpec(
            num_scalar_prefetch=len(scalars),
            grid=grid,
            in_specs=list(in_specs) + [anywhere] * len(extra),
            out_specs=list(out_specs) + [anywhere] * len(carry),
            scratch_shapes=list(scratch),
        ),
        out_shape=[struct(shape, kind) for shape, kind in outs]
        + [struct(item.shape, item.dtype) for item in carry],
        input_output_aliases=aliases,
        compiler_params=pltpu.CompilerParams(
            dimension_semantics=("arbitrary",) * len(grid), vmem_limit_bytes=VMEM_LIMIT
        ),
        cost_estimate=pl.CostEstimate(
            flops=int(micros * 1.0e9), bytes_accessed=int(micros * 2.0e6), transcendentals=0
        ),
        name=name,
    )(*scalars, *inputs, *extra)


def gate(item, after):
    (item,) = launch(
        lambda *_: None, "gate", (1,), (), (), [], [], [], micros=1, after=after, carry=[item]
    )
    return item


def exchange(rows, way, turn):
    axis, stride, count = way
    route = []
    for place in range(lax.axis_size(axis)):
        at = (place // stride) % count
        other = at ^ turn if count & (count - 1) == 0 else (at + turn) % count
        route.append((place, place + (other - at) * stride))
    return lax.ppermute(rows, axis, route)


def coordinate(way):
    axis, stride, count = way
    return ((lax.axis_index(axis) // stride) % count).astype(jnp.int32)


def fold(stacks, lines, way, shared=0, after=()):
    count = 1 if way is None else way[2]
    heights, width = [parts[0].shape[0] for parts in stacks], stacks[0][0].shape[1]
    heights[-1] -= lines
    shares = [height // count for height in heights]
    outs = [((sum(shares) + shared, width), BF16)] * count
    if way is None:
        outs += [((lines, width), F32)] if lines else []
    elif lines > shared:
        outs += [((lines - shared, width), F32)]
    parts = [part for stack in stacks for part in stack]
    if all(share % 16 == 0 for share in shares):
        at = coordinate(way).reshape(1) if way else jnp.zeros((1,), jnp.int32)
        return launch(
            functools.partial(fold_kernel, [len(stack) for stack in stacks], lines, shared, count),
            "fold",
            (1,),
            (at,),
            tuple(parts),
            [fixed(part.shape) for part in parts],
            outs,
            [fixed(shape) for shape, _ in outs],
            [pltpu.VMEM((height, width), BF16) for height in heights] if count > 1 else [],
            micros=2,
            after=after,
        )
    (height,), (share,) = heights, shares
    total = sum(part.astype(F32) for part in parts)
    if way is None:
        return [total[:height].astype(BF16)] + ([total[height:]] if lines else [])
    at = coordinate(way)
    results = [
        jnp.concatenate(
            [
                lax.dynamic_slice_in_dim(total, apart(at, count, turn) * share, share, 0),
                total[height : height + shared],
            ],
            axis=0,
        ).astype(BF16)
        for turn in range(count)
    ]
    return results + ([total[height + shared :]] if lines > shared else [])


def swap(gives, way):
    return [gives[0]] + [exchange(gives[turn], way, turn) for turn in range(1, way[2])]


def fetch(own, way):
    return [own] + [exchange(own, way, turn) for turn in range(1, way[2])]


def spread(parts, way, after=(), carry=()):
    own, count = parts[0], way[2]
    share, width = own.shape
    at = coordinate(way)
    if share % 16 == 0:
        whole, *carry = launch(
            functools.partial(spread_kernel, count),
            "spread",
            (1,),
            (at.reshape(1),),
            tuple(parts),
            [fixed(own.shape)] * count,
            [((share * count, width), BF16)],
            [fixed((share * count, width))],
            micros=2,
            after=after,
            carry=carry,
        )
        return (whole, *carry) if carry else whole
    stack = jnp.stack(parts)
    turns = [at ^ place if count & (count - 1) == 0 else (at - place) % count for place in range(count)]
    whole = jnp.concatenate(
        [lax.dynamic_index_in_dim(stack, turn, 0, False) for turn in turns], axis=0
    )
    return (whole, *carry) if carry else whole


def finish(own, got, width, places, counts, after=()):
    high = (lax.axis_index("dp") % 2).astype(jnp.int32).reshape(1)
    squares = sum(counts)
    return launch(
        functools.partial(finish_kernel, places, counts),
        "finish",
        (1,),
        (high,),
        (own, got),
        [fixed(own.shape)] * 2,
        [((width, width), F32)] * squares,
        [fixed((width, width))] * squares,
        micros=2,
        after=after,
    )


def on_device(
    tokens,
    memory,
    cotangent,
    target_length,
    memory_length,
    expert_of,
    self_norm_gain,
    self_norm_bias,
    self_query,
    self_key,
    self_value,
    self_out,
    self_query_bias,
    self_value_bias,
    self_out_bias,
    cross_norm_gain,
    cross_norm_bias,
    cross_query,
    cross_key,
    cross_value,
    cross_out,
    cross_attention_query_bias,
    cross_value_bias,
    cross_out_bias,
    expert_norm_gain,
    expert_norm_bias,
    expert_in,
    expert_in_bias,
    expert_out,
    expert_out_bias,
):
    seqs, length, width = tokens.shape
    mem_rows = memory.shape[1]
    local_count, _, hidden_width = expert_in.shape
    groups = lax.axis_size("expert")
    places = lax.axis_size("dp")
    own_group = lax.axis_index("expert")
    column = lax.axis_index("dp")

    shifts = list(range(1, groups)) + [0]
    whole = groups == seqs
    rows_shape, square = (length, width), (width, width)
    mem_shape, heads_shape = (mem_rows, width), (HEADS, length)
    turned = (width, length)
    in_smem = pl.BlockSpec(memory_space=pltpu.SMEM)
    lines = [
        self_norm_gain,
        self_norm_bias,
        self_query_bias,
        self_value_bias,
        self_out_bias,
        cross_norm_gain,
        cross_norm_bias,
        cross_attention_query_bias,
        cross_value_bias,
        cross_out_bias,
        expert_norm_gain,
        expert_norm_bias,
    ]
    in_vmem = pl.BlockSpec(memory_space=pltpu.VMEM)
    order, picks, used, slot_of, spot_of, vectors, *grads = pl.pallas_call(
        functools.partial(plan_kernel, shifts, local_count),
        in_specs=[in_smem] * 3 + [in_vmem] * (1 + VECTORS),
        out_specs=[in_smem] * 5 + [in_vmem] * (1 + groups),
        out_shape=[
            struct((seqs + 1,), jnp.int32),
            struct((groups,), jnp.int32),
            struct((groups,), jnp.int32),
            struct((seqs,), jnp.int32),
            struct((groups,), jnp.int32),
            struct((16, width), F32),
        ]
        + [struct(rows_shape, BF16)] * groups,
        compiler_params=pltpu.CompilerParams(vmem_limit_bytes=VMEM_LIMIT),
        name="plan",
    )(
        jnp.stack([own_group, column, jnp.int32(places)]).astype(jnp.int32),
        expert_of,
        target_length,
        cotangent,
        *[line.reshape(1, width) for line in lines],
    )

    def move(rows, slot, back=False):
        shift = shifts[slot]
        if shift == 0:
            return rows
        turn = -shift if back else shift
        return lax.ppermute(rows, "expert", [(g, (g + turn) % groups) for g in range(groups)])

    def arranged(per_slot):
        if whole:
            return per_slot
        stack = jnp.stack(per_slot)
        return [lax.dynamic_index_in_dim(stack, slot_of[at], 0, False) for at in range(seqs)]

    position = lambda shape, start=0: at_position(shape, start, seqs)
    sequence = lambda shape, start=0: at_sequence(shape, start, seqs)
    self_matrices = (self_query, self_key, self_value, self_out)
    cross_matrices = (cross_query, cross_key, cross_value, cross_out)
    half = seqs // 2
    high = (column % 2).astype(jnp.int32).reshape(1)

    saved = [
        (rows_shape, F32),
        (rows_shape, F32),
        (rows_shape, BF16),
        (rows_shape, BF16),
        (rows_shape, BF16),
        (turned, BF16),
        (heads_shape, F32),
        (rows_shape, BF16),
        (mem_shape, BF16),
        (mem_shape, BF16),
        (turned, BF16),
        (heads_shape, F32),
    ]

    def forward(start, steps, kept, after):
        results = launch(
            functools.partial(forward_kernel, start, steps),
            "forward",
            (steps,),
            (order, target_length, memory_length),
            (tokens, memory, vectors) + self_matrices + cross_matrices,
            [sequence(rows_shape, start), sequence(mem_shape, start), fixed(vectors.shape)]
            + [fixed(square)] * 8,
            [(rows_shape, BF16)] * steps + [((seqs,) + shape, kind) for shape, kind in saved],
            [fixed(rows_shape)] * steps + [position(shape, start) for shape, _ in saved],
            [pltpu.VMEM(turned, BF16)],
            micros=0.01,
            after=after,
            into={at + steps: item for at, item in enumerate(kept)},
        )
        return results[:steps], results[steps:]

    grads_in = [move(grads[slot], slot) for slot in range(groups)]
    normed_one, kept = forward(0, half, [], [])
    normed_two, kept = forward(half, seqs - half, kept, [grads_in[0]])
    normed = list(normed_one) + list(normed_two)
    (
        later,
        middle,
        query_one,
        key_one,
        value_one,
        context_one,
        logsum_one,
        query_two,
        key_two,
        value_two,
        context_two,
        logsum_two,
    ) = kept

    if whole:
        rows_in = [move(normed[slot], slot) for slot in range(groups)]
    else:
        joined = jnp.stack(normed)
        rows_in = [
            move(lax.dynamic_index_in_dim(joined, spot_of[slot], 0, False), slot)
            for slot in range(groups)
        ]
    tiles = 4
    tile_width = hidden_width // tiles
    hidden_tile = pl.BlockSpec((length, tile_width), lambda t, *_: (0, t))
    line_tile = pl.BlockSpec((1, tile_width), lambda t, *_: (0, t))
    hidden, grad_pre, made, grad_rows, pre_sum, grads_sum = {}, {}, {}, {}, {}, {}

    wide = 2 * tile_width
    wide_tile = pl.BlockSpec((length, wide), lambda t, *_: (0, t))

    def expert(slot, after):
        results = launch(
            functools.partial(expert_kernel, slot),
            "expert",
            (tiles // 2,),
            (picks, used),
            (rows_in[slot], grads_in[slot], expert_in, expert_in_bias, expert_out, expert_out_bias),
            [
                fixed(rows_shape),
                fixed(rows_shape),
                pl.BlockSpec((1, width, wide), lambda t, pick, _: (pick[slot], 0, t)),
                pl.BlockSpec((local_count, wide), lambda t, *_: (0, t)),
                pl.BlockSpec((1, wide, width), lambda t, pick, _: (pick[slot], t, 0)),
                fixed((local_count, width)),
            ],
            [((length, hidden_width), BF16)] * 2
            + [(rows_shape, BF16)] * 2
            + [((1, hidden_width), F32), ((1, width), F32)],
            [wide_tile, wide_tile, fixed(rows_shape), fixed(rows_shape)]
            + [pl.BlockSpec((1, wide), lambda t, *_: (0, t))]
            + [fixed((1, width))],
            [pltpu.VMEM(rows_shape, F32)] * 2,
            micros=0.01,
            after=after,
        )
        for table, result in zip((hidden, grad_pre, made, grad_rows, pre_sum, grads_sum), results):
            table[slot] = result

    back_scratch = [
        pltpu.VMEM((width, mem_rows), BF16),
        pltpu.VMEM(rows_shape, BF16),
        pltpu.VMEM(heads_shape, F32),
        pltpu.VMEM(turned, BF16),
    ]

    def sums_shape(count, final, lines=0):
        if final:
            return [((count * width // 2 + lines, width), BF16)] * 2
        return [((count,) + square, BF16)]

    def cross_back(start, steps, grads, given, filled, final, after, carry=(), micros=26):
        first = given is None
        total = sums_shape(5, final)
        return launch(
            functools.partial(cross_back_kernel, start, first, final, steps),
            "cross_back",
            (steps,),
            (order, target_length, memory_length, high),
            tuple(grads)
            + (() if first else tuple(given))
            + (cotangent, memory, later, middle, query_two, key_two, value_two, context_two)
            + (logsum_two, context_one, vectors)
            + cross_matrices,
            [once(rows_shape)] * steps
            + ([] if first else [once((5,) + square), once((8, width))])
            + [
                sequence(rows_shape, start),
                sequence(mem_shape, start),
                position(rows_shape, start),
                position(rows_shape, start),
                position(rows_shape, start),
                position(mem_shape, start),
                position(mem_shape, start),
                position(turned, start),
                position(heads_shape, start),
                position(turned, start),
                fixed(vectors.shape),
            ]
            + [once(square)] * 4,
            [((seqs,) + rows_shape, F32)]
            + [((seqs,) + mem_shape, BF16)] * 2
            + total
            + [((8, width), F32)],
            [position(rows_shape, start), position(mem_shape, start), position(mem_shape, start)]
            + [fixed(shape) for shape, _ in total]
            + [fixed((8, width))],
            [pltpu.VMEM((5,) + square, F32), pltpu.VMEM((8, width), F32), pltpu.VMEM(rows_shape, BF16)]
            + back_scratch,
            micros=micros,
            after=after,
            into={at: item for at, item in enumerate(filled)},
            carry=carry,
        )

    def self_back(start, steps, given, filled, final, after):
        first = given is None
        total = sums_shape(3, final, LINES) if final else sums_shape(3, final) + [((8, width), F32)]
        return launch(
            functools.partial(self_back_kernel, start, first, final),
            "self_back",
            (steps,),
            (order, target_length, high),
            (() if first else tuple(given))
            + (cross_lines, expert_lines)
            + (tokens, grad_middle, query_one, key_one, value_one, context_one, logsum_one, columns)
            + self_matrices,
            ([] if first else [once((3,) + square), once((8, width))])
            + [fixed((8, width)), fixed((EXPERT_LINES, width))]
            + [
                sequence(rows_shape, start),
                position(rows_shape, start),
                position(rows_shape, start),
                position(rows_shape, start),
                position(rows_shape, start),
                position(turned, start),
                position(heads_shape, start),
                fixed(columns.shape),
            ]
            + [once(square)] * 4,
            [((seqs,) + rows_shape, BF16)] * 3 + total,
            [position(rows_shape, start)] * 3 + [fixed(shape) for shape, _ in total],
            [pltpu.VMEM((3,) + square, F32), pltpu.VMEM((8, width), F32)] + back_scratch,
            micros=10 * steps,
            after=after,
            into={at: item for at, item in enumerate(filled)},
        )

    back = {}

    def send_back(slot):
        back[slot] = move(grad_rows[slot], slot, True)

    if whole:
        expert(3, [])
        send_back(3)
        results = cross_back(
            3, 1, [back[3]], None, [], False, grads_in[1:3], micros=0.01
        )
        filled, running = results[:3], results[3:5]
        expert(0, running[1:])
        expert(1, [made[0]])
        expert(2, [made[1]])
        for slot in range(3):
            send_back(slot)
    else:
        for slot in range(groups):
            expert(slot, [])
            send_back(slot)

    in_sums, out_sums, expert_lines = launch(
        functools.partial(expert_weights_kernel, groups),
        "expert_weights",
        (tiles,),
        (picks, used),
        tuple(rows_in)
        + tuple(grads_in)
        + tuple(table[slot] for table in (hidden, grad_pre, pre_sum, grads_sum) for slot in range(groups)),
        [once(rows_shape)] * (2 * groups)
        + [hidden_tile] * (2 * groups)
        + [line_tile] * groups
        + [fixed((1, width))] * groups,
        [
            ((local_count, width, hidden_width), BF16),
            ((local_count, hidden_width, width), BF16),
            ((EXPERT_LINES, width), F32),
        ],
        [
            pl.BlockSpec((local_count, width, tile_width), lambda t, *_: (0, 0, t)),
            pl.BlockSpec((local_count, tile_width, width), lambda t, *_: (0, t, 0)),
            fixed((EXPERT_LINES, width)),
        ],
        [
            pltpu.VMEM((local_count, width, tile_width), F32),
            pltpu.VMEM((local_count, tile_width, width), F32),
            pltpu.VMEM((local_count, 1, tile_width), F32),
            pltpu.VMEM((local_count, 1, width), F32),
        ],
        micros=17,
        after=[back[0]] if whole else [],
    )
    expert_in_grad = lax.psum_scatter(in_sums, "dp", scatter_dimension=1, tiled=True)
    expert_out_grad = lax.psum_scatter(out_sums, "dp", scatter_dimension=1, tiled=True)

    if whole:
        away = [slot for slot in range(groups) if shifts[slot]]
        results = cross_back(
            0, 2, [back[0], back[1]], running, filled, False, [in_sums], [made[slot] for slot in away]
        )
        filled, running = results[:3], results[3:5]
        for at, slot in enumerate(away):
            made[slot] = results[5 + at]
        made_home = [move(made[slot], slot, True) for slot in range(groups)]
        *results, cross_keep, cross_give, cross_lines = cross_back(
            2, 1, [back[2]], running, filled, True, []
        )
    else:
        *results, cross_keep, cross_give, cross_lines = cross_back(
            0, seqs, arranged([back[slot] for slot in range(groups)]), None, [], True, []
        )
        made_home = arranged([move(made[slot], slot, True) for slot in range(groups)])
    grad_middle, grad_key_two, grad_value_two = results

    chips = places // 2
    core, plane, line = ("dp", 1, 2), ("dp", 2, chips), ("expert", 1, groups)
    columns = jnp.concatenate([vectors.T, jnp.zeros((width, 128 - vectors.shape[0]), F32)], axis=1)

    def tokens_back(start, steps, grads, filled, after):
        return launch(
            functools.partial(tokens_back_kernel, start),
            "tokens_back",
            (steps,),
            (order, target_length),
            (tokens, grad_middle, *grads, vectors)
            + self_matrices[:3],
            [sequence(rows_shape, start)]
            + [position(rows_shape, start)] * 4
            + [fixed(vectors.shape)]
            + [once(square)] * 3,
            [((seqs,) + rows_shape, F32)],
            [sequence(rows_shape, start)],
            micros=4 * steps,
            after=after,
            into={at: item for at, item in enumerate(filled)},
        )

    def memory_back(after):
        return launch(
            memory_back_kernel,
            "memory_back",
            (seqs,),
            (order,),
            (grad_key_two, grad_value_two, cross_key, cross_value),
            [position(mem_shape)] * 2 + [once(square)] * 2,
            [((seqs,) + mem_shape, F32)],
            [sequence(mem_shape)],
            micros=5,
            after=after,
        )[0]

    def output_rows(after):
        return launch(
            functools.partial(output_kernel, seqs),
            "output",
            (seqs,),
            (order, target_length),
            (later, *made_home),
            [position(rows_shape)] + [once(rows_shape)] * seqs,
            [((seqs,) + rows_shape, BF16)],
            [sequence(rows_shape)],
            micros=5,
            after=after,
        )[0]

    def casts(items, after):
        return launch(
            cast_kernel,
            "cast",
            (1,),
            (),
            tuple(items),
            [fixed(item.shape) for item in items],
            [(item.shape, F32) for item in items],
            [fixed(item.shape) for item in items],
            micros=3,
            after=after,
        )

    cross_got = exchange(gate(cross_give, made_home[:1]), core, 1)
    memory_grad = memory_back([])
    cross_parts = swap(fold([[cross_keep, cross_got]], 0, plane, after=[memory_grad]), plane)
    *grads_one, weights_run, vectors_run = self_back(
        0, half, None, [], False, [cross_parts[0]]
    )
    cross_line = swap(fold([cross_parts], 0, line, after=grads_one[:1]), line)
    filled = tokens_back(0, half, grads_one, [], [cross_line[0], *made_home[1:2]])
    (cross_share,) = fold([cross_line], 0, None, after=filled)
    cross_fetched = fetch(cross_share, line)
    *grads_one, self_keep, self_give = self_back(
        half,
        seqs - half,
        (weights_run, vectors_run),
        grads_one,
        True,
        [cross_share, *filled],
    )

    cross_rows, self_give = spread(
        cross_fetched, line, after=[self_keep, *made_home[2:3]], carry=[self_give]
    )
    self_got = exchange(self_give, core, 1)
    cross_fetched = fetch(cross_rows, plane)
    expert_in_grad, expert_out_grad = casts([expert_in_grad, expert_out_grad], [cross_rows])

    self_parts = swap(
        fold([[self_keep, self_got]], LINES, plane, LINES, after=[expert_in_grad]), plane
    )
    output = output_rows([self_parts[0]])

    *gives, own_lines = fold([self_parts], LINES, line, SHARED_LINES, after=[output])
    self_line = swap(gives, line)
    cross_rows = spread(cross_fetched, plane, after=[output])
    cross_got = exchange(cross_rows, core, 1)
    filled = tokens_back(half, 1, grads_one, filled, [self_line[0], cross_rows])

    self_share, totals = fold([self_line], SHARED_LINES, None, after=filled)
    self_fetched = fetch(self_share, line)
    (tokens_grad,) = tokens_back(half + 1, seqs - half - 1, grads_one, filled, [self_share])

    self_rows = spread(self_fetched, line, after=[tokens_grad])
    self_fetched = fetch(self_rows, plane)
    cross_q, cross_k, cross_v, cross_o, self_o = finish(
        cross_rows, cross_got, width, 1, [5], [self_rows]
    )
    self_rows = spread(self_fetched, plane, after=[cross_q])
    self_q, self_k, self_v = finish(self_rows, exchange(self_rows, core, 1), width, 1, [3])

    in_count = local_count * hidden_width // width
    in_bias = own_lines[:in_count].reshape(local_count, hidden_width)
    out_bias = own_lines[in_count : in_count + local_count]
    in_share, out_share = hidden_width // places, width // places
    return (
        output,
        tokens_grad,
        memory_grad,
        totals[2],
        totals[3],
        self_q,
        self_k,
        self_v,
        self_o,
        totals[0],
        totals[1],
        totals[15],
        totals[13],
        totals[14],
        cross_q,
        cross_k,
        cross_v,
        cross_o,
        totals[12],
        totals[11],
        totals[10],
        totals[8],
        totals[9],
        expert_in_grad,
        lax.dynamic_slice_in_dim(in_bias, column * in_share, in_share, 1),
        expert_out_grad,
        lax.dynamic_slice_in_dim(out_bias, column * out_share, out_share, 1),
    )


def solution(mesh):
    rows = P(("expert", "dp"), None, None)
    counts = P(("expert", "dp"))
    split = (P("expert", None, None), P("expert", None)) * 2
    shares = (P("expert", "dp", None), P("expert", "dp")) * 2
    return jax.shard_map(
        on_device,
        mesh=mesh,
        in_specs=(rows,) * 3 + (counts,) * 2 + (P(),) * 21 + split,
        out_specs=(rows,) * 3 + (P(),) * 20 + shares,
        check_vma=False,
    )
```
